32 devices in a mesh: gx: 4 (over y, core), gy: 8 (over z, x).
Axes of the slice: x: 2, y: 2, z: 4, core: 2. Of those that a mesh axis runs over, the one named last changes fastest.
Arguments:
- query_rows: bfloat16 [4096, 1024], P(('gx', 'gy')), may hold values from -6 to 6
- key_rows: bfloat16 [4096, 1024], P(('gx', 'gy')), may hold values from -6 to 6
- value_rows: bfloat16 [4096, 1024], P(('gx', 'gy')), may hold values from -6 to 6
- out_grad: bfloat16 [4096, 1024], P(('gx', 'gy')), may hold values from -6 to 6
- gate_class: int32 [4096], P(('gx', 'gy')), may hold values from 0 to 31
- gate_table: float32 [32, 20, 8], replicated, may hold values from 0 to 1, as said below
Outputs:
- query_grad: bfloat16 [4096, 1024], P(('gx', 'gy'))
- key_grad: bfloat16 [4096, 1024], P(('gx', 'gy'))
- value_grad: bfloat16 [4096, 1024], P(('gx', 'gy'))
The draws below stay inside these ranges and needn't reach their ends.
Inputs may be any that keep to these rules, and one draw needn't show every extreme that they name: `gate_class`: row of the gate table for each token. `gate_table`: every entry is positive.
All inputs are finite; a program needn't handle non-finite values.
Results may differ from the reference program's by a relative error of at most 0.0054.
Values may be sent and summed in bfloat16 or wider, within the bound.
No kernel may reach another device: no remote copies, remote signals or barrier semaphores. Data moves between devices by JAX's collectives and lax.ppermute only.
A program may use at most 64 MiB of HBM per device.

```python
import jax
import jax.numpy as jnp
from jax import lax

TOK_DEV = 128
H = 8
HS = 128
G = 32
LEVELS = 20
TOKENS = 4096
HD = 1024


def draw_gate_table(key, part):
    level_index = jnp.arange(LEVELS, dtype=jnp.float32)
    spans = jnp.maximum(level_index - 1.0, 0.0)
    level_scale = jnp.exp2(-0.5 * spans) / jnp.sqrt(jnp.float32(HS))
    base = jnp.exp(jax.random.uniform(key, (G, LEVELS, H), jnp.float32, jnp.log(0.1), 0.0))
    return (base * level_scale[None, :, None]).astype(jnp.float32)


def touch_ends(drawn, key, smallest, high):
    dims = drawn.shape
    index_at = [jax.random.randint(jax.random.fold_in(key, axis), (), 0, dims[axis]) for axis in range(len(dims))]
    drawn = drawn.at[tuple(index_at)].set(smallest)
    longest = dims.index(max(dims))
    index_at[longest] = (index_at[longest] + 1) % dims[longest]
    return drawn.at[tuple(index_at)].set(high)


def block_levels(stream_key, shape, cuts, low, top_value):
    gain = 1.0
    for dim, blocks in cuts:
        heights = jax.random.uniform(jax.random.fold_in(jax.random.fold_in(stream_key, 6), dim), (blocks,), jnp.float32, low / len(cuts), top_value / len(cuts))
        gain = gain * jnp.repeat(jnp.exp(heights), shape[dim] // blocks).reshape((-1,) + (1,) * (len(shape) - 1 - dim))
    return gain


def centred(rng, shape, spread, limit, cuts=(), kind=jnp.bfloat16):
    values = spread * jax.random.normal(rng, shape, jnp.float32)
    if cuts:
        values = values * block_levels(rng, shape, cuts, -0.22, 0.18)
    return jnp.clip(values, -limit, limit).astype(kind)


def setup_inputs(seed: int = 0) -> dict:
    streams_of = jax.random.split(jax.random.key(seed), 7)
    query_rows = centred(streams_of[0], (TOKENS, HD), 1.0, 6.0, ((0, 32),))
    key_rows = centred(streams_of[1], (TOKENS, HD), 1.0, 6.0, ((0, 32),))
    value_rows = centred(streams_of[2], (TOKENS, HD), 1.0, 6.0, ((0, 32),))
    out_grad = centred(streams_of[3], (TOKENS, HD), 1.0, 6.0, ((0, 32),))
    gate_class = touch_ends(jax.random.randint(streams_of[4], (TOKENS,), 0, G), jax.random.fold_in(streams_of[4], 1), 0, G - 1).astype(jnp.int32)
    gate_table = draw_gate_table(jax.random.fold_in(streams_of[6], 71), 0)
    return {"query_rows": query_rows, "key_rows": key_rows, "value_rows": value_rows, "out_grad": out_grad, "gate_class": gate_class, "gate_table": gate_table}


def block_weights(gate_rows, amount):
    block_depth = amount.bit_length() - 1
    positions = jnp.arange(amount, dtype=jnp.int32)
    xor_place = jnp.bitwise_xor(positions[:, None], positions[None, :])
    level_map = jnp.zeros((amount, amount), jnp.int32)
    for bit_index in range(block_depth):
        level_map = level_map + (xor_place >= 2 ** bit_index).astype(jnp.int32)
    causal = positions[None, :] <= positions[:, None]
    weights = jnp.zeros((gate_rows.shape[2], amount, amount), jnp.float32)
    for tree_level in range(block_depth + 1):
        chosen = jnp.logical_and(level_map == tree_level, causal)
        picked = gate_rows[:, tree_level, :].T[:, :, None]
        weights = weights + jnp.where(chosen[None, :, :], picked, jnp.zeros((), weights.dtype))
    return weights


def to_bfloat(values):
    return lax.optimization_barrier(values.astype(jnp.bfloat16)).astype(jnp.float32)


def sibling_sums(values, span):
    number = values.shape[0]
    rest = values.shape[1:]
    blocks = jnp.sum(values.reshape((number // span, span) + rest), axis=1)
    pairs = blocks.reshape((number // (2 * span), 2) + rest)[:, ::-1]
    flipped = pairs.reshape((number // span,) + rest)
    return jnp.repeat(flipped, span, axis=0)


def reference(query_rows, key_rows, value_rows, out_grad, gate_class, gate_table):
    group_count = TOKENS // TOK_DEV
    block_depth = TOK_DEV.bit_length() - 1
    device_depth = group_count.bit_length() - 1
    gates = gate_table[gate_class].astype(jnp.float32)
    gate_blocks = gates.reshape(group_count, TOK_DEV, LEVELS, H)
    shape_four = (group_count, TOK_DEV, H, HS)
    query_f = query_rows.reshape(shape_four).astype(jnp.float32)
    key_f = key_rows.reshape(shape_four).astype(jnp.float32)
    value_f = value_rows.reshape(shape_four).astype(jnp.float32)
    grad_f = out_grad.reshape(shape_four).astype(jnp.float32)

    def local_block(pieces):
        query_part, key_part, value_part, grad_part, gate_part = pieces
        scores = jnp.einsum('thd,shd->hts', query_part, key_part)
        pair_grads = jnp.einsum('the,she->hts', grad_part, value_part)
        weights = block_weights(gate_part, TOK_DEV)
        weighted_grads = to_bfloat(weights * pair_grads)
        weighted_scores = to_bfloat(weights * scores)
        local_query = jnp.einsum('hts,shd->thd', weighted_grads, key_part)
        local_key = jnp.einsum('hts,thd->shd', weighted_grads, query_part)
        local_value = jnp.einsum('hts,the->she', weighted_scores, grad_part)
        return local_query, local_key, local_value

    local_query, local_key, local_value = lax.map(local_block, (query_f, key_f, value_f, grad_f, gate_blocks))
    group_states = jnp.einsum('nthd,nthe->nhde', key_f, value_f)
    group_ids = jnp.arange(group_count, dtype=jnp.int32)
    query_grad = local_query
    state_grad = jnp.zeros_like(group_states)
    for tree_level in range(device_depth):
        span = 2 ** tree_level
        flags = ((group_ids // span) % 2).astype(jnp.float32)
        gate_level = gate_blocks[:, :, block_depth + 1 + tree_level, :] * flags[:, None, None]
        rounded_state = to_bfloat(sibling_sums(group_states, span))
        query_grad = query_grad + gate_level[..., None] * jnp.einsum('nthe,nhde->nthd', grad_f, rounded_state)
        scaled_query = to_bfloat(gate_level[..., None] * query_f)
        level_grad = jnp.einsum('nthd,nthe->nhde', scaled_query, grad_f)
        state_grad = state_grad + sibling_sums(level_grad, span)
    rounded_grad = to_bfloat(state_grad)
    key_grad = local_key + jnp.einsum('nthe,nhde->nthd', value_f, rounded_grad)
    value_grad = local_value + jnp.einsum('nthd,nhde->nthe', key_f, rounded_grad)
    return (query_grad.reshape(TOKENS, H * HS).astype(jnp.bfloat16),
            key_grad.reshape(TOKENS, H * HS).astype(jnp.bfloat16),
            value_grad.reshape(TOKENS, H * HS).astype(jnp.bfloat16))
```

```python
import jax
import jax.numpy as jnp
from jax import lax
from jax.sharding import PartitionSpec as P

NEAR = 3


def level_bits(amount):
    return amount.bit_length() - 1


def trade(block, axis, offset):
    count = lax.axis_size(axis)
    return lax.ppermute(block, axis, [(place, place ^ offset) for place in range(count)])


def gate_values(gate_class, gate_table):
    classes, levels, head_count = gate_table.shape
    picker = (gate_class[:, None] == jnp.arange(classes, dtype=jnp.int32)[None, :]).astype(
        jnp.float32
    )
    picked = jnp.dot(
        picker,
        gate_table.reshape(classes, levels * head_count),
        precision=lax.Precision.HIGHEST,
        preferred_element_type=jnp.float32,
    )
    return picked.reshape(gate_class.shape[0], levels, head_count)


def block_weights(gate_rows, amount):
    block_depth = level_bits(amount)
    positions = jnp.arange(amount, dtype=jnp.int32)
    xor_place = jnp.bitwise_xor(positions[:, None], positions[None, :])
    level_map = jnp.zeros((amount, amount), jnp.int32)
    for bit_index in range(block_depth):
        level_map = level_map + (xor_place >= 2**bit_index).astype(jnp.int32)
    causal = positions[None, :] <= positions[:, None]
    weights = jnp.zeros((gate_rows.shape[2], amount, amount), jnp.float32)
    for tree_level in range(block_depth + 1):
        chosen = jnp.logical_and(level_map == tree_level, causal)
        picked = gate_rows[:, tree_level, :].T[:, :, None]
        weights = weights + jnp.where(chosen[None, :, :], picked, jnp.zeros((), jnp.float32))
    return weights


def per_device(query_rows, key_rows, value_rows, out_grad, gate_class, gate_table):
    row_count = query_rows.shape[0]
    head_count = gate_table.shape[2]
    head_size = query_rows.shape[1] // head_count
    inner_bits = level_bits(lax.axis_size("gy"))
    outer_bits = level_bits(lax.axis_size("gx"))
    total_levels = inner_bits + outer_bits
    block_depth = level_bits(row_count)
    inner_index = lax.axis_index("gy")
    outer_index = lax.axis_index("gx")
    block_index = (outer_index << inner_bits) | inner_index
    flags = [((block_index >> level) & 1) == 1 for level in range(total_levels)]

    def swap(block, bit):
        if bit < inner_bits:
            return trade(block, "gy", 1 << bit)
        return trade(block, "gx", 1 << (bit - inner_bits))

    def wide(values):
        return values.astype(jnp.float32)

    def narrow(values):
        return values.astype(jnp.bfloat16)

    gate_rows = gate_values(gate_class, gate_table)
    level_gates = gate_rows[:, block_depth + 1 : block_depth + 1 + total_levels, :]
    shape_three = (row_count, head_count, head_size)
    query_heads = query_rows.reshape(shape_three)
    key_heads = key_rows.reshape(shape_three)
    value_heads = value_rows.reshape(shape_three)
    grad_heads = out_grad.reshape(shape_three)

    def payload(level):
        scaled = narrow(level_gates[:, level, :, None] * wide(query_heads))
        left = jnp.where(flags[level], scaled, key_heads)
        right = jnp.where(flags[level], grad_heads, value_heads)
        return narrow(
            jnp.einsum("thd,the->hde", left, right, preferred_element_type=jnp.float32)
        )

    quarter = head_count // 4
    half = head_count // 2
    cell = (head_size, head_size)
    z_place = (inner_index >> 1) & 3
    x_place = inner_index & 1

    upper = jnp.stack([payload(level) for level in range(NEAR, total_levels)], axis=1)
    upper = upper.reshape((4, quarter, total_levels - NEAR) + cell)

    def upper_part(place):
        return lax.dynamic_index_in_dim(upper, place, 0, keepdims=False)

    came = [trade(upper_part(z_place ^ offset), "gy", offset << 1) for offset in (3, 2, 1)]
    part = wide(upper_part(z_place)) + wide(came[0]) + wide(came[1]) + wide(came[2])
    parts = [part[:, place] for place in range(total_levels - NEAR)]
    done_parts = []
    for level in range(NEAR, total_levels):
        seen = wide(swap(narrow(jnp.stack(parts, axis=1)), level))
        done_parts.append(seen[:, 0])
        parts = [parts[place] + seen[:, place] for place in range(1, len(parts))]
    shares = jnp.stack(done_parts, axis=1)
    shares = narrow(shares + wide(swap(narrow(shares), 0)))
    pieces = [shares] + [trade(shares, "gy", offset << 1) for offset in (1, 2, 3)]
    near_pair = [
        jnp.where(z_place & 1 == 1, pieces[1], pieces[0]),
        jnp.where(z_place & 1 == 1, pieces[0], pieces[1]),
    ]
    far_pair = [
        jnp.where(z_place & 1 == 1, pieces[3], pieces[2]),
        jnp.where(z_place & 1 == 1, pieces[2], pieces[3]),
    ]
    far_side = z_place & 2 == 2
    ordered = [
        jnp.where(far_side, far_pair[0], near_pair[0]),
        jnp.where(far_side, far_pair[1], near_pair[1]),
        jnp.where(far_side, near_pair[0], far_pair[0]),
        jnp.where(far_side, near_pair[1], far_pair[1]),
    ]
    upper_done = jnp.concatenate(ordered, axis=0)

    low_two = payload(2).reshape((2, half) + cell)
    low_one = payload(1)
    two_other = lax.dynamic_index_in_dim(low_two, 1 - x_place, 0, keepdims=False)
    two_own = lax.dynamic_index_in_dim(low_two, x_place, 0, keepdims=False)
    seen = wide(swap(jnp.concatenate([low_one, two_other], axis=0), 0))
    one_sum = wide(low_one) + seen[:head_count]
    two_sum = wide(two_own) + seen[head_count:]
    arrived = swap(jnp.concatenate([narrow(one_sum), narrow(two_sum)], axis=0), 1)
    one_done = arrived[:head_count]
    two_sum = two_sum + wide(arrived[head_count:])
    two_half = swap(narrow(two_sum), 2)
    two_rest = swap(two_half, 0)
    two_done = jnp.concatenate(
        [
            jnp.where(x_place == 0, two_half, two_rest),
            jnp.where(x_place == 0, two_rest, two_half),
        ],
        axis=0,
    )
    zero_done = swap(payload(0), 0)
    states = [zero_done, one_done, two_done]
    states = states + [upper_done[:, place] for place in range(total_levels - NEAR)]

    scores = jnp.einsum("thd,shd->hts", query_heads, key_heads, preferred_element_type=jnp.float32)
    pair_grads = jnp.einsum(
        "the,she->hts", grad_heads, value_heads, preferred_element_type=jnp.float32
    )
    weights = block_weights(gate_rows, row_count)
    weighted_grads = narrow(weights * pair_grads)
    weighted_scores = narrow(weights * scores)
    query_total = jnp.einsum(
        "hts,shd->thd", weighted_grads, key_heads, preferred_element_type=jnp.float32
    )
    key_total = jnp.einsum(
        "hts,thd->shd", weighted_grads, query_heads, preferred_element_type=jnp.float32
    )
    value_total = jnp.einsum(
        "hts,the->she", weighted_scores, grad_heads, preferred_element_type=jnp.float32
    )
    state_grad = jnp.zeros((head_count,) + cell, jnp.float32)
    for level in range(total_levels):
        level_term = jnp.einsum(
            "the,hde->thd", grad_heads, states[level], preferred_element_type=jnp.float32
        )
        gate_here = jnp.where(flags[level], level_gates[:, level, :], 0.0)
        query_total = query_total + gate_here[:, :, None] * level_term
        state_grad = state_grad + jnp.where(flags[level], 0.0, wide(states[level]))
    grad_rounded = narrow(state_grad)
    key_total = key_total + jnp.einsum(
        "the,hde->thd", value_heads, grad_rounded, preferred_element_type=jnp.float32
    )
    value_total = value_total + jnp.einsum(
        "thd,hde->the", key_heads, grad_rounded, preferred_element_type=jnp.float32
    )
    width = head_count * head_size
    return (
        narrow(query_total.reshape(row_count, width)),
        narrow(key_total.reshape(row_count, width)),
        narrow(value_total.reshape(row_count, width)),
    )


def solution(mesh):
    rows = P(("gx", "gy"), None)
    return jax.shard_map(
        per_device,
        mesh=mesh,
        in_specs=(rows, rows, rows, rows, P(("gx", "gy")), P()),
        out_specs=(rows, rows, rows),
        check_vma=False,
    )
```

```python
import functools

import jax
import jax.numpy as jnp
from jax import lax
from jax.experimental import pallas as pl
from jax.experimental.pallas import tpu as pltpu
from jax.sharding import PartitionSpec as P

NEAR = 3
VMEM_BYTES = 48 * 1024 * 1024


def level_bits(amount):
    return amount.bit_length() - 1


def wide(values):
    return values.astype(jnp.float32)


def narrow(values):
    return values.astype(jnp.bfloat16)


def product(left, right, left_dim, right_dim):
    return lax.dot_general(
        left,
        right,
        (((left_dim,), (right_dim,)), ((), ())),
        preferred_element_type=jnp.float32,
    )


def gate_lanes(class_ref, table_ref, first, last):
    classes = table_ref.shape[2]
    tokens = class_ref.shape[1]
    rows = (last - first) * table_ref.shape[1]
    numbers = lax.broadcasted_iota(jnp.int32, (classes, tokens), 0)
    picker = (numbers == class_ref[...]).astype(jnp.float32)
    table = table_ref[first:last].reshape(rows, classes)
    return jnp.dot(
        table, picker, precision=lax.Precision.HIGHEST, preferred_element_type=jnp.float32
    )


def payload_kernel(
    levels, offset, head_size, flag_ref, class_ref, table_ref, q_ref, k_ref, v_ref, g_ref, out_ref
):
    head_count = table_ref.shape[1]
    gates = gate_lanes(class_ref, table_ref, offset + levels[0], offset + levels[-1] + 1)
    for head in range(head_count):
        columns = pl.ds(head * head_size, head_size)
        query_turned = wide(q_ref[:, columns].T)
        key_turned = wide(k_ref[:, columns].T)
        grad_here = g_ref[:, columns]
        value_here = v_ref[:, columns]
        for place, level in enumerate(levels):
            row = place * head_count + head
            flag = flag_ref[level] == 1
            left = jnp.where(flag, gates[row : row + 1, :] * query_turned, key_turned)
            right = jnp.where(flag, wide(grad_here), wide(value_here))
            out_ref[place, head] = narrow(product(narrow(left), narrow(right), 1, 0))


def local_kernel(
    block_depth, head_size, class_ref, table_ref, q_ref, k_ref, v_ref, g_ref, qo_ref, ko_ref, vo_ref
):
    head_count = table_ref.shape[1]
    tokens = q_ref.shape[0]
    gates = gate_lanes(class_ref, table_ref, 0, block_depth + 1)
    source = lax.broadcasted_iota(jnp.int32, (tokens, tokens), 0)
    target = lax.broadcasted_iota(jnp.int32, (tokens, tokens), 1)
    apart = jnp.bitwise_xor(source, target)
    causal = source <= target
    for head in range(head_count):
        columns = pl.ds(head * head_size, head_size)
        query_here = q_ref[:, columns]
        key_here = k_ref[:, columns]
        value_here = v_ref[:, columns]
        grad_here = g_ref[:, columns]
        weight = jnp.broadcast_to(gates[head : head + 1, :], (tokens, tokens))
        for level in range(1, block_depth + 1):
            row = level * head_count + head
            weight = jnp.where(apart >= 2 ** (level - 1), gates[row : row + 1, :], weight)
        weight = jnp.where(causal, weight, 0.0)
        weighted_scores = narrow(weight * product(key_here, query_here, 1, 1))
        weighted_grads = narrow(weight * product(value_here, grad_here, 1, 1))
        qo_ref[:, columns] = product(weighted_grads, key_here, 0, 0)
        ko_ref[:, columns] = product(weighted_grads, query_here, 1, 0)
        vo_ref[:, columns] = product(weighted_scores, grad_here, 1, 0)


def gate_columns(class_ref, table_ref, first, last):
    return gate_lanes(class_ref, table_ref, first, last).T


def final_kernel(
    offset,
    head_size,
    total,
    inner,
    flag_ref,
    class_ref,
    table_ref,
    k_ref,
    v_ref,
    g_ref,
    ql_ref,
    kl_ref,
    vl_ref,
    zero_ref,
    one_ref,
    two_own_ref,
    two_other_ref,
    piece0_ref,
    piece1_ref,
    piece2_ref,
    piece3_ref,
    split_own_ref,
    split_other_ref,
    qo_ref,
    ko_ref,
    vo_ref,
    held_ref,
):
    head_count = table_ref.shape[1]
    half = head_count // 2
    quarter = head_count // 4
    eighth = head_count // 8
    gates = gate_columns(class_ref, table_ref, offset, offset + total)
    x_place = flag_ref[0]
    z_place = flag_ref[1] + 2 * flag_ref[2]
    core = flag_ref[inner]
    held_ref[0] = zero_ref[...]
    held_ref[1] = one_ref[...]
    held_ref[2, pl.ds(x_place * half, half)] = two_own_ref[...]
    held_ref[2, pl.ds((1 - x_place) * half, half)] = two_other_ref[...]
    pieces = (piece0_ref, piece1_ref, piece2_ref, piece3_ref)
    split = inner + 1
    for level in range(NEAR, split):
        for offs in range(4):
            first = jnp.bitwise_xor(z_place, offs) * quarter
            held_ref[level, pl.ds(first, quarter)] = pieces[offs][level - NEAR]
    for level in range(split, total):
        for offs in range(4):
            first = jnp.bitwise_xor(z_place, offs) * eighth
            rows = pl.ds(offs * eighth, eighth)
            held_ref[level, pl.ds(core * half + first, eighth)] = split_own_ref[level - split, rows]
            held_ref[level, pl.ds((1 - core) * half + first, eighth)] = split_other_ref[
                level - split, rows
            ]
    for head in range(head_count):
        columns = pl.ds(head * head_size, head_size)
        grad_here = g_ref[:, columns]
        query_total = ql_ref[:, columns]
        state_grad = jnp.zeros((head_size, head_size), jnp.float32)
        for level in range(total):
            state = held_ref[level, head]
            term = product(grad_here, state, 1, 1)
            row = level * head_count + head
            on = wide(flag_ref[level])
            query_total = query_total + (gates[:, row : row + 1] * on) * term
            state_grad = state_grad + wide(state) * (1.0 - on)
        grad_rounded = narrow(state_grad)
        qo_ref[:, columns] = narrow(query_total)
        ko_ref[:, columns] = narrow(
            kl_ref[:, columns] + product(v_ref[:, columns], grad_rounded, 1, 1)
        )
        vo_ref[:, columns] = narrow(
            vl_ref[:, columns] + product(k_ref[:, columns], grad_rounded, 1, 0)
        )


def per_device(query_rows, key_rows, value_rows, out_grad, gate_class, gate_table):
    row_count, width = query_rows.shape
    head_count = gate_table.shape[2]
    head_size = width // head_count
    inner_bits = level_bits(lax.axis_size("gy"))
    outer_bits = level_bits(lax.axis_size("gx"))
    total = inner_bits + outer_bits
    block_depth = level_bits(row_count)
    offset = block_depth + 1
    inner_index = lax.axis_index("gy")
    outer_index = lax.axis_index("gx")
    block_index = (outer_index << inner_bits) | inner_index
    flag_bits = (block_index >> jnp.arange(total, dtype=jnp.int32)) & 1
    inner_size = lax.axis_size("gy")
    device_count = inner_size * lax.axis_size("gx")

    def swap(block, *bits):
        mask = sum(1 << bit for bit in bits)
        if mask < inner_size:
            return lax.ppermute(block, "gy", [(i, i ^ mask) for i in range(inner_size)])
        if mask % inner_size == 0:
            mask = mask // inner_size
            size = lax.axis_size("gx")
            return lax.ppermute(block, "gx", [(i, i ^ mask) for i in range(size)])
        return lax.ppermute(block, ("gx", "gy"), [(i, i ^ mask) for i in range(device_count)])

    class_lanes = gate_class.reshape(1, row_count)
    table = jnp.transpose(gate_table, (1, 2, 0))
    smem = pl.BlockSpec(memory_space=pltpu.SMEM)
    vmem = pl.BlockSpec(memory_space=pltpu.VMEM)
    cell = (head_size, head_size)
    params = pltpu.CompilerParams(vmem_limit_bytes=VMEM_BYTES)

    def payloads(levels):
        flops = 2 * len(levels) * row_count * width * head_size
        return pl.pallas_call(
            functools.partial(payload_kernel, levels, offset, head_size),
            out_shape=jax.ShapeDtypeStruct((len(levels), head_count) + cell, jnp.bfloat16),
            in_specs=[smem] + [vmem] * 6,
            out_specs=vmem,
            compiler_params=params,
            cost_estimate=pl.CostEstimate(
                flops=flops, bytes_accessed=10 * row_count * width, transcendentals=0
            ),
        )(flag_bits, class_lanes, table, query_rows, key_rows, value_rows, out_grad)

    quarter = head_count // 4
    half = head_count // 2
    eighth = head_count // 8
    z_place = (inner_index >> 1) & 3
    x_place = inner_index & 1
    core = outer_index & 1
    split = inner_bits + 1
    whole_levels = split - NEAR
    split_levels = total - split

    upper = payloads(tuple(range(NEAR, total)))
    lead = upper[:whole_levels]
    late = upper[whole_levels:].reshape((split_levels, 2, half) + cell)
    late_other = lax.dynamic_index_in_dim(late, 1 - core, 1, keepdims=False)
    late_own = lax.dynamic_index_in_dim(late, core, 1, keepdims=False)
    sent = jnp.concatenate([upper[whole_levels - 1], late_other.reshape((-1,) + cell)], axis=0)
    seen = swap(sent, inner_bits)
    late_sum = narrow(wide(late_own) + wide(seen[head_count:].reshape((split_levels, half) + cell)))
    full = jnp.concatenate([lead[: whole_levels - 1], seen[None, :head_count]], axis=0)
    full = full.reshape((whole_levels, 4, quarter) + cell)
    late_sum = late_sum.reshape((split_levels, 4, eighth) + cell)

    def z_share(place):
        first = lax.dynamic_index_in_dim(full, place, 1, keepdims=False)
        second = lax.dynamic_index_in_dim(late_sum, place, 1, keepdims=False)
        return jnp.concatenate([first.reshape((-1,) + cell), second.reshape((-1,) + cell)], axis=0)

    came = [
        swap(z_share(z_place ^ offs), *[bit + 1 for bit in range(2) if offs >> bit & 1])
        for offs in (3, 2, 1)
    ]
    part = wide(z_share(z_place)) + wide(came[0]) + wide(came[1]) + wide(came[2])
    cut = whole_levels * quarter
    whole_part = part[:cut].reshape((whole_levels, quarter) + cell)
    split_part = part[cut:].reshape((split_levels, eighth) + cell)
    parts = {level: whole_part[level - NEAR] for level in range(NEAR, split)}
    parts.update({level: split_part[level - split] for level in range(split, total)})

    def flat(levels):
        return narrow(jnp.concatenate([parts[level] for level in levels], axis=0))

    for bit in range(NEAR, total - 1):
        if bit == inner_bits:
            continue
        going = [level for level in range(bit, total) if level != inner_bits or bit < inner_bits]
        seen_part = wide(swap(flat(going), bit))
        row = 0
        for level in going:
            size = parts[level].shape[0]
            got = seen_part[row : row + size]
            parts[level] = got if level == bit else parts[level] + got
            row += size
    top = total - 1
    below = list(range(NEAR, top))
    top_sent = flat([top])
    below_sent = flat(below)
    top_near = swap(top_sent, top)
    top_far = swap(top_sent, 0, top)
    below_far = swap(below_sent, 0)
    below_done = narrow(wide(below_sent) + wide(below_far))
    top_done = narrow(wide(top_near) + wide(top_far))
    shares = jnp.concatenate([below_done, top_done], axis=0)
    pieces = [shares] + [
        swap(shares, *[bit + 1 for bit in range(2) if offs >> bit & 1]) for offs in (1, 2, 3)
    ]
    split_own = jnp.stack(
        [piece[cut:].reshape((split_levels, eighth) + cell) for piece in pieces], axis=1
    ).reshape((split_levels, half) + cell)
    split_other = swap(split_own, inner_bits)
    whole_pieces = [piece[:cut].reshape((whole_levels, quarter) + cell) for piece in pieces]

    lower = payloads(tuple(range(NEAR)))
    low_two = lower[2].reshape((2, half) + cell)
    two_other = lax.dynamic_index_in_dim(low_two, 1 - x_place, 0, keepdims=False)
    two_own = lax.dynamic_index_in_dim(low_two, x_place, 0, keepdims=False)
    two_sum = wide(two_own) + wide(swap(two_other, 0))
    near_seen = swap(lower[:2], 0)
    zero_done = near_seen[0]
    one_done = swap(narrow(wide(lower[1]) + wide(near_seen[1])), 1)
    two_sum = two_sum + wide(swap(narrow(two_sum), 1))
    two_half = swap(narrow(two_sum), 2)
    two_rest = swap(two_half, 0)

    big = jax.ShapeDtypeStruct((row_count, width), jnp.float32)
    query_local, key_local, value_local = pl.pallas_call(
        functools.partial(local_kernel, block_depth, head_size),
        out_shape=(big, big, big),
        in_specs=[vmem] * 6,
        out_specs=(vmem, vmem, vmem),
        compiler_params=params,
        cost_estimate=pl.CostEstimate(
            flops=10 * row_count * width * row_count,
            bytes_accessed=20 * row_count * width,
            transcendentals=0,
        ),
    )(class_lanes, table, query_rows, key_rows, value_rows, out_grad)

    small = jax.ShapeDtypeStruct((row_count, width), jnp.bfloat16)
    return pl.pallas_call(
        functools.partial(final_kernel, offset, head_size, total, inner_bits),
        out_shape=(small, small, small),
        in_specs=[smem] + [vmem] * 18,
        out_specs=(vmem, vmem, vmem),
        scratch_shapes=[pltpu.VMEM((total, head_count) + cell, jnp.bfloat16)],
        compiler_params=params,
        cost_estimate=pl.CostEstimate(
            flops=(2 * total + 4) * row_count * width * head_size,
            bytes_accessed=24 * row_count * width,
            transcendentals=0,
        ),
    )(
        flag_bits,
        class_lanes,
        table,
        key_rows,
        value_rows,
        out_grad,
        query_local,
        key_local,
        value_local,
        zero_done,
        one_done,
        two_half,
        two_rest,
        *whole_pieces,
        split_own,
        split_other,
    )


def solution(mesh):
    rows = P(("gx", "gy"), None)
    return jax.shard_map(
        per_device,
        mesh=mesh,
        in_specs=(rows, rows, rows, rows, P(("gx", "gy")), P()),
        out_specs=(rows, rows, rows),
        check_vma=False,
    )
```

```python
import functools

import jax
import jax.numpy as jnp
from jax import lax
from jax.experimental import pallas as pl
from jax.experimental.pallas import tpu as pltpu
from jax.sharding import PartitionSpec as P

NEAR = 3
VMEM_BYTES = 16 * 1024 * 1024


def level_bits(amount):
    return amount.bit_length() - 1


def wide(values):
    return values.astype(jnp.float32)


def narrow(values):
    return values.astype(jnp.bfloat16)


def product(left, right, left_dim, right_dim):
    return lax.dot_general(
        left,
        right,
        (((left_dim,), (right_dim,)), ((), ())),
        preferred_element_type=jnp.float32,
    )


def gate_lanes(class_ref, table_ref, first, last):
    classes = table_ref.shape[2]
    tokens = class_ref.shape[1]
    rows = (last - first) * table_ref.shape[1]
    numbers = lax.broadcasted_iota(jnp.int32, (classes, tokens), 0)
    picker = (numbers == class_ref[...]).astype(jnp.float32)
    table = table_ref[first:last].reshape(rows, classes)
    return jnp.dot(
        table, picker, precision=lax.Precision.HIGHEST, preferred_element_type=jnp.float32
    )


def payload_cell(flags, gates, rows, level_places, q_ref, k_ref, v_ref, g_ref, columns, store):
    query_turned = wide(q_ref[:, columns].T)
    key_turned = wide(k_ref[:, columns].T)
    grad_here = wide(g_ref[:, columns])
    value_here = wide(v_ref[:, columns])
    for place in level_places:
        row = rows[place]
        flag = flags[place] == 1
        left = jnp.where(flag, gates[row : row + 1, :] * query_turned, key_turned)
        right = jnp.where(flag, grad_here, value_here)
        store(place, narrow(product(narrow(left), narrow(right), 1, 0)))


def upper_kernel(
    levels,
    split,
    offset,
    head_size,
    flag_ref,
    class_hbm,
    table_hbm,
    q_hbm,
    k_hbm,
    v_hbm,
    g_hbm,
    sent_ref,
    keep_ref,
    *rest,
):
    lead_refs = rest[:-7]
    class_ref, table_ref, q_ref, k_ref, v_ref, g_ref, arrived = rest[-7:]
    moves = [
        pltpu.make_async_copy(source, target, arrived.at[place])
        for place, (source, target) in enumerate(
            (
                (class_hbm, class_ref),
                (table_hbm, table_ref),
                (q_hbm, q_ref),
                (k_hbm, k_ref),
                (g_hbm, g_ref),
                (v_hbm, v_ref),
            )
        )
    ]
    for move in moves:
        move.start()
    moves[0].wait()
    moves[1].wait()
    head_count = table_ref.shape[1]
    half = head_count // 2
    core = flag_ref[split - 1]
    gates = gate_lanes(class_ref, table_ref, offset + levels[0], offset + levels[-1] + 1)
    for move in moves[2:]:
        move.wait()
    flags = [flag_ref[level] for level in levels]
    for head in range(head_count):
        rows = [place * head_count + head for place in range(len(levels))]

        def store(place, value):
            level = levels[place]
            if level < split - 1:
                lead_refs[0][level - levels[0], head] = value
            elif level == split - 1:
                sent_ref[head] = value
            else:
                row = (level - split) * half + head % half

                @pl.when(core == head // half)
                def _():
                    keep_ref[row] = value

                @pl.when(core != head // half)
                def _():
                    sent_ref[head_count + row] = value

        columns = pl.ds(head * head_size, head_size)
        payload_cell(
            flags, gates, rows, range(len(levels)), q_ref, k_ref, v_ref, g_ref, columns, store
        )


def share_kernel(head_count, places, flag_ref, seen_ref, keep_ref, *refs):
    lead_refs = refs[:-4]
    out_refs = refs[-4:]
    quarter = head_count // 4
    eighth = head_count // 8
    z_place = flag_ref[1] + 2 * flag_ref[2]
    for offs in range(4):
        place = jnp.bitwise_xor(z_place, offs)
        row = 0
        for lead in range(places[0] - 1):
            out_refs[offs][row : row + quarter] = lead_refs[0][lead, pl.ds(place * quarter, quarter)]
            row += quarter
        out_refs[offs][row : row + quarter] = seen_ref[pl.ds(place * quarter, quarter)]
        row += quarter
        for late in range(places[1]):
            first = late * (head_count // 2) + place * eighth
            total = wide(keep_ref[pl.ds(first, eighth)])
            total = total + wide(seen_ref[pl.ds(head_count + first, eighth)])
            out_refs[offs][row : row + eighth] = narrow(total)
            row += eighth


def lower_kernel(
    offset,
    head_size,
    flag_ref,
    class_ref,
    table_ref,
    q_ref,
    k_ref,
    v_ref,
    g_ref,
    after_ref,
    two_own_ref,
    two_other_ref,
    near_ref,
):
    head_count = table_ref.shape[1]
    half = head_count // 2
    x_place = flag_ref[0]
    gates = gate_lanes(class_ref, table_ref, offset, offset + NEAR)
    flags = [flag_ref[level] for level in range(NEAR)]
    for head in range(head_count):
        rows = [place * head_count + head for place in range(NEAR)]

        def store(place, value):
            if place < 2:
                near_ref[place, head] = value
                return

            @pl.when(x_place == head // half)
            def _():
                two_own_ref[head % half] = value

            @pl.when(x_place != head // half)
            def _():
                two_other_ref[head % half] = value

        columns = pl.ds(head * head_size, head_size)
        payload_cell(flags, gates, rows, range(NEAR), q_ref, k_ref, v_ref, g_ref, columns, store)


def four_sum_kernel(top_rows, own_ref, *refs):
    came_refs = refs[:-2]
    below_ref, top_ref = refs[-2:]
    total = wide(own_ref[...])
    for came_ref in came_refs:
        total = total + wide(came_ref[...])
    rows = total.shape[0] - top_rows
    below_ref[...] = narrow(total[:rows])
    top_ref[...] = narrow(total[rows:])


def pair_sum_kernel(below_ref, far_ref, near_top_ref, far_top_ref, out_ref):
    rows = below_ref.shape[0]
    out_ref[:rows] = narrow(wide(below_ref[...]) + wide(far_ref[...]))
    out_ref[rows:] = narrow(wide(near_top_ref[...]) + wide(far_top_ref[...]))


def gather_kernel(cut, piece0_ref, piece1_ref, piece2_ref, piece3_ref, out_ref):
    for offs, piece_ref in enumerate((piece0_ref, piece1_ref, piece2_ref, piece3_ref)):
        split_levels = out_ref.shape[0]
        eighth = out_ref.shape[1] // 4
        for level in range(split_levels):
            first = cut + level * eighth
            out_ref[level, offs * eighth : (offs + 1) * eighth] = piece_ref[first : first + eighth]


def near_sum_kernel(near_ref, seen_ref, one_ref):
    one_ref[...] = narrow(wide(near_ref[1]) + wide(seen_ref[1]))


def local_kernel(
    block_depth, head_size, class_ref, table_ref, q_ref, k_ref, v_ref, g_ref, qo_ref, ko_ref, vo_ref
):
    head_count = table_ref.shape[1]
    tokens = q_ref.shape[0]
    gates = gate_lanes(class_ref, table_ref, 0, block_depth + 1)
    source = lax.broadcasted_iota(jnp.int32, (tokens, tokens), 0)
    target = lax.broadcasted_iota(jnp.int32, (tokens, tokens), 1)
    apart = jnp.bitwise_xor(source, target)
    causal = source <= target
    for head in range(head_count):
        columns = pl.ds(head * head_size, head_size)
        query_here = q_ref[:, columns]
        key_here = k_ref[:, columns]
        value_here = v_ref[:, columns]
        grad_here = g_ref[:, columns]
        weight = jnp.broadcast_to(gates[head : head + 1, :], (tokens, tokens))
        for level in range(1, block_depth + 1):
            row = level * head_count + head
            weight = jnp.where(apart >= 2 ** (level - 1), gates[row : row + 1, :], weight)
        weight = jnp.where(causal, weight, 0.0)
        weighted_scores = narrow(weight * product(key_here, query_here, 1, 1))
        weighted_grads = narrow(weight * product(value_here, grad_here, 1, 1))
        qo_ref[:, columns] = product(weighted_grads, key_here, 0, 0)
        ko_ref[:, columns] = product(weighted_grads, query_here, 1, 0)
        vo_ref[:, columns] = product(weighted_scores, grad_here, 1, 0)


def gate_columns(class_ref, table_ref, first, last):
    return gate_lanes(class_ref, table_ref, first, last).T


def final_kernel(
    offset,
    head_size,
    total,
    inner,
    flag_ref,
    class_ref,
    table_ref,
    k_ref,
    v_ref,
    g_ref,
    ql_ref,
    kl_ref,
    vl_ref,
    near_ref,
    one_ref,
    two_own_ref,
    two_other_ref,
    piece0_ref,
    piece1_ref,
    piece2_ref,
    piece3_ref,
    split_own_ref,
    split_other_ref,
    qo_ref,
    ko_ref,
    vo_ref,
    held_ref,
):
    head_count = table_ref.shape[1]
    half = head_count // 2
    quarter = head_count // 4
    eighth = head_count // 8
    gates = gate_columns(class_ref, table_ref, offset, offset + total)
    x_place = flag_ref[0]
    z_place = flag_ref[1] + 2 * flag_ref[2]
    core = flag_ref[inner]
    held_ref[0] = near_ref[0]
    held_ref[1] = one_ref[...]
    held_ref[2, pl.ds(x_place * half, half)] = two_own_ref[...]
    held_ref[2, pl.ds((1 - x_place) * half, half)] = two_other_ref[...]
    pieces = (piece0_ref, piece1_ref, piece2_ref, piece3_ref)
    split = inner + 1
    for level in range(NEAR, split):
        for offs in range(4):
            first = jnp.bitwise_xor(z_place, offs) * quarter
            row = (level - NEAR) * quarter
            held_ref[level, pl.ds(first, quarter)] = pieces[offs][row : row + quarter]
    for level in range(split, total):
        for offs in range(4):
            first = jnp.bitwise_xor(z_place, offs) * eighth
            rows = pl.ds(offs * eighth, eighth)
            held_ref[level, pl.ds(core * half + first, eighth)] = split_own_ref[level - split, rows]
            held_ref[level, pl.ds((1 - core) * half + first, eighth)] = split_other_ref[
                level - split, rows
            ]
    for head in range(head_count):
        columns = pl.ds(head * head_size, head_size)
        grad_here = g_ref[:, columns]
        query_total = ql_ref[:, columns]
        state_grad = jnp.zeros((head_size, head_size), jnp.float32)
        for level in range(total):
            state = held_ref[level, head]
            term = product(grad_here, state, 1, 1)
            row = level * head_count + head
            on = wide(flag_ref[level])
            query_total = query_total + (gates[:, row : row + 1] * on) * term
            state_grad = state_grad + wide(state) * (1.0 - on)
        grad_rounded = narrow(state_grad)
        qo_ref[:, columns] = narrow(query_total)
        ko_ref[:, columns] = narrow(
            kl_ref[:, columns] + product(v_ref[:, columns], grad_rounded, 1, 1)
        )
        vo_ref[:, columns] = narrow(
            vl_ref[:, columns] + product(k_ref[:, columns], grad_rounded, 1, 0)
        )


def per_device(query_rows, key_rows, value_rows, out_grad, gate_class, gate_table):
    row_count, width = query_rows.shape
    head_count = gate_table.shape[2]
    head_size = width // head_count
    inner_bits = level_bits(lax.axis_size("gy"))
    outer_bits = level_bits(lax.axis_size("gx"))
    total = inner_bits + outer_bits
    block_depth = level_bits(row_count)
    offset = block_depth + 1
    inner_index = lax.axis_index("gy")
    outer_index = lax.axis_index("gx")
    block_index = (outer_index << inner_bits) | inner_index
    flag_bits = (block_index >> jnp.arange(total, dtype=jnp.int32)) & 1
    inner_size = lax.axis_size("gy")
    device_count = inner_size * lax.axis_size("gx")

    def swap(block, *bits):
        mask = sum(1 << bit for bit in bits)
        if mask < inner_size:
            return lax.ppermute(block, "gy", [(i, i ^ mask) for i in range(inner_size)])
        if mask % inner_size == 0:
            mask = mask // inner_size
            size = lax.axis_size("gx")
            return lax.ppermute(block, "gx", [(i, i ^ mask) for i in range(size)])
        return lax.ppermute(block, ("gx", "gy"), [(i, i ^ mask) for i in range(device_count)])

    class_lanes = gate_class.reshape(1, row_count)
    table = jnp.transpose(gate_table, (1, 2, 0))
    smem = pl.BlockSpec(memory_space=pltpu.SMEM)
    vmem = pl.BlockSpec(memory_space=pltpu.VMEM)
    hbm = pl.BlockSpec(memory_space=pltpu.HBM)
    anywhere = pl.BlockSpec(memory_space=pl.ANY)
    cell = (head_size, head_size)
    params = pltpu.CompilerParams(vmem_limit_bytes=VMEM_BYTES)

    def cells(*lead):
        return jax.ShapeDtypeStruct(lead + cell, jnp.bfloat16)

    def call(kernel, in_specs, outs, operands, flops=0, scratch=()):
        moved = sum(operand.size * operand.dtype.itemsize for operand in operands)
        return pl.pallas_call(
            kernel,
            out_shape=outs,
            in_specs=in_specs,
            out_specs=jax.tree.map(lambda _: vmem, outs),
            scratch_shapes=scratch,
            compiler_params=params,
            cost_estimate=pl.CostEstimate(flops=flops, bytes_accessed=moved, transcendentals=0),
        )(*operands)

    quarter = head_count // 4
    half = head_count // 2
    eighth = head_count // 8
    split = inner_bits + 1
    whole_levels = split - NEAR
    split_levels = total - split
    cut = whole_levels * quarter
    share_rows = cut + split_levels * eighth
    block = pltpu.VMEM((row_count, width), jnp.bfloat16)

    levels = tuple(range(NEAR, total))
    outs = (cells(head_count + split_levels * half), cells(split_levels * half))
    if whole_levels > 1:
        outs = outs + (cells(whole_levels - 1, head_count),)
    sent, keep, *lead = call(
        functools.partial(upper_kernel, levels, split, offset, head_size),
        [smem] + [hbm] * 6,
        outs,
        (flag_bits, class_lanes, table, query_rows, key_rows, value_rows, out_grad),
        flops=2 * len(levels) * row_count * width * head_size,
        scratch=[
            pltpu.VMEM(class_lanes.shape, jnp.int32),
            pltpu.VMEM(table.shape, jnp.float32),
            block,
            block,
            block,
            block,
            pltpu.SemaphoreType.DMA((6,)),
        ],
    )
    seen = swap(sent, inner_bits)
    own_share, *shares_out = call(
        functools.partial(share_kernel, head_count, (whole_levels, split_levels)),
        [smem] + [vmem] * (2 + len(lead)),
        (cells(share_rows),) * 4,
        (flag_bits, seen, keep, *lead),
    )

    def z_bits(offs):
        return [bit + 1 for bit in range(2) if offs >> bit & 1]

    came = [swap(shares_out[offs - 1], *z_bits(offs)) for offs in (3, 2, 1)]
    top = total - 1
    below, top_sent = call(
        functools.partial(four_sum_kernel, eighth),
        [vmem] * 4,
        (cells(share_rows - eighth), cells(eighth)),
        (own_share, *came),
    )
    middle = [bit for bit in range(NEAR, top) if bit != inner_bits]
    if middle:
        part = wide(jnp.concatenate([below, top_sent], axis=0))
        parts = {
            level: part[(level - NEAR) * quarter : (level - NEAR + 1) * quarter]
            for level in range(NEAR, split)
        }
        for level in range(split, total):
            row = cut + (level - split) * eighth
            parts[level] = part[row : row + eighth]
        for bit in middle:
            going = range(bit, total)
            block_sent = narrow(jnp.concatenate([parts[level] for level in going], axis=0))
            seen_part = wide(swap(block_sent, bit))
            row = 0
            for level in going:
                size = parts[level].shape[0]
                got = seen_part[row : row + size]
                parts[level] = got if level == bit else parts[level] + got
                row += size
        below = narrow(jnp.concatenate([parts[level] for level in range(NEAR, top)], axis=0))
        top_sent = narrow(parts[top])
    shares = call(
        pair_sum_kernel,
        [vmem] * 4,
        cells(share_rows),
        (below, swap(below, 0), swap(top_sent, top), swap(top_sent, 0, top)),
    )
    pieces = [shares] + [swap(shares, *z_bits(offs)) for offs in (1, 2, 3)]
    split_own = call(
        functools.partial(gather_kernel, cut), [vmem] * 4, cells(split_levels, half), pieces
    )
    split_other = swap(split_own, inner_bits)

    two_own, two_other, near = call(
        functools.partial(lower_kernel, offset, head_size),
        [smem] + [vmem] * 6 + [anywhere],
        (cells(half), cells(half), cells(2, head_count)),
        (flag_bits, class_lanes, table, query_rows, key_rows, value_rows, out_grad, own_share),
        flops=2 * NEAR * row_count * width * head_size,
    )
    two_sum = narrow(wide(two_own) + wide(swap(two_other, 0)))
    near_seen = swap(near, 0)
    one_sum = call(near_sum_kernel, [vmem] * 2, cells(head_count), (near, near_seen))
    one_done = swap(one_sum, 1)
    two_sum = narrow(wide(two_sum) + wide(swap(two_sum, 1)))
    two_half = swap(two_sum, 2)
    two_rest = swap(two_half, 0)

    big = jax.ShapeDtypeStruct((row_count, width), jnp.float32)
    query_local, key_local, value_local = call(
        functools.partial(local_kernel, block_depth, head_size),
        [vmem] * 6,
        (big, big, big),
        (class_lanes, table, query_rows, key_rows, value_rows, out_grad),
        flops=10 * row_count * width * row_count,
    )

    small = jax.ShapeDtypeStruct((row_count, width), jnp.bfloat16)
    return call(
        functools.partial(final_kernel, offset, head_size, total, inner_bits),
        [smem] + [vmem] * 18,
        (small, small, small),
        (
            flag_bits,
            class_lanes,
            table,
            key_rows,
            value_rows,
            out_grad,
            query_local,
            key_local,
            value_local,
            near_seen,
            one_done,
            two_half,
            two_rest,
            *pieces,
            split_own,
            split_other,
        ),
        flops=(2 * total + 4) * row_count * width * head_size,
        scratch=[pltpu.VMEM((total, head_count) + cell, jnp.bfloat16)],
    )


def solution(mesh):
    rows = P(("gx", "gy"), None)
    return jax.shard_map(
        per_device,
        mesh=mesh,
        in_specs=(rows, rows, rows, rows, P(("gx", "gy")), P()),
        out_specs=(rows, rows, rows),
        check_vma=False,
    )
```

```python
import functools

import jax
import jax.numpy as jnp
from jax import lax
from jax.experimental import pallas as pl
from jax.experimental.pallas import tpu as pltpu
from jax.sharding import PartitionSpec as P

NEAR = 3
VMEM_BYTES = 16 * 1024 * 1024
FIRST_BYTES = 16 * 1024 * 1024


def level_bits(amount):
    return amount.bit_length() - 1


def wide(values):
    return values.astype(jnp.float32)


def narrow(values):
    return values.astype(jnp.bfloat16)


def product(left, right, left_dim, right_dim):
    return lax.dot_general(
        left,
        right,
        (((left_dim,), (right_dim,)), ((), ())),
        preferred_element_type=jnp.float32,
    )


def gate_lanes(class_ref, table_ref, first, last):
    classes = table_ref.shape[2]
    tokens = class_ref.shape[1]
    rows = (last - first) * table_ref.shape[1]
    numbers = lax.broadcasted_iota(jnp.int32, (classes, tokens), 0)
    picker = (numbers == class_ref[...]).astype(jnp.float32)
    table = table_ref[first:last].reshape(rows, classes)
    return jnp.dot(
        table, picker, precision=lax.Precision.HIGHEST, preferred_element_type=jnp.float32
    )


def payload_cell(flags, gates, rows, level_places, q_ref, k_ref, v_ref, g_ref, columns, store):
    query_turned = wide(q_ref[:, columns].T)
    key_turned = wide(k_ref[:, columns].T)
    grad_here = wide(g_ref[:, columns])
    value_here = wide(v_ref[:, columns])
    for place in level_places:
        row = rows[place]
        flag = flags[place] == 1
        left = jnp.where(flag, gates[row : row + 1, :] * query_turned, key_turned)
        right = jnp.where(flag, grad_here, value_here)
        store(place, narrow(product(narrow(left), narrow(right), 1, 0)))


def upper_kernel(
    levels,
    split,
    offset,
    head_size,
    flag_ref,
    class_hbm,
    table_hbm,
    q_hbm,
    k_hbm,
    v_hbm,
    g_hbm,
    sent_ref,
    keep_ref,
    *rest,
):
    lead_refs = rest[:-8]
    class_ref, table_ref, q_ref, k_ref, v_ref, g_ref, late_ref, arrived = rest[-8:]
    moves = [
        pltpu.make_async_copy(source, target, arrived.at[place])
        for place, (source, target) in enumerate(
            (
                (class_hbm, class_ref),
                (table_hbm, table_ref),
                (q_hbm, q_ref),
                (k_hbm, k_ref),
                (g_hbm, g_ref),
                (v_hbm, v_ref),
            )
        )
    ]
    for move in moves:
        move.start()
    moves[0].wait()
    moves[1].wait()
    head_count = table_ref.shape[1]
    half = head_count // 2
    core = flag_ref[split - 1]
    gates = gate_lanes(class_ref, table_ref, offset + levels[0], offset + levels[-1] + 1)
    for move in moves[2:]:
        move.wait()
    flags = [flag_ref[level] for level in levels]
    for head in range(head_count):
        rows = [place * head_count + head for place in range(len(levels))]

        def store(place, value):
            level = levels[place]
            if level < split - 1:
                lead_refs[0][level - levels[0], head] = value
            elif level == split - 1:
                sent_ref[head] = value
            else:
                late_ref[level - split, head] = value

        columns = pl.ds(head * head_size, head_size)
        payload_cell(
            flags, gates, rows, range(len(levels)), q_ref, k_ref, v_ref, g_ref, columns, store
        )
    for place in range(levels[-1] + 1 - split):
        row = place * half
        keep_ref[row : row + half] = late_ref[place, pl.ds(core * half, half)]
        sent_ref[head_count + row : head_count + row + half] = late_ref[
            place, pl.ds((1 - core) * half, half)
        ]


def share_kernel(head_count, places, flag_ref, seen_ref, keep_ref, after_ref, *refs):
    lead_refs = refs[:-4]
    out_refs = refs[-4:]
    quarter = head_count // 4
    eighth = head_count // 8
    z_place = flag_ref[1] + 2 * flag_ref[2]
    for offs in range(4):
        place = jnp.bitwise_xor(z_place, offs)
        row = 0
        for lead in range(places[0] - 1):
            out_refs[offs][row : row + quarter] = lead_refs[0][lead, pl.ds(place * quarter, quarter)]
            row += quarter
        out_refs[offs][row : row + quarter] = seen_ref[pl.ds(place * quarter, quarter)]
        row += quarter
        for late in range(places[1]):
            first = late * (head_count // 2) + place * eighth
            total = wide(keep_ref[pl.ds(first, eighth)])
            total = total + wide(seen_ref[pl.ds(head_count + first, eighth)])
            out_refs[offs][row : row + eighth] = narrow(total)
            row += eighth


def lower_kernel(
    offset,
    head_size,
    flag_ref,
    class_ref,
    table_ref,
    q_ref,
    k_ref,
    v_ref,
    g_ref,
    after_ref,
    two_own_ref,
    sent_ref,
    zero_ref,
    two_ref,
):
    head_count = table_ref.shape[1]
    half = head_count // 2
    x_place = flag_ref[0]
    gates = gate_lanes(class_ref, table_ref, offset, offset + NEAR)
    flags = [flag_ref[level] for level in range(NEAR)]
    for head in range(head_count):
        rows = [place * head_count + head for place in range(NEAR)]

        def store(place, value):
            if place == 0:
                zero_ref[head] = value
            elif place == 1:
                sent_ref[half + head] = value
            else:
                two_ref[head] = value

        columns = pl.ds(head * head_size, head_size)
        payload_cell(flags, gates, rows, range(NEAR), q_ref, k_ref, v_ref, g_ref, columns, store)
    two_own_ref[...] = two_ref[pl.ds(x_place * half, half)]
    sent_ref[:half] = two_ref[pl.ds((1 - x_place) * half, half)]


def four_sum_kernel(top_rows, own_ref, after_ref, *refs):
    came_refs = refs[:-2]
    below_ref, top_ref = refs[-2:]
    total = wide(own_ref[...])
    for came_ref in came_refs:
        total = total + wide(came_ref[...])
    rows = total.shape[0] - top_rows
    below_ref[...] = narrow(total[:rows])
    top_ref[...] = narrow(total[rows:])


def pair_sum_kernel(below_ref, far_ref, near_top_ref, far_top_ref, out_ref):
    rows = below_ref.shape[0]
    out_ref[:rows] = narrow(wide(below_ref[...]) + wide(far_ref[...]))
    out_ref[rows:] = narrow(wide(near_top_ref[...]) + wide(far_top_ref[...]))


def gather_kernel(cut, piece0_ref, piece1_ref, piece2_ref, piece3_ref, out_ref):
    for offs, piece_ref in enumerate((piece0_ref, piece1_ref, piece2_ref, piece3_ref)):
        split_levels = out_ref.shape[0]
        eighth = out_ref.shape[1] // 4
        for level in range(split_levels):
            first = cut + level * eighth
            out_ref[level, offs * eighth : (offs + 1) * eighth] = piece_ref[first : first + eighth]


def lower_sum_kernel(own_ref, sent_ref, seen_ref, after_ref, two_ref, one_ref):
    half = own_ref.shape[0]
    two_ref[...] = narrow(wide(own_ref[...]) + wide(seen_ref[:half]))
    one_ref[...] = narrow(wide(sent_ref[half:]) + wide(seen_ref[half:]))


def local_kernel(
    block_depth,
    head_size,
    class_ref,
    table_ref,
    q_ref,
    k_ref,
    v_ref,
    g_ref,
    after_ref,
    held_ref,
    qo_ref,
    ko_ref,
    vo_ref,
    held_out_ref,
):
    head_count = table_ref.shape[1]
    tokens = q_ref.shape[0]
    gates = gate_lanes(class_ref, table_ref, 0, block_depth + 1)
    source = lax.broadcasted_iota(jnp.int32, (tokens, tokens), 0)
    target = lax.broadcasted_iota(jnp.int32, (tokens, tokens), 1)
    apart = jnp.bitwise_xor(source, target)
    causal = source <= target
    for head in range(head_count):
        columns = pl.ds(head * head_size, head_size)
        query_here = q_ref[:, columns]
        key_here = k_ref[:, columns]
        value_here = v_ref[:, columns]
        grad_here = g_ref[:, columns]
        weight = jnp.broadcast_to(gates[head : head + 1, :], (tokens, tokens))
        for level in range(1, block_depth + 1):
            row = level * head_count + head
            weight = jnp.where(apart >= 2 ** (level - 1), gates[row : row + 1, :], weight)
        weight = jnp.where(causal, weight, 0.0)
        weighted_scores = narrow(weight * product(key_here, query_here, 1, 1))
        weighted_grads = narrow(weight * product(value_here, grad_here, 1, 1))
        qo_ref[:, columns] = product(weighted_grads, key_here, 0, 0)
        ko_ref[:, columns] = product(weighted_grads, query_here, 1, 0)
        vo_ref[:, columns] = product(weighted_scores, grad_here, 1, 0)


def gate_columns(class_ref, table_ref, first, last):
    return gate_lanes(class_ref, table_ref, first, last).T


def final_kernel(
    offset,
    head_size,
    total,
    inner,
    flag_ref,
    class_ref,
    table_ref,
    k_ref,
    v_ref,
    g_ref,
    ql_ref,
    kl_ref,
    vl_ref,
    zero_ref,
    one_ref,
    two_own_ref,
    two_other_ref,
    piece0_ref,
    piece1_ref,
    piece2_ref,
    piece3_ref,
    split_own_ref,
    split_other_ref,
    qo_ref,
    ko_ref,
    vo_ref,
    held_ref,
):
    head_count = table_ref.shape[1]
    half = head_count // 2
    quarter = head_count // 4
    eighth = head_count // 8
    gates = gate_columns(class_ref, table_ref, offset, offset + total)
    x_place = flag_ref[0]
    z_place = flag_ref[1] + 2 * flag_ref[2]
    core = flag_ref[inner]
    held_ref[0] = zero_ref[...]
    held_ref[1] = one_ref[...]
    held_ref[2, pl.ds(x_place * half, half)] = two_own_ref[...]
    held_ref[2, pl.ds((1 - x_place) * half, half)] = two_other_ref[...]
    pieces = (piece0_ref, piece1_ref, piece2_ref, piece3_ref)
    split = inner + 1
    for level in range(NEAR, split):
        for offs in range(4):
            first = jnp.bitwise_xor(z_place, offs) * quarter
            row = (level - NEAR) * quarter
            held_ref[level, pl.ds(first, quarter)] = pieces[offs][row : row + quarter]
    for level in range(split, total):
        for offs in range(4):
            first = jnp.bitwise_xor(z_place, offs) * eighth
            rows = pl.ds(offs * eighth, eighth)
            held_ref[level, pl.ds(core * half + first, eighth)] = split_own_ref[level - split, rows]
            held_ref[level, pl.ds((1 - core) * half + first, eighth)] = split_other_ref[
                level - split, rows
            ]
    for head in range(head_count):
        columns = pl.ds(head * head_size, head_size)
        grad_here = g_ref[:, columns]
        query_total = ql_ref[:, columns]
        state_grad = jnp.zeros((head_size, head_size), jnp.float32)
        for level in range(total):
            state = held_ref[level, head]
            term = product(grad_here, state, 1, 1)
            row = level * head_count + head
            on = wide(flag_ref[level])
            query_total = query_total + (gates[:, row : row + 1] * on) * term
            state_grad = state_grad + wide(state) * (1.0 - on)
        grad_rounded = narrow(state_grad)
        qo_ref[:, columns] = narrow(query_total)
        ko_ref[:, columns] = narrow(
            kl_ref[:, columns] + product(v_ref[:, columns], grad_rounded, 1, 1)
        )
        vo_ref[:, columns] = narrow(
            vl_ref[:, columns] + product(k_ref[:, columns], grad_rounded, 1, 0)
        )


def per_device(query_rows, key_rows, value_rows, out_grad, gate_class, gate_table):
    row_count, width = query_rows.shape
    head_count = gate_table.shape[2]
    head_size = width // head_count
    inner_bits = level_bits(lax.axis_size("gy"))
    outer_bits = level_bits(lax.axis_size("gx"))
    total = inner_bits + outer_bits
    block_depth = level_bits(row_count)
    offset = block_depth + 1
    inner_index = lax.axis_index("gy")
    outer_index = lax.axis_index("gx")
    block_index = (outer_index << inner_bits) | inner_index
    flag_bits = (block_index >> jnp.arange(total, dtype=jnp.int32)) & 1
    inner_size = lax.axis_size("gy")
    device_count = inner_size * lax.axis_size("gx")

    def swap(block, *bits):
        mask = sum(1 << bit for bit in bits)
        if mask < inner_size:
            return lax.ppermute(block, "gy", [(i, i ^ mask) for i in range(inner_size)])
        if mask % inner_size == 0:
            mask = mask // inner_size
            size = lax.axis_size("gx")
            return lax.ppermute(block, "gx", [(i, i ^ mask) for i in range(size)])
        return lax.ppermute(block, ("gx", "gy"), [(i, i ^ mask) for i in range(device_count)])

    class_lanes = gate_class.reshape(1, row_count)
    table = jnp.transpose(gate_table, (1, 2, 0))
    smem = pl.BlockSpec(memory_space=pltpu.SMEM)
    vmem = pl.BlockSpec(memory_space=pltpu.VMEM)
    hbm = pl.BlockSpec(memory_space=pltpu.HBM)
    anywhere = pl.BlockSpec(memory_space=pl.ANY)
    cell = (head_size, head_size)

    def cells(*lead):
        return jax.ShapeDtypeStruct(lead + cell, jnp.bfloat16)

    def call(kernel, in_specs, outs, operands, flops=0, scratch=(), grant=VMEM_BYTES, out_specs=None, aliases=None):
        moved = sum(operand.size * operand.dtype.itemsize for operand in operands)
        return pl.pallas_call(
            kernel,
            out_shape=outs,
            in_specs=in_specs,
            out_specs=out_specs or jax.tree.map(lambda _: vmem, outs),
            input_output_aliases=aliases or {},
            scratch_shapes=scratch,
            compiler_params=pltpu.CompilerParams(vmem_limit_bytes=grant),
            cost_estimate=pl.CostEstimate(flops=flops, bytes_accessed=moved, transcendentals=0),
        )(*operands)

    quarter = head_count // 4
    half = head_count // 2
    eighth = head_count // 8
    split = inner_bits + 1
    whole_levels = split - NEAR
    split_levels = total - split
    cut = whole_levels * quarter
    share_rows = cut + split_levels * eighth
    block = pltpu.VMEM((row_count, width), jnp.bfloat16)

    levels = tuple(range(NEAR, total))
    first_reads = (class_lanes, table, query_rows, key_rows, value_rows, out_grad)
    outs = (cells(head_count + split_levels * half), cells(split_levels * half))
    if whole_levels > 1:
        outs = outs + (cells(whole_levels - 1, head_count),)
    sent, keep, *lead = call(
        functools.partial(upper_kernel, levels, split, offset, head_size),
        [smem] + [hbm] * 6,
        outs,
        (flag_bits, *[pltpu.with_memory_space_constraint(held, pltpu.HBM) for held in first_reads]),
        flops=2 * len(levels) * row_count * width * head_size,
        scratch=[
            pltpu.VMEM(class_lanes.shape, jnp.int32),
            pltpu.VMEM(table.shape, jnp.float32),
            block,
            block,
            block,
            block,
            pltpu.VMEM((split_levels, head_count) + cell, jnp.bfloat16),
            pltpu.SemaphoreType.DMA((6,)),
        ],
        grant=FIRST_BYTES,
    )
    seen = swap(sent, inner_bits)
    two_own, lower_sent, zero = call(
        functools.partial(lower_kernel, offset, head_size),
        [smem] + [vmem] * 6 + [anywhere],
        (cells(half), cells(half + head_count), cells(head_count)),
        (flag_bits, class_lanes, table, query_rows, key_rows, value_rows, out_grad, keep),
        flops=2 * NEAR * row_count * width * head_size,
        scratch=[pltpu.VMEM((head_count,) + cell, jnp.bfloat16)],
    )
    own_share, *shares_out = call(
        functools.partial(share_kernel, head_count, (whole_levels, split_levels)),
        [smem] + [vmem] * 2 + [anywhere] + [vmem] * len(lead),
        (cells(share_rows),) * 4,
        (flag_bits, seen, keep, two_own, *lead),
    )
    big = jax.ShapeDtypeStruct((row_count, width), jnp.float32)
    query_local, key_local, value_local, zero = call(
        functools.partial(local_kernel, block_depth, head_size),
        [vmem] * 6 + [anywhere] * 2,
        (big, big, big, cells(head_count)),
        (class_lanes, table, query_rows, key_rows, value_rows, out_grad, own_share, zero),
        out_specs=(vmem, vmem, vmem, anywhere),
        aliases={7: 3},
        flops=10 * row_count * width * row_count,
    )

    def z_bits(offs):
        return [bit + 1 for bit in range(2) if offs >> bit & 1]

    came = [swap(shares_out[offs - 1], *z_bits(offs)) for offs in (3, 2, 1)]
    top = total - 1
    below, top_sent = call(
        functools.partial(four_sum_kernel, eighth),
        [vmem, anywhere] + [vmem] * 3,
        (cells(share_rows - eighth), cells(eighth)),
        (own_share, query_local, *came),
    )
    middle = [bit for bit in range(NEAR, top) if bit != inner_bits]
    if middle:
        part = wide(jnp.concatenate([below, top_sent], axis=0))
        parts = {
            level: part[(level - NEAR) * quarter : (level - NEAR + 1) * quarter]
            for level in range(NEAR, split)
        }
        for level in range(split, total):
            row = cut + (level - split) * eighth
            parts[level] = part[row : row + eighth]
        for bit in middle:
            going = range(bit, total)
            block_sent = narrow(jnp.concatenate([parts[level] for level in going], axis=0))
            seen_part = wide(swap(block_sent, bit))
            row = 0
            for level in going:
                size = parts[level].shape[0]
                got = seen_part[row : row + size]
                parts[level] = got if level == bit else parts[level] + got
                row += size
        below = narrow(jnp.concatenate([parts[level] for level in range(NEAR, top)], axis=0))
        top_sent = narrow(parts[top])
    shares = call(
        pair_sum_kernel,
        [vmem] * 4,
        cells(share_rows),
        (below, swap(below, 0), swap(top_sent, top), swap(top_sent, 0, top)),
    )
    pieces = [shares] + [swap(shares, *z_bits(offs)) for offs in (1, 2, 3)]
    split_own = call(
        functools.partial(gather_kernel, cut), [vmem] * 4, cells(split_levels, half), pieces
    )
    split_other = swap(split_own, inner_bits)

    two_sum, one_sum = call(
        lower_sum_kernel,
        [vmem] * 3 + [anywhere],
        (cells(half), cells(head_count)),
        (two_own, lower_sent, swap(lower_sent, 0), query_local),
    )
    two_sum = narrow(wide(two_sum) + wide(swap(two_sum, 1)))
    two_half = swap(two_sum, 2)
    two_rest = swap(two_half, 0)
    one_done = swap(one_sum, 1)
    zero_done = swap(zero, 0)

    small = jax.ShapeDtypeStruct((row_count, width), jnp.bfloat16)
    return call(
        functools.partial(final_kernel, offset, head_size, total, inner_bits),
        [smem] + [vmem] * 18,
        (small, small, small),
        (
            flag_bits,
            class_lanes,
            table,
            key_rows,
            value_rows,
            out_grad,
            query_local,
            key_local,
            value_local,
            zero_done,
            one_done,
            two_half,
            two_rest,
            *pieces,
            split_own,
            split_other,
        ),
        flops=(2 * total + 4) * row_count * width * head_size,
        scratch=[pltpu.VMEM((total, head_count) + cell, jnp.bfloat16)],
    )


def solution(mesh):
    rows = P(("gx", "gy"), None)
    return jax.shard_map(
        per_device,
        mesh=mesh,
        in_specs=(rows, rows, rows, rows, P(("gx", "gy")), P()),
        out_specs=(rows, rows, rows),
        check_vma=False,
    )
```

```python
import functools

import jax
import jax.numpy as jnp
from jax import lax
from jax.experimental import pallas as pl
from jax.experimental.pallas import tpu as pltpu
from jax.sharding import PartitionSpec as P

NEAR = 3
VMEM_BYTES = 16 * 1024 * 1024
FIRST_BYTES = 16 * 1024 * 1024


def level_bits(amount):
    return amount.bit_length() - 1


def wide(values):
    return values.astype(jnp.float32)


def narrow(values):
    return values.astype(jnp.bfloat16)


def product(left, right, left_dim, right_dim):
    return lax.dot_general(
        left,
        right,
        (((left_dim,), (right_dim,)), ((), ())),
        preferred_element_type=jnp.float32,
    )


def gate_lanes(class_ref, table_ref, first, last):
    classes = table_ref.shape[2]
    tokens = class_ref.shape[1]
    rows = (last - first) * table_ref.shape[1]
    numbers = lax.broadcasted_iota(jnp.int32, (classes, tokens), 0)
    picker = (numbers == class_ref[...]).astype(jnp.float32)
    table = table_ref[first:last].reshape(rows, classes)
    return jnp.dot(
        table, picker, precision=lax.Precision.HIGHEST, preferred_element_type=jnp.float32
    )


def payload_cell(flags, gates, rows, level_places, q_ref, k_ref, v_ref, g_ref, columns, store):
    query_turned = wide(q_ref[:, columns].T)
    key_turned = wide(k_ref[:, columns].T)
    grad_here = wide(g_ref[:, columns])
    value_here = wide(v_ref[:, columns])
    for place in level_places:
        row = rows[place]
        flag = flags[place] == 1
        left = jnp.where(flag, gates[row : row + 1, :] * query_turned, key_turned)
        right = jnp.where(flag, grad_here, value_here)
        store(place, narrow(product(narrow(left), narrow(right), 1, 0)))


def upper_kernel(
    levels,
    split,
    offset,
    head_size,
    flag_ref,
    class_hbm,
    table_hbm,
    q_hbm,
    k_hbm,
    v_hbm,
    g_hbm,
    sent_ref,
    keep_ref,
    *rest,
):
    lead_refs = rest[:-8]
    class_ref, table_ref, q_ref, k_ref, v_ref, g_ref, late_ref, arrived = rest[-8:]
    moves = [
        pltpu.make_async_copy(source, target, arrived.at[place])
        for place, (source, target) in enumerate(
            (
                (class_hbm, class_ref),
                (table_hbm, table_ref),
                (q_hbm, q_ref),
                (k_hbm, k_ref),
                (g_hbm, g_ref),
                (v_hbm, v_ref),
            )
        )
    ]
    for move in moves:
        move.start()
    moves[0].wait()
    moves[1].wait()
    head_count = table_ref.shape[1]
    half = head_count // 2
    core = flag_ref[split - 1]
    gates = gate_lanes(class_ref, table_ref, offset + levels[0], offset + levels[-1] + 1)
    for move in moves[2:]:
        move.wait()
    flags = [flag_ref[level] for level in levels]
    for head in range(head_count):
        rows = [place * head_count + head for place in range(len(levels))]

        def store(place, value):
            level = levels[place]
            if level < split - 1:
                lead_refs[0][level - levels[0], head] = value
            elif level == split - 1:
                sent_ref[head] = value
            else:
                late_ref[level - split, head] = value

        columns = pl.ds(head * head_size, head_size)
        payload_cell(
            flags, gates, rows, range(len(levels)), q_ref, k_ref, v_ref, g_ref, columns, store
        )
    for place in range(levels[-1] + 1 - split):
        row = place * half
        keep_ref[row : row + half] = late_ref[place, pl.ds(core * half, half)]
        sent_ref[head_count + row : head_count + row + half] = late_ref[
            place, pl.ds((1 - core) * half, half)
        ]


def share_kernel(head_count, places, flag_ref, seen_ref, keep_ref, after_ref, *refs):
    lead_refs = refs[:-4]
    out_refs = refs[-4:]
    quarter = head_count // 4
    eighth = head_count // 8
    z_place = flag_ref[1] + 2 * flag_ref[2]
    for offs in range(4):
        place = jnp.bitwise_xor(z_place, offs)
        row = 0
        for lead in range(places[0] - 1):
            out_refs[offs][row : row + quarter] = lead_refs[0][lead, pl.ds(place * quarter, quarter)]
            row += quarter
        out_refs[offs][row : row + quarter] = seen_ref[pl.ds(place * quarter, quarter)]
        row += quarter
        for late in range(places[1]):
            first = late * (head_count // 2) + place * eighth
            total = wide(keep_ref[pl.ds(first, eighth)])
            total = total + wide(seen_ref[pl.ds(head_count + first, eighth)])
            out_refs[offs][row : row + eighth] = narrow(total)
            row += eighth


def lower_kernel(
    offset,
    head_size,
    flag_ref,
    class_ref,
    table_ref,
    q_ref,
    k_ref,
    v_ref,
    g_ref,
    after_ref,
    two_own_ref,
    two_other_ref,
    near_ref,
    two_ref,
):
    head_count = table_ref.shape[1]
    half = head_count // 2
    x_place = flag_ref[0]
    gates = gate_lanes(class_ref, table_ref, offset, offset + NEAR)
    flags = [flag_ref[level] for level in range(NEAR)]
    for head in range(head_count):
        rows = [place * head_count + head for place in range(NEAR)]

        def store(place, value):
            if place < 2:
                near_ref[place, head] = value
            else:
                two_ref[head] = value

        columns = pl.ds(head * head_size, head_size)
        payload_cell(flags, gates, rows, range(NEAR), q_ref, k_ref, v_ref, g_ref, columns, store)
    two_own_ref[...] = two_ref[pl.ds(x_place * half, half)]
    two_other_ref[...] = two_ref[pl.ds((1 - x_place) * half, half)]


def four_sum_kernel(top_rows, own_ref, after_ref, *refs):
    came_refs = refs[:-2]
    below_ref, top_ref = refs[-2:]
    total = wide(own_ref[...])
    for came_ref in came_refs:
        total = total + wide(came_ref[...])
    rows = total.shape[0] - top_rows
    below_ref[...] = narrow(total[:rows])
    top_ref[...] = narrow(total[rows:])


def pair_sum_kernel(below_ref, far_ref, near_top_ref, far_top_ref, out_ref):
    rows = below_ref.shape[0]
    out_ref[:rows] = narrow(wide(below_ref[...]) + wide(far_ref[...]))
    out_ref[rows:] = narrow(wide(near_top_ref[...]) + wide(far_top_ref[...]))


def gather_kernel(cut, piece0_ref, piece1_ref, piece2_ref, piece3_ref, out_ref):
    for offs, piece_ref in enumerate((piece0_ref, piece1_ref, piece2_ref, piece3_ref)):
        split_levels = out_ref.shape[0]
        eighth = out_ref.shape[1] // 4
        for level in range(split_levels):
            first = cut + level * eighth
            out_ref[level, offs * eighth : (offs + 1) * eighth] = piece_ref[first : first + eighth]


def two_sum_kernel(own_ref, seen_ref, after_ref, out_ref):
    out_ref[...] = narrow(wide(own_ref[...]) + wide(seen_ref[...]))


def near_sum_kernel(near_ref, seen_ref, one_ref):
    one_ref[...] = narrow(wide(near_ref[1]) + wide(seen_ref[1]))


def local_kernel(
    block_depth,
    head_size,
    class_ref,
    table_ref,
    q_ref,
    k_ref,
    v_ref,
    g_ref,
    after_ref,
    qo_ref,
    ko_ref,
    vo_ref,
):
    head_count = table_ref.shape[1]
    tokens = q_ref.shape[0]
    gates = gate_lanes(class_ref, table_ref, 0, block_depth + 1)
    source = lax.broadcasted_iota(jnp.int32, (tokens, tokens), 0)
    target = lax.broadcasted_iota(jnp.int32, (tokens, tokens), 1)
    apart = jnp.bitwise_xor(source, target)
    causal = source <= target
    for head in range(head_count):
        columns = pl.ds(head * head_size, head_size)
        query_here = q_ref[:, columns]
        key_here = k_ref[:, columns]
        value_here = v_ref[:, columns]
        grad_here = g_ref[:, columns]
        weight = jnp.broadcast_to(gates[head : head + 1, :], (tokens, tokens))
        for level in range(1, block_depth + 1):
            row = level * head_count + head
            weight = jnp.where(apart >= 2 ** (level - 1), gates[row : row + 1, :], weight)
        weight = jnp.where(causal, weight, 0.0)
        weighted_scores = narrow(weight * product(key_here, query_here, 1, 1))
        weighted_grads = narrow(weight * product(value_here, grad_here, 1, 1))
        qo_ref[:, columns] = product(weighted_grads, key_here, 0, 0)
        ko_ref[:, columns] = product(weighted_grads, query_here, 1, 0)
        vo_ref[:, columns] = product(weighted_scores, grad_here, 1, 0)


def gate_columns(class_ref, table_ref, first, last):
    return gate_lanes(class_ref, table_ref, first, last).T


def final_kernel(
    offset,
    head_size,
    total,
    inner,
    flag_ref,
    class_ref,
    table_ref,
    k_ref,
    v_ref,
    g_ref,
    ql_ref,
    kl_ref,
    vl_ref,
    near_ref,
    one_ref,
    two_own_ref,
    two_other_ref,
    piece0_ref,
    piece1_ref,
    piece2_ref,
    piece3_ref,
    split_own_ref,
    split_other_ref,
    qo_ref,
    ko_ref,
    vo_ref,
    held_ref,
):
    head_count = table_ref.shape[1]
    half = head_count // 2
    quarter = head_count // 4
    eighth = head_count // 8
    gates = gate_columns(class_ref, table_ref, offset, offset + total)
    x_place = flag_ref[0]
    z_place = flag_ref[1] + 2 * flag_ref[2]
    core = flag_ref[inner]
    held_ref[0] = near_ref[0]
    held_ref[1] = one_ref[...]
    held_ref[2, pl.ds(x_place * half, half)] = two_own_ref[...]
    held_ref[2, pl.ds((1 - x_place) * half, half)] = two_other_ref[...]
    pieces = (piece0_ref, piece1_ref, piece2_ref, piece3_ref)
    split = inner + 1
    for level in range(NEAR, split):
        for offs in range(4):
            first = jnp.bitwise_xor(z_place, offs) * quarter
            row = (level - NEAR) * quarter
            held_ref[level, pl.ds(first, quarter)] = pieces[offs][row : row + quarter]
    for level in range(split, total):
        for offs in range(4):
            first = jnp.bitwise_xor(z_place, offs) * eighth
            rows = pl.ds(offs * eighth, eighth)
            held_ref[level, pl.ds(core * half + first, eighth)] = split_own_ref[level - split, rows]
            held_ref[level, pl.ds((1 - core) * half + first, eighth)] = split_other_ref[
                level - split, rows
            ]
    for head in range(head_count):
        columns = pl.ds(head * head_size, head_size)
        grad_here = g_ref[:, columns]
        query_total = ql_ref[:, columns]
        state_grad = jnp.zeros((head_size, head_size), jnp.float32)
        for level in range(total):
            state = held_ref[level, head]
            term = product(grad_here, state, 1, 1)
            row = level * head_count + head
            on = wide(flag_ref[level])
            query_total = query_total + (gates[:, row : row + 1] * on) * term
            state_grad = state_grad + wide(state) * (1.0 - on)
        grad_rounded = narrow(state_grad)
        qo_ref[:, columns] = narrow(query_total)
        ko_ref[:, columns] = narrow(
            kl_ref[:, columns] + product(v_ref[:, columns], grad_rounded, 1, 1)
        )
        vo_ref[:, columns] = narrow(
            vl_ref[:, columns] + product(k_ref[:, columns], grad_rounded, 1, 0)
        )


def per_device(query_rows, key_rows, value_rows, out_grad, gate_class, gate_table):
    row_count, width = query_rows.shape
    head_count = gate_table.shape[2]
    head_size = width // head_count
    inner_bits = level_bits(lax.axis_size("gy"))
    outer_bits = level_bits(lax.axis_size("gx"))
    total = inner_bits + outer_bits
    block_depth = level_bits(row_count)
    offset = block_depth + 1
    inner_index = lax.axis_index("gy")
    outer_index = lax.axis_index("gx")
    block_index = (outer_index << inner_bits) | inner_index
    flag_bits = (block_index >> jnp.arange(total, dtype=jnp.int32)) & 1
    inner_size = lax.axis_size("gy")
    device_count = inner_size * lax.axis_size("gx")

    def swap(block, *bits):
        mask = sum(1 << bit for bit in bits)
        if mask < inner_size:
            return lax.ppermute(block, "gy", [(i, i ^ mask) for i in range(inner_size)])
        if mask % inner_size == 0:
            mask = mask // inner_size
            size = lax.axis_size("gx")
            return lax.ppermute(block, "gx", [(i, i ^ mask) for i in range(size)])
        return lax.ppermute(block, ("gx", "gy"), [(i, i ^ mask) for i in range(device_count)])

    class_lanes = gate_class.reshape(1, row_count)
    table = jnp.transpose(gate_table, (1, 2, 0))
    smem = pl.BlockSpec(memory_space=pltpu.SMEM)
    vmem = pl.BlockSpec(memory_space=pltpu.VMEM)
    hbm = pl.BlockSpec(memory_space=pltpu.HBM)
    anywhere = pl.BlockSpec(memory_space=pl.ANY)
    cell = (head_size, head_size)

    def cells(*lead):
        return jax.ShapeDtypeStruct(lead + cell, jnp.bfloat16)

    def call(kernel, in_specs, outs, operands, flops=0, scratch=(), grant=VMEM_BYTES):
        moved = sum(operand.size * operand.dtype.itemsize for operand in operands)
        return pl.pallas_call(
            kernel,
            out_shape=outs,
            in_specs=in_specs,
            out_specs=jax.tree.map(lambda _: vmem, outs),
            scratch_shapes=scratch,
            compiler_params=pltpu.CompilerParams(vmem_limit_bytes=grant),
            cost_estimate=pl.CostEstimate(flops=flops, bytes_accessed=moved, transcendentals=0),
        )(*operands)

    quarter = head_count // 4
    half = head_count // 2
    eighth = head_count // 8
    split = inner_bits + 1
    whole_levels = split - NEAR
    split_levels = total - split
    cut = whole_levels * quarter
    share_rows = cut + split_levels * eighth
    block = pltpu.VMEM((row_count, width), jnp.bfloat16)

    levels = tuple(range(NEAR, total))
    first_reads = (class_lanes, table, query_rows, key_rows, value_rows, out_grad)
    outs = (cells(head_count + split_levels * half), cells(split_levels * half))
    if whole_levels > 1:
        outs = outs + (cells(whole_levels - 1, head_count),)
    sent, keep, *lead = call(
        functools.partial(upper_kernel, levels, split, offset, head_size),
        [smem] + [hbm] * 6,
        outs,
        (flag_bits, *[pltpu.with_memory_space_constraint(held, pltpu.HBM) for held in first_reads]),
        flops=2 * len(levels) * row_count * width * head_size,
        scratch=[
            pltpu.VMEM(class_lanes.shape, jnp.int32),
            pltpu.VMEM(table.shape, jnp.float32),
            block,
            block,
            block,
            block,
            pltpu.VMEM((split_levels, head_count) + cell, jnp.bfloat16),
            pltpu.SemaphoreType.DMA((6,)),
        ],
        grant=FIRST_BYTES,
    )
    seen = swap(sent, inner_bits)
    two_own, two_other, near = call(
        functools.partial(lower_kernel, offset, head_size),
        [smem] + [vmem] * 6 + [anywhere],
        (cells(half), cells(half), cells(2, head_count)),
        (flag_bits, class_lanes, table, query_rows, key_rows, value_rows, out_grad, keep),
        flops=2 * NEAR * row_count * width * head_size,
        scratch=[pltpu.VMEM((head_count,) + cell, jnp.bfloat16)],
    )
    own_share, *shares_out = call(
        functools.partial(share_kernel, head_count, (whole_levels, split_levels)),
        [smem] + [vmem] * 2 + [anywhere] + [vmem] * len(lead),
        (cells(share_rows),) * 4,
        (flag_bits, seen, keep, two_own, *lead),
    )
    big = jax.ShapeDtypeStruct((row_count, width), jnp.float32)
    query_local, key_local, value_local = call(
        functools.partial(local_kernel, block_depth, head_size),
        [vmem] * 6 + [anywhere],
        (big, big, big),
        (class_lanes, table, query_rows, key_rows, value_rows, out_grad, own_share),
        flops=10 * row_count * width * row_count,
    )

    def z_bits(offs):
        return [bit + 1 for bit in range(2) if offs >> bit & 1]

    came = [swap(shares_out[offs - 1], *z_bits(offs)) for offs in (3, 2, 1)]
    top = total - 1
    below, top_sent = call(
        functools.partial(four_sum_kernel, eighth),
        [vmem, anywhere] + [vmem] * 3,
        (cells(share_rows - eighth), cells(eighth)),
        (own_share, query_local, *came),
    )
    middle = [bit for bit in range(NEAR, top) if bit != inner_bits]
    if middle:
        part = wide(jnp.concatenate([below, top_sent], axis=0))
        parts = {
            level: part[(level - NEAR) * quarter : (level - NEAR + 1) * quarter]
            for level in range(NEAR, split)
        }
        for level in range(split, total):
            row = cut + (level - split) * eighth
            parts[level] = part[row : row + eighth]
        for bit in middle:
            going = range(bit, total)
            block_sent = narrow(jnp.concatenate([parts[level] for level in going], axis=0))
            seen_part = wide(swap(block_sent, bit))
            row = 0
            for level in going:
                size = parts[level].shape[0]
                got = seen_part[row : row + size]
                parts[level] = got if level == bit else parts[level] + got
                row += size
        below = narrow(jnp.concatenate([parts[level] for level in range(NEAR, top)], axis=0))
        top_sent = narrow(parts[top])
    two_sum = call(
        two_sum_kernel,
        [vmem] * 2 + [anywhere],
        cells(half),
        (two_own, swap(two_other, 0), query_local),
    )
    two_sum = call(
        two_sum_kernel, [vmem] * 2 + [anywhere], cells(half), (two_sum, swap(two_sum, 1), two_sum)
    )
    two_half = swap(two_sum, 2)
    shares = call(
        pair_sum_kernel,
        [vmem] * 4,
        cells(share_rows),
        (below, swap(below, 0), swap(top_sent, top), swap(top_sent, 0, top)),
    )
    two_rest = swap(two_half, 0)
    near_seen = swap(near, 0)
    one_done = swap(call(near_sum_kernel, [vmem] * 2, cells(head_count), (near, near_seen)), 1)
    pieces = [shares] + [swap(shares, *z_bits(offs)) for offs in (1, 2, 3)]
    split_own = call(
        functools.partial(gather_kernel, cut), [vmem] * 4, cells(split_levels, half), pieces
    )
    split_other = swap(split_own, inner_bits)

    small = jax.ShapeDtypeStruct((row_count, width), jnp.bfloat16)
    return call(
        functools.partial(final_kernel, offset, head_size, total, inner_bits),
        [smem] + [vmem] * 18,
        (small, small, small),
        (
            flag_bits,
            class_lanes,
            table,
            key_rows,
            value_rows,
            out_grad,
            query_local,
            key_local,
            value_local,
            near_seen,
            one_done,
            two_half,
            two_rest,
            *pieces,
            split_own,
            split_other,
        ),
        flops=(2 * total + 4) * row_count * width * head_size,
        scratch=[pltpu.VMEM((total, head_count) + cell, jnp.bfloat16)],
    )


def solution(mesh):
    rows = P(("gx", "gy"), None)
    return jax.shard_map(
        per_device,
        mesh=mesh,
        in_specs=(rows, rows, rows, rows, P(("gx", "gy")), P()),
        out_specs=(rows, rows, rows),
        check_vma=False,
    )
```

```python
import functools

import jax
import jax.numpy as jnp
from jax import lax
from jax.experimental import pallas as pl
from jax.experimental.pallas import tpu as pltpu
from jax.sharding import PartitionSpec as P

NEAR = 3
VMEM_BYTES = 16 * 1024 * 1024
FIRST_BYTES = 16 * 1024 * 1024


def level_bits(amount):
    return amount.bit_length() - 1


def wide(values):
    return values.astype(jnp.float32)


def narrow(values):
    return values.astype(jnp.bfloat16)


def product(left, right, left_dim, right_dim):
    return lax.dot_general(
        left,
        right,
        (((left_dim,), (right_dim,)), ((), ())),
        preferred_element_type=jnp.float32,
    )


def gate_lanes(class_ref, table_ref, first, last):
    classes = table_ref.shape[2]
    tokens = class_ref.shape[1]
    rows = (last - first) * table_ref.shape[1]
    numbers = lax.broadcasted_iota(jnp.int32, (classes, tokens), 0)
    picker = (numbers == class_ref[...]).astype(jnp.float32)
    table = table_ref[first:last].reshape(rows, classes)
    return jnp.dot(
        table, picker, precision=lax.Precision.HIGHEST, preferred_element_type=jnp.float32
    )


def payload_cell(flags, gates, rows, level_places, q_ref, k_ref, v_ref, g_ref, columns, store):
    query_turned = wide(q_ref[:, columns].T)
    key_turned = wide(k_ref[:, columns].T)
    grad_here = wide(g_ref[:, columns])
    value_here = wide(v_ref[:, columns])
    for place in level_places:
        row = rows[place]
        flag = flags[place] == 1
        left = jnp.where(flag, gates[row : row + 1, :] * query_turned, key_turned)
        right = jnp.where(flag, grad_here, value_here)
        store(place, narrow(product(narrow(left), narrow(right), 1, 0)))


def upper_kernel(
    levels,
    split,
    offset,
    head_size,
    flag_ref,
    class_hbm,
    table_hbm,
    q_hbm,
    k_hbm,
    v_hbm,
    g_hbm,
    sent_ref,
    keep_ref,
    *rest,
):
    lead_refs = rest[:-8]
    class_ref, table_ref, q_ref, k_ref, v_ref, g_ref, late_ref, arrived = rest[-8:]
    moves = [
        pltpu.make_async_copy(source, target, arrived.at[place])
        for place, (source, target) in enumerate(
            (
                (class_hbm, class_ref),
                (table_hbm, table_ref),
                (q_hbm, q_ref),
                (k_hbm, k_ref),
                (g_hbm, g_ref),
                (v_hbm, v_ref),
            )
        )
    ]
    for move in moves:
        move.start()
    moves[0].wait()
    moves[1].wait()
    head_count = table_ref.shape[1]
    half = head_count // 2
    core = flag_ref[split - 1]
    gates = gate_lanes(class_ref, table_ref, offset + levels[0], offset + levels[-1] + 1)
    for move in moves[2:]:
        move.wait()
    flags = [flag_ref[level] for level in levels]
    for head in range(head_count):
        rows = [place * head_count + head for place in range(len(levels))]

        def store(place, value):
            level = levels[place]
            if level < split - 1:
                lead_refs[0][level - levels[0], head] = value
            elif level == split - 1:
                sent_ref[head] = value
            else:
                late_ref[level - split, head] = value

        columns = pl.ds(head * head_size, head_size)
        payload_cell(
            flags, gates, rows, range(len(levels)), q_ref, k_ref, v_ref, g_ref, columns, store
        )
    for place in range(levels[-1] + 1 - split):
        row = place * half
        keep_ref[row : row + half] = late_ref[place, pl.ds(core * half, half)]
        sent_ref[head_count + row : head_count + row + half] = late_ref[
            place, pl.ds((1 - core) * half, half)
        ]


def share_kernel(head_count, places, flag_ref, seen_ref, keep_ref, after_ref, *refs):
    lead_refs = refs[:-4]
    out_refs = refs[-4:]
    quarter = head_count // 4
    eighth = head_count // 8
    z_place = flag_ref[1] + 2 * flag_ref[2]
    for offs in range(4):
        place = jnp.bitwise_xor(z_place, offs)
        row = 0
        for lead in range(places[0] - 1):
            out_refs[offs][row : row + quarter] = lead_refs[0][lead, pl.ds(place * quarter, quarter)]
            row += quarter
        out_refs[offs][row : row + quarter] = seen_ref[pl.ds(place * quarter, quarter)]
        row += quarter
        for late in range(places[1]):
            first = late * (head_count // 2) + place * eighth
            total = wide(keep_ref[pl.ds(first, eighth)])
            total = total + wide(seen_ref[pl.ds(head_count + first, eighth)])
            out_refs[offs][row : row + eighth] = narrow(total)
            row += eighth


def lower_kernel(
    offset,
    head_size,
    flag_ref,
    class_ref,
    table_ref,
    q_ref,
    k_ref,
    v_ref,
    g_ref,
    after_ref,
    two_own_ref,
    two_other_ref,
    zero_ref,
    one_ref,
    two_ref,
):
    head_count = table_ref.shape[1]
    half = head_count // 2
    x_place = flag_ref[0]
    gates = gate_lanes(class_ref, table_ref, offset, offset + NEAR)
    flags = [flag_ref[level] for level in range(NEAR)]
    for head in range(head_count):
        rows = [place * head_count + head for place in range(NEAR)]

        def store(place, value):
            (zero_ref, one_ref, two_ref)[place][head] = value

        columns = pl.ds(head * head_size, head_size)
        payload_cell(flags, gates, rows, range(NEAR), q_ref, k_ref, v_ref, g_ref, columns, store)
    two_own_ref[...] = two_ref[pl.ds(x_place * half, half)]
    two_other_ref[...] = two_ref[pl.ds((1 - x_place) * half, half)]


def four_sum_kernel(top_rows, own_ref, after_ref, *refs):
    came_refs = refs[:-2]
    below_ref, top_ref = refs[-2:]
    total = wide(own_ref[...])
    for came_ref in came_refs:
        total = total + wide(came_ref[...])
    rows = total.shape[0] - top_rows
    below_ref[...] = narrow(total[:rows])
    top_ref[...] = narrow(total[rows:])


def pair_sum_kernel(below_ref, far_ref, near_top_ref, far_top_ref, *refs):
    out_ref = refs[-1]
    rows = below_ref.shape[0]
    out_ref[:rows] = narrow(wide(below_ref[...]) + wide(far_ref[...]))
    out_ref[rows:] = narrow(wide(near_top_ref[...]) + wide(far_top_ref[...]))


def gather_kernel(cut, piece0_ref, piece1_ref, piece2_ref, piece3_ref, after_ref, out_ref):
    for offs, piece_ref in enumerate((piece0_ref, piece1_ref, piece2_ref, piece3_ref)):
        split_levels = out_ref.shape[0]
        eighth = out_ref.shape[1] // 4
        for level in range(split_levels):
            first = cut + level * eighth
            out_ref[level, offs * eighth : (offs + 1) * eighth] = piece_ref[first : first + eighth]


def two_sum_kernel(own_ref, seen_ref, after_ref, out_ref):
    out_ref[...] = narrow(wide(own_ref[...]) + wide(seen_ref[...]))


def local_kernel(
    block_depth,
    head_size,
    class_ref,
    table_ref,
    q_ref,
    k_ref,
    v_ref,
    g_ref,
    after_ref,
    qo_ref,
    ko_ref,
    vo_ref,
):
    head_count = table_ref.shape[1]
    tokens = q_ref.shape[0]
    gates = gate_lanes(class_ref, table_ref, 0, block_depth + 1)
    source = lax.broadcasted_iota(jnp.int32, (tokens, tokens), 0)
    target = lax.broadcasted_iota(jnp.int32, (tokens, tokens), 1)
    apart = jnp.bitwise_xor(source, target)
    causal = source <= target
    for head in range(head_count):
        columns = pl.ds(head * head_size, head_size)
        query_here = q_ref[:, columns]
        key_here = k_ref[:, columns]
        value_here = v_ref[:, columns]
        grad_here = g_ref[:, columns]
        weight = jnp.broadcast_to(gates[head : head + 1, :], (tokens, tokens))
        for level in range(1, block_depth + 1):
            row = level * head_count + head
            weight = jnp.where(apart >= 2 ** (level - 1), gates[row : row + 1, :], weight)
        weight = jnp.where(causal, weight, 0.0)
        weighted_scores = narrow(weight * product(key_here, query_here, 1, 1))
        weighted_grads = narrow(weight * product(value_here, grad_here, 1, 1))
        qo_ref[:, columns] = product(weighted_grads, key_here, 0, 0)
        ko_ref[:, columns] = product(weighted_grads, query_here, 1, 0)
        vo_ref[:, columns] = product(weighted_scores, grad_here, 1, 0)


def gate_columns(class_ref, table_ref, first, last):
    return gate_lanes(class_ref, table_ref, first, last).T


def final_kernel(
    offset,
    head_size,
    total,
    inner,
    flag_ref,
    class_ref,
    table_ref,
    k_ref,
    v_ref,
    g_ref,
    ql_ref,
    kl_ref,
    vl_ref,
    zero_ref,
    one_ref,
    two_own_ref,
    two_other_ref,
    piece0_ref,
    piece1_ref,
    piece2_ref,
    piece3_ref,
    split_own_ref,
    split_other_ref,
    qo_ref,
    ko_ref,
    vo_ref,
    held_ref,
):
    head_count = table_ref.shape[1]
    half = head_count // 2
    quarter = head_count // 4
    eighth = head_count // 8
    gates = gate_columns(class_ref, table_ref, offset, offset + total)
    x_place = flag_ref[0]
    z_place = flag_ref[1] + 2 * flag_ref[2]
    core = flag_ref[inner]
    held_ref[0] = zero_ref[...]
    held_ref[1] = one_ref[...]
    held_ref[2, pl.ds(x_place * half, half)] = two_own_ref[...]
    held_ref[2, pl.ds((1 - x_place) * half, half)] = two_other_ref[...]
    pieces = (piece0_ref, piece1_ref, piece2_ref, piece3_ref)
    split = inner + 1
    for level in range(NEAR, split):
        for offs in range(4):
            first = jnp.bitwise_xor(z_place, offs) * quarter
            row = (level - NEAR) * quarter
            held_ref[level, pl.ds(first, quarter)] = pieces[offs][row : row + quarter]
    for level in range(split, total):
        for offs in range(4):
            first = jnp.bitwise_xor(z_place, offs) * eighth
            rows = pl.ds(offs * eighth, eighth)
            held_ref[level, pl.ds(core * half + first, eighth)] = split_own_ref[level - split, rows]
            held_ref[level, pl.ds((1 - core) * half + first, eighth)] = split_other_ref[
                level - split, rows
            ]
    for head in range(head_count):
        columns = pl.ds(head * head_size, head_size)
        grad_here = g_ref[:, columns]
        query_total = ql_ref[:, columns]
        state_grad = jnp.zeros((head_size, head_size), jnp.float32)
        for level in range(total):
            state = held_ref[level, head]
            term = product(grad_here, state, 1, 1)
            row = level * head_count + head
            on = wide(flag_ref[level])
            query_total = query_total + (gates[:, row : row + 1] * on) * term
            state_grad = state_grad + wide(state) * (1.0 - on)
        grad_rounded = narrow(state_grad)
        qo_ref[:, columns] = narrow(query_total)
        ko_ref[:, columns] = narrow(
            kl_ref[:, columns] + product(v_ref[:, columns], grad_rounded, 1, 1)
        )
        vo_ref[:, columns] = narrow(
            vl_ref[:, columns] + product(k_ref[:, columns], grad_rounded, 1, 0)
        )


def per_device(query_rows, key_rows, value_rows, out_grad, gate_class, gate_table):
    row_count, width = query_rows.shape
    head_count = gate_table.shape[2]
    head_size = width // head_count
    inner_bits = level_bits(lax.axis_size("gy"))
    outer_bits = level_bits(lax.axis_size("gx"))
    total = inner_bits + outer_bits
    block_depth = level_bits(row_count)
    offset = block_depth + 1
    inner_index = lax.axis_index("gy")
    outer_index = lax.axis_index("gx")
    block_index = (outer_index << inner_bits) | inner_index
    flag_bits = (block_index >> jnp.arange(total, dtype=jnp.int32)) & 1
    inner_size = lax.axis_size("gy")
    device_count = inner_size * lax.axis_size("gx")

    def swap(block, *bits):
        mask = sum(1 << bit for bit in bits)
        if mask < inner_size:
            return lax.ppermute(block, "gy", [(i, i ^ mask) for i in range(inner_size)])
        if mask % inner_size == 0:
            mask = mask // inner_size
            size = lax.axis_size("gx")
            return lax.ppermute(block, "gx", [(i, i ^ mask) for i in range(size)])
        return lax.ppermute(block, ("gx", "gy"), [(i, i ^ mask) for i in range(device_count)])

    class_lanes = gate_class.reshape(1, row_count)
    table = jnp.transpose(gate_table, (1, 2, 0))
    smem = pl.BlockSpec(memory_space=pltpu.SMEM)
    vmem = pl.BlockSpec(memory_space=pltpu.VMEM)
    hbm = pl.BlockSpec(memory_space=pltpu.HBM)
    anywhere = pl.BlockSpec(memory_space=pl.ANY)
    cell = (head_size, head_size)

    def cells(*lead):
        return jax.ShapeDtypeStruct(lead + cell, jnp.bfloat16)

    def call(kernel, in_specs, outs, operands, flops=0, scratch=(), grant=VMEM_BYTES, carry=()):
        moved = sum(operand.size * operand.dtype.itemsize for operand in operands)
        outs = tuple(outs) if isinstance(outs, (tuple, list)) else (outs,)
        count, taken = len(outs), len(operands)
        if carry:
            inner = kernel
            held = len(carry)

            def kernel(*refs):
                inner(*refs[:taken], *refs[taken + held : taken + held + count], *refs[taken + 2 * held + count :])

        results = pl.pallas_call(
            kernel,
            out_shape=outs + tuple(jax.ShapeDtypeStruct(item.shape, item.dtype) for item in carry),
            in_specs=in_specs + [anywhere] * len(carry),
            out_specs=(vmem,) * count + (anywhere,) * len(carry),
            input_output_aliases={taken + place: count + place for place in range(len(carry))},
            scratch_shapes=scratch,
            compiler_params=pltpu.CompilerParams(vmem_limit_bytes=grant),
            cost_estimate=pl.CostEstimate(flops=flops, bytes_accessed=moved, transcendentals=0),
        )(*operands, *carry)
        return results if len(results) > 1 else results[0]

    quarter = head_count // 4
    half = head_count // 2
    eighth = head_count // 8
    split = inner_bits + 1
    whole_levels = split - NEAR
    split_levels = total - split
    cut = whole_levels * quarter
    share_rows = cut + split_levels * eighth
    block = pltpu.VMEM((row_count, width), jnp.bfloat16)

    levels = tuple(range(NEAR, total))
    first_reads = (class_lanes, table, query_rows, key_rows, value_rows, out_grad)
    outs = (cells(head_count + split_levels * half), cells(split_levels * half))
    if whole_levels > 1:
        outs = outs + (cells(whole_levels - 1, head_count),)
    sent, keep, *lead = call(
        functools.partial(upper_kernel, levels, split, offset, head_size),
        [smem] + [hbm] * 6,
        outs,
        (flag_bits, *[pltpu.with_memory_space_constraint(held, pltpu.HBM) for held in first_reads]),
        flops=2 * len(levels) * row_count * width * head_size,
        scratch=[
            pltpu.VMEM(class_lanes.shape, jnp.int32),
            pltpu.VMEM(table.shape, jnp.float32),
            block,
            block,
            block,
            block,
            pltpu.VMEM((split_levels, head_count) + cell, jnp.bfloat16),
            pltpu.SemaphoreType.DMA((6,)),
        ],
        grant=FIRST_BYTES,
    )
    seen = swap(sent, inner_bits)
    two_own, two_other, zero, one = call(
        functools.partial(lower_kernel, offset, head_size),
        [smem] + [vmem] * 6 + [anywhere],
        (cells(half), cells(half), cells(head_count), cells(head_count)),
        (flag_bits, class_lanes, table, query_rows, key_rows, value_rows, out_grad, keep),
        flops=2 * NEAR * row_count * width * head_size,
        scratch=[pltpu.VMEM((head_count,) + cell, jnp.bfloat16)],
    )
    own_share, *shares_out, zero = call(
        functools.partial(share_kernel, head_count, (whole_levels, split_levels)),
        [smem] + [vmem] * 2 + [anywhere] + [vmem] * len(lead),
        (cells(share_rows),) * 4,
        (flag_bits, seen, keep, two_own, *lead),
        carry=(zero,),
    )
    big = jax.ShapeDtypeStruct((row_count, width), jnp.float32)
    query_local, key_local, value_local = call(
        functools.partial(local_kernel, block_depth, head_size),
        [vmem] * 6 + [anywhere],
        (big, big, big),
        (class_lanes, table, query_rows, key_rows, value_rows, out_grad, own_share),
        flops=10 * row_count * width * row_count,
    )

    def z_bits(offs):
        return [bit + 1 for bit in range(2) if offs >> bit & 1]

    came = [swap(shares_out[offs - 1], *z_bits(offs)) for offs in (3, 2, 1)]
    top = total - 1
    below, top_sent = call(
        functools.partial(four_sum_kernel, eighth),
        [vmem, anywhere] + [vmem] * 3,
        (cells(share_rows - eighth), cells(eighth)),
        (own_share, query_local, *came),
    )
    middle = [bit for bit in range(NEAR, top) if bit != inner_bits]
    if middle:
        part = wide(jnp.concatenate([below, top_sent], axis=0))
        parts = {
            level: part[(level - NEAR) * quarter : (level - NEAR + 1) * quarter]
            for level in range(NEAR, split)
        }
        for level in range(split, total):
            row = cut + (level - split) * eighth
            parts[level] = part[row : row + eighth]
        for bit in middle:
            going = range(bit, total)
            block_sent = narrow(jnp.concatenate([parts[level] for level in going], axis=0))
            seen_part = wide(swap(block_sent, bit))
            row = 0
            for level in going:
                size = parts[level].shape[0]
                got = seen_part[row : row + size]
                parts[level] = got if level == bit else parts[level] + got
                row += size
        below = narrow(jnp.concatenate([parts[level] for level in range(NEAR, top)], axis=0))
        top_sent = narrow(parts[top])
    two_sum = call(
        two_sum_kernel,
        [vmem] * 2 + [anywhere],
        cells(half),
        (two_own, swap(two_other, 0), query_local),
    )
    two_sum = call(
        two_sum_kernel, [vmem] * 2 + [anywhere], cells(half), (two_sum, swap(two_sum, 1), two_sum)
    )
    one_sum = call(
        two_sum_kernel, [vmem] * 2 + [anywhere], cells(head_count), (one, swap(one, 0), query_local)
    )
    one_done = swap(one_sum, 1)
    zero_done = swap(zero, 0)
    two_half = swap(two_sum, 2)
    two_rest = swap(two_half, 0)
    shares = call(
        pair_sum_kernel,
        [vmem] * 4 + [anywhere] * 3,
        cells(share_rows),
        (below, swap(below, 0), swap(top_sent, top), swap(top_sent, 0, top), two_sum, one_sum, zero_done),
    )
    pieces = [shares] + [swap(shares, *z_bits(offs)) for offs in (1, 2, 3)]
    split_own = call(
        functools.partial(gather_kernel, cut),
        [vmem] * 4 + [anywhere],
        cells(split_levels, half),
        (*pieces, two_half),
    )
    split_other = swap(split_own, inner_bits)

    small = jax.ShapeDtypeStruct((row_count, width), jnp.bfloat16)
    return call(
        functools.partial(final_kernel, offset, head_size, total, inner_bits),
        [smem] + [vmem] * 18,
        (small, small, small),
        (
            flag_bits,
            class_lanes,
            table,
            key_rows,
            value_rows,
            out_grad,
            query_local,
            key_local,
            value_local,
            zero_done,
            one_done,
            two_half,
            two_rest,
            *pieces,
            split_own,
            split_other,
        ),
        flops=(2 * total + 4) * row_count * width * head_size,
        scratch=[pltpu.VMEM((total, head_count) + cell, jnp.bfloat16)],
    )


def solution(mesh):
    rows = P(("gx", "gy"), None)
    return jax.shard_map(
        per_device,
        mesh=mesh,
        in_specs=(rows, rows, rows, rows, P(("gx", "gy")), P()),
        out_specs=(rows, rows, rows),
        check_vma=False,
    )
```

```python
import functools

import jax
import jax.numpy as jnp
from jax import lax
from jax.experimental import pallas as pl
from jax.experimental.pallas import tpu as pltpu
from jax.sharding import PartitionSpec as P

NEAR = 3
VMEM_BYTES = 16 * 1024 * 1024
FIRST_BYTES = 16 * 1024 * 1024


def level_bits(amount):
    return amount.bit_length() - 1


def wide(values):
    return values.astype(jnp.float32)


def narrow(values):
    return values.astype(jnp.bfloat16)


def product(left, right, left_dim, right_dim):
    return lax.dot_general(
        left,
        right,
        (((left_dim,), (right_dim,)), ((), ())),
        preferred_element_type=jnp.float32,
    )


def gate_lanes(class_ref, table_ref, first, last):
    classes = table_ref.shape[2]
    tokens = class_ref.shape[1]
    rows = (last - first) * table_ref.shape[1]
    numbers = lax.broadcasted_iota(jnp.int32, (classes, tokens), 0)
    picker = (numbers == class_ref[...]).astype(jnp.float32)
    table = table_ref[first:last].reshape(rows, classes)
    return jnp.dot(
        table, picker, precision=lax.Precision.HIGHEST, preferred_element_type=jnp.float32
    )


def payload_cell(flags, gates, rows, level_places, q_ref, k_ref, v_ref, g_ref, columns, store):
    query_turned = wide(q_ref[:, columns].T)
    key_turned = wide(k_ref[:, columns].T)
    grad_here = wide(g_ref[:, columns])
    value_here = wide(v_ref[:, columns])
    for place in level_places:
        row = rows[place]
        flag = flags[place] == 1
        left = jnp.where(flag, gates[row : row + 1, :] * query_turned, key_turned)
        right = jnp.where(flag, grad_here, value_here)
        store(place, narrow(product(narrow(left), narrow(right), 1, 0)))


def upper_kernel(
    levels,
    split,
    offset,
    head_size,
    flag_ref,
    class_hbm,
    table_hbm,
    q_hbm,
    k_hbm,
    v_hbm,
    g_hbm,
    sent_ref,
    keep_ref,
    *rest,
):
    lead_refs = rest[:-8]
    class_ref, table_ref, q_ref, k_ref, v_ref, g_ref, late_ref, arrived = rest[-8:]
    moves = [
        pltpu.make_async_copy(source, target, arrived.at[place])
        for place, (source, target) in enumerate(
            (
                (class_hbm, class_ref),
                (table_hbm, table_ref),
                (q_hbm, q_ref),
                (k_hbm, k_ref),
                (g_hbm, g_ref),
                (v_hbm, v_ref),
            )
        )
    ]
    for move in moves:
        move.start()
    moves[0].wait()
    moves[1].wait()
    head_count = table_ref.shape[1]
    half = head_count // 2
    core = flag_ref[split - 1]
    gates = gate_lanes(class_ref, table_ref, offset + levels[0], offset + levels[-1] + 1)
    for move in moves[2:]:
        move.wait()
    flags = [flag_ref[level] for level in levels]
    for head in range(head_count):
        rows = [place * head_count + head for place in range(len(levels))]

        def store(place, value):
            level = levels[place]
            if level < split - 1:
                lead_refs[0][level - levels[0], head] = value
            elif level == split - 1:
                sent_ref[head] = value
            else:
                late_ref[level - split, head] = value

        columns = pl.ds(head * head_size, head_size)
        payload_cell(
            flags, gates, rows, range(len(levels)), q_ref, k_ref, v_ref, g_ref, columns, store
        )
    for place in range(levels[-1] + 1 - split):
        row = place * half
        keep_ref[row : row + half] = late_ref[place, pl.ds(core * half, half)]
        sent_ref[head_count + row : head_count + row + half] = late_ref[
            place, pl.ds((1 - core) * half, half)
        ]


def share_kernel(head_count, places, flag_ref, seen_ref, keep_ref, after_ref, *refs):
    lead_refs = refs[:-4]
    out_refs = refs[-4:]
    quarter = head_count // 4
    eighth = head_count // 8
    z_place = flag_ref[1] + 2 * flag_ref[2]
    for offs in range(4):
        place = jnp.bitwise_xor(z_place, offs)
        row = 0
        for lead in range(places[0] - 1):
            out_refs[offs][row : row + quarter] = lead_refs[0][lead, pl.ds(place * quarter, quarter)]
            row += quarter
        out_refs[offs][row : row + quarter] = seen_ref[pl.ds(place * quarter, quarter)]
        row += quarter
        for late in range(places[1]):
            first = late * (head_count // 2) + place * eighth
            total = wide(keep_ref[pl.ds(first, eighth)])
            total = total + wide(seen_ref[pl.ds(head_count + first, eighth)])
            out_refs[offs][row : row + eighth] = narrow(total)
            row += eighth


def lower_kernel(
    offset,
    head_size,
    flag_ref,
    class_ref,
    table_ref,
    q_ref,
    k_ref,
    v_ref,
    g_ref,
    after_ref,
    two_own_ref,
    two_other_ref,
    zero_ref,
    one_ref,
    two_ref,
):
    head_count = table_ref.shape[1]
    half = head_count // 2
    x_place = flag_ref[0]
    gates = gate_lanes(class_ref, table_ref, offset, offset + NEAR)
    flags = [flag_ref[level] for level in range(NEAR)]
    for head in range(head_count):
        rows = [place * head_count + head for place in range(NEAR)]

        def store(place, value):
            (zero_ref, one_ref, two_ref)[place][head] = value

        columns = pl.ds(head * head_size, head_size)
        payload_cell(flags, gates, rows, range(NEAR), q_ref, k_ref, v_ref, g_ref, columns, store)
    two_own_ref[...] = two_ref[pl.ds(x_place * half, half)]
    two_other_ref[...] = two_ref[pl.ds((1 - x_place) * half, half)]


def four_sum_kernel(top_rows, own_ref, after_ref, *refs):
    came_refs = refs[:-2]
    below_ref, top_ref = refs[-2:]
    total = wide(own_ref[...])
    for came_ref in came_refs:
        total = total + wide(came_ref[...])
    rows = total.shape[0] - top_rows
    below_ref[...] = narrow(total[:rows])
    top_ref[...] = narrow(total[rows:])


def pair_sum_kernel(below_ref, far_ref, near_top_ref, far_top_ref, *refs):
    out_ref = refs[-1]
    rows = below_ref.shape[0]
    out_ref[:rows] = narrow(wide(below_ref[...]) + wide(far_ref[...]))
    out_ref[rows:] = narrow(wide(near_top_ref[...]) + wide(far_top_ref[...]))


def gather_kernel(cut, piece0_ref, piece1_ref, piece2_ref, piece3_ref, after_ref, out_ref):
    for offs, piece_ref in enumerate((piece0_ref, piece1_ref, piece2_ref, piece3_ref)):
        split_levels = out_ref.shape[0]
        eighth = out_ref.shape[1] // 4
        for level in range(split_levels):
            first = cut + level * eighth
            out_ref[level, offs * eighth : (offs + 1) * eighth] = piece_ref[first : first + eighth]


def two_sum_kernel(own_ref, seen_ref, after_ref, out_ref):
    out_ref[...] = narrow(wide(own_ref[...]) + wide(seen_ref[...]))


def local_kernel(
    block_depth,
    head_size,
    total,
    flag_ref,
    class_ref,
    table_ref,
    q_ref,
    k_ref,
    v_ref,
    g_ref,
    after_ref,
    qo_ref,
    ko_ref,
    vo_ref,
    gate_ref,
):
    head_count = table_ref.shape[1]
    tokens = q_ref.shape[0]
    offset = block_depth + 1
    gates = gate_lanes(class_ref, table_ref, 0, offset + total)
    for level in range(total):
        first = (offset + level) * head_count
        row = level * head_count
        on = wide(flag_ref[level])
        gate_ref[:, row : row + head_count] = (gates[first : first + head_count] * on).T
    source = lax.broadcasted_iota(jnp.int32, (tokens, tokens), 0)
    target = lax.broadcasted_iota(jnp.int32, (tokens, tokens), 1)
    apart = jnp.bitwise_xor(source, target)
    causal = source <= target
    for head in range(head_count):
        columns = pl.ds(head * head_size, head_size)
        query_here = q_ref[:, columns]
        key_here = k_ref[:, columns]
        value_here = v_ref[:, columns]
        grad_here = g_ref[:, columns]
        weight = jnp.broadcast_to(gates[head : head + 1, :], (tokens, tokens))
        for level in range(1, block_depth + 1):
            row = level * head_count + head
            weight = jnp.where(apart >= 2 ** (level - 1), gates[row : row + 1, :], weight)
        weight = jnp.where(causal, weight, 0.0)
        weighted_scores = narrow(weight * product(key_here, query_here, 1, 1))
        weighted_grads = narrow(weight * product(value_here, grad_here, 1, 1))
        qo_ref[:, columns] = product(weighted_grads, key_here, 0, 0)
        ko_ref[:, columns] = product(weighted_grads, query_here, 1, 0)
        vo_ref[:, columns] = product(weighted_scores, grad_here, 1, 0)


def final_kernel(
    head_count,
    head_size,
    total,
    inner,
    flag_ref,
    gate_ref,
    k_ref,
    v_ref,
    g_ref,
    ql_ref,
    kl_ref,
    vl_ref,
    zero_ref,
    one_ref,
    two_own_ref,
    two_other_ref,
    piece0_ref,
    piece1_ref,
    piece2_ref,
    piece3_ref,
    split_own_ref,
    split_other_ref,
    qo_hbm,
    ko_hbm,
    vo_hbm,
    held_ref,
    qo_ref,
    ko_ref,
    vo_ref,
    sent,
):
    half = head_count // 2
    quarter = head_count // 4
    eighth = head_count // 8
    x_place = flag_ref[0]
    z_place = flag_ref[1] + 2 * flag_ref[2]
    core = flag_ref[inner]
    held_ref[0] = zero_ref[...]
    held_ref[1] = one_ref[...]
    held_ref[2, pl.ds(x_place * half, half)] = two_own_ref[...]
    held_ref[2, pl.ds((1 - x_place) * half, half)] = two_other_ref[...]
    pieces = (piece0_ref, piece1_ref, piece2_ref, piece3_ref)
    split = inner + 1
    for level in range(NEAR, split):
        for offs in range(4):
            first = jnp.bitwise_xor(z_place, offs) * quarter
            row = (level - NEAR) * quarter
            held_ref[level, pl.ds(first, quarter)] = pieces[offs][row : row + quarter]
    for level in range(split, total):
        for offs in range(4):
            first = jnp.bitwise_xor(z_place, offs) * eighth
            rows = pl.ds(offs * eighth, eighth)
            held_ref[level, pl.ds(core * half + first, eighth)] = split_own_ref[level - split, rows]
            held_ref[level, pl.ds((1 - core) * half + first, eighth)] = split_other_ref[
                level - split, rows
            ]
    moves = []
    for head in range(head_count):
        columns = pl.ds(head * head_size, head_size)
        grad_here = g_ref[:, columns]
        query_total = ql_ref[:, columns]
        state_grad = jnp.zeros((head_size, head_size), jnp.float32)
        for level in range(total):
            state = held_ref[level, head]
            term = product(grad_here, state, 1, 1)
            row = level * head_count + head
            query_total = query_total + gate_ref[:, row : row + 1] * term
            state_grad = state_grad + wide(state) * (1.0 - wide(flag_ref[level]))
        grad_rounded = narrow(state_grad)
        qo_ref[:, columns] = narrow(query_total)
        ko_ref[:, columns] = narrow(
            kl_ref[:, columns] + product(v_ref[:, columns], grad_rounded, 1, 1)
        )
        vo_ref[:, columns] = narrow(
            vl_ref[:, columns] + product(k_ref[:, columns], grad_rounded, 1, 0)
        )
        for place, (source, target) in enumerate(
            ((qo_ref, qo_hbm), (ko_ref, ko_hbm), (vo_ref, vo_hbm))
        ):
            move = pltpu.make_async_copy(
                source.at[:, columns], target.at[:, columns], sent.at[place, head]
            )
            move.start()
            moves.append(move)
    for move in moves:
        move.wait()


def per_device(query_rows, key_rows, value_rows, out_grad, gate_class, gate_table):
    row_count, width = query_rows.shape
    head_count = gate_table.shape[2]
    head_size = width // head_count
    inner_bits = level_bits(lax.axis_size("gy"))
    outer_bits = level_bits(lax.axis_size("gx"))
    total = inner_bits + outer_bits
    block_depth = level_bits(row_count)
    offset = block_depth + 1
    inner_index = lax.axis_index("gy")
    outer_index = lax.axis_index("gx")
    block_index = (outer_index << inner_bits) | inner_index
    flag_bits = (block_index >> jnp.arange(total, dtype=jnp.int32)) & 1
    inner_size = lax.axis_size("gy")
    device_count = inner_size * lax.axis_size("gx")

    def swap(block, *bits):
        mask = sum(1 << bit for bit in bits)
        if mask < inner_size:
            return lax.ppermute(block, "gy", [(i, i ^ mask) for i in range(inner_size)])
        if mask % inner_size == 0:
            mask = mask // inner_size
            size = lax.axis_size("gx")
            return lax.ppermute(block, "gx", [(i, i ^ mask) for i in range(size)])
        return lax.ppermute(block, ("gx", "gy"), [(i, i ^ mask) for i in range(device_count)])

    class_lanes = gate_class.reshape(1, row_count)
    table = jnp.transpose(gate_table, (1, 2, 0))
    smem = pl.BlockSpec(memory_space=pltpu.SMEM)
    vmem = pl.BlockSpec(memory_space=pltpu.VMEM)
    hbm = pl.BlockSpec(memory_space=pltpu.HBM)
    anywhere = pl.BlockSpec(memory_space=pl.ANY)
    cell = (head_size, head_size)

    def cells(*lead):
        return jax.ShapeDtypeStruct(lead + cell, jnp.bfloat16)

    def call(kernel, in_specs, outs, operands, flops=0, scratch=(), grant=VMEM_BYTES, carry=(), out_space=vmem):
        moved = sum(operand.size * operand.dtype.itemsize for operand in operands)
        outs = tuple(outs) if isinstance(outs, (tuple, list)) else (outs,)
        count, taken = len(outs), len(operands)
        if carry:
            inner = kernel
            held = len(carry)

            def kernel(*refs):
                inner(*refs[:taken], *refs[taken + held : taken + held + count], *refs[taken + 2 * held + count :])

        results = pl.pallas_call(
            kernel,
            out_shape=outs + tuple(jax.ShapeDtypeStruct(item.shape, item.dtype) for item in carry),
            in_specs=in_specs + [anywhere] * len(carry),
            out_specs=(out_space,) * count + (anywhere,) * len(carry),
            input_output_aliases={taken + place: count + place for place in range(len(carry))},
            scratch_shapes=scratch,
            compiler_params=pltpu.CompilerParams(vmem_limit_bytes=grant),
            cost_estimate=pl.CostEstimate(flops=flops, bytes_accessed=moved, transcendentals=0),
        )(*operands, *carry)
        return results if len(results) > 1 else results[0]

    quarter = head_count // 4
    half = head_count // 2
    eighth = head_count // 8
    split = inner_bits + 1
    whole_levels = split - NEAR
    split_levels = total - split
    cut = whole_levels * quarter
    share_rows = cut + split_levels * eighth
    block = pltpu.VMEM((row_count, width), jnp.bfloat16)

    levels = tuple(range(NEAR, total))
    first_reads = (class_lanes, table, query_rows, key_rows, value_rows, out_grad)
    outs = (cells(head_count + split_levels * half), cells(split_levels * half))
    if whole_levels > 1:
        outs = outs + (cells(whole_levels - 1, head_count),)
    sent, keep, *lead = call(
        functools.partial(upper_kernel, levels, split, offset, head_size),
        [smem] + [hbm] * 6,
        outs,
        (flag_bits, *[pltpu.with_memory_space_constraint(held, pltpu.HBM) for held in first_reads]),
        flops=2 * len(levels) * row_count * width * head_size,
        scratch=[
            pltpu.VMEM(class_lanes.shape, jnp.int32),
            pltpu.VMEM(table.shape, jnp.float32),
            block,
            block,
            block,
            block,
            pltpu.VMEM((split_levels, head_count) + cell, jnp.bfloat16),
            pltpu.SemaphoreType.DMA((6,)),
        ],
        grant=FIRST_BYTES,
    )
    seen = swap(sent, inner_bits)
    two_own, two_other, zero, one = call(
        functools.partial(lower_kernel, offset, head_size),
        [smem] + [vmem] * 6 + [anywhere],
        (cells(half), cells(half), cells(head_count), cells(head_count)),
        (flag_bits, class_lanes, table, query_rows, key_rows, value_rows, out_grad, keep),
        flops=2 * NEAR * row_count * width * head_size,
        scratch=[pltpu.VMEM((head_count,) + cell, jnp.bfloat16)],
    )
    own_share, *shares_out, zero = call(
        functools.partial(share_kernel, head_count, (whole_levels, split_levels)),
        [smem] + [vmem] * 2 + [anywhere] + [vmem] * len(lead),
        (cells(share_rows),) * 4,
        (flag_bits, seen, keep, two_own, *lead),
        carry=(zero,),
    )
    big = jax.ShapeDtypeStruct((row_count, width), jnp.float32)
    gate_shape = jax.ShapeDtypeStruct((row_count, total * head_count), jnp.float32)
    query_local, key_local, value_local, gate_columns = call(
        functools.partial(local_kernel, block_depth, head_size, total),
        [smem] + [vmem] * 6 + [anywhere],
        (big, big, big, gate_shape),
        (flag_bits, class_lanes, table, query_rows, key_rows, value_rows, out_grad, own_share),
        flops=10 * row_count * width * row_count,
    )

    def z_bits(offs):
        return [bit + 1 for bit in range(2) if offs >> bit & 1]

    came = [swap(shares_out[offs - 1], *z_bits(offs)) for offs in (3, 2, 1)]
    top = total - 1
    below, top_sent = call(
        functools.partial(four_sum_kernel, eighth),
        [vmem, anywhere] + [vmem] * 3,
        (cells(share_rows - eighth), cells(eighth)),
        (own_share, query_local, *came),
    )
    middle = [bit for bit in range(NEAR, top) if bit != inner_bits]
    if middle:
        part = wide(jnp.concatenate([below, top_sent], axis=0))
        parts = {
            level: part[(level - NEAR) * quarter : (level - NEAR + 1) * quarter]
            for level in range(NEAR, split)
        }
        for level in range(split, total):
            row = cut + (level - split) * eighth
            parts[level] = part[row : row + eighth]
        for bit in middle:
            going = range(bit, total)
            block_sent = narrow(jnp.concatenate([parts[level] for level in going], axis=0))
            seen_part = wide(swap(block_sent, bit))
            row = 0
            for level in going:
                size = parts[level].shape[0]
                got = seen_part[row : row + size]
                parts[level] = got if level == bit else parts[level] + got
                row += size
        below = narrow(jnp.concatenate([parts[level] for level in range(NEAR, top)], axis=0))
        top_sent = narrow(parts[top])
    two_sum = call(
        two_sum_kernel,
        [vmem] * 2 + [anywhere],
        cells(half),
        (two_own, swap(two_other, 0), query_local),
    )
    two_sum = call(
        two_sum_kernel, [vmem] * 2 + [anywhere], cells(half), (two_sum, swap(two_sum, 1), two_sum)
    )
    one_sum = call(
        two_sum_kernel, [vmem] * 2 + [anywhere], cells(head_count), (one, swap(one, 0), query_local)
    )
    one_done = swap(one_sum, 1)
    zero_done = swap(zero, 0)
    two_half = swap(two_sum, 2)
    two_rest = swap(two_half, 0)
    shares = call(
        pair_sum_kernel,
        [vmem] * 4 + [anywhere] * 3,
        cells(share_rows),
        (below, swap(below, 0), swap(top_sent, top), swap(top_sent, 0, top), two_sum, one_sum, zero_done),
    )
    pieces = [shares] + [swap(shares, *z_bits(offs)) for offs in (1, 2, 3)]
    split_own = call(
        functools.partial(gather_kernel, cut),
        [vmem] * 4 + [anywhere],
        cells(split_levels, half),
        (*pieces, two_half),
    )
    split_other = swap(split_own, inner_bits)

    small = jax.ShapeDtypeStruct((row_count, width), jnp.bfloat16)
    return call(
        functools.partial(final_kernel, head_count, head_size, total, inner_bits),
        [smem] + [vmem] * 17,
        (small, small, small),
        (
            flag_bits,
            gate_columns,
            key_rows,
            value_rows,
            out_grad,
            query_local,
            key_local,
            value_local,
            zero_done,
            one_done,
            two_half,
            two_rest,
            *pieces,
            split_own,
            split_other,
        ),
        flops=(2 * total + 4) * row_count * width * head_size,
        scratch=[
            pltpu.VMEM((total, head_count) + cell, jnp.bfloat16),
            block,
            block,
            block,
            pltpu.SemaphoreType.DMA((3, head_count)),
        ],
        out_space=hbm,
    )


def solution(mesh):
    rows = P(("gx", "gy"), None)
    return jax.shard_map(
        per_device,
        mesh=mesh,
        in_specs=(rows, rows, rows, rows, P(("gx", "gy")), P()),
        out_specs=(rows, rows, rows),
        check_vma=False,
    )
```

```python
import functools

import jax
import jax.numpy as jnp
from jax import lax
from jax.experimental import pallas as pl
from jax.experimental.pallas import tpu as pltpu
from jax.sharding import PartitionSpec as P

NEAR = 3
VMEM_BYTES = 16 * 1024 * 1024
FIRST_BYTES = 16 * 1024 * 1024


def level_bits(amount):
    return amount.bit_length() - 1


def wide(values):
    return values.astype(jnp.float32)


def narrow(values):
    return values.astype(jnp.bfloat16)


def product(left, right, left_dim, right_dim):
    return lax.dot_general(
        left,
        right,
        (((left_dim,), (right_dim,)), ((), ())),
        preferred_element_type=jnp.float32,
    )


def gate_lanes(class_ref, table_ref, first, last):
    classes = table_ref.shape[2]
    tokens = class_ref.shape[1]
    rows = (last - first) * table_ref.shape[1]
    numbers = lax.broadcasted_iota(jnp.int32, (classes, tokens), 0)
    picker = (numbers == class_ref[...]).astype(jnp.float32)
    table = table_ref[first:last].reshape(rows, classes)
    return jnp.dot(
        table, picker, precision=lax.Precision.HIGHEST, preferred_element_type=jnp.float32
    )


def payload_cell(flags, gates, rows, level_places, q_ref, k_ref, v_ref, g_ref, columns, store):
    query_turned = wide(q_ref[:, columns].T)
    key_turned = wide(k_ref[:, columns].T)
    grad_here = wide(g_ref[:, columns])
    value_here = wide(v_ref[:, columns])
    for place in level_places:
        row = rows[place]
        flag = flags[place] == 1
        left = jnp.where(flag, gates[row : row + 1, :] * query_turned, key_turned)
        right = jnp.where(flag, grad_here, value_here)
        store(place, narrow(product(narrow(left), narrow(right), 1, 0)))


def upper_kernel(
    levels,
    split,
    offset,
    head_size,
    flag_ref,
    class_hbm,
    table_hbm,
    q_hbm,
    k_hbm,
    v_hbm,
    g_hbm,
    sent_ref,
    keep_ref,
    *rest,
):
    lead_refs = rest[:-8]
    class_ref, table_ref, q_ref, k_ref, v_ref, g_ref, late_ref, arrived = rest[-8:]
    moves = [
        pltpu.make_async_copy(source, target, arrived.at[place])
        for place, (source, target) in enumerate(
            (
                (class_hbm, class_ref),
                (table_hbm, table_ref),
                (q_hbm, q_ref),
                (k_hbm, k_ref),
                (g_hbm, g_ref),
                (v_hbm, v_ref),
            )
        )
    ]
    for move in moves:
        move.start()
    moves[0].wait()
    moves[1].wait()
    head_count = table_ref.shape[1]
    half = head_count // 2
    core = flag_ref[split - 1]
    gates = gate_lanes(class_ref, table_ref, offset + levels[0], offset + levels[-1] + 1)
    for move in moves[2:]:
        move.wait()
    flags = [flag_ref[level] for level in levels]
    for head in range(head_count):
        rows = [place * head_count + head for place in range(len(levels))]

        def store(place, value):
            level = levels[place]
            if level < split - 1:
                lead_refs[0][level - levels[0], head] = value
            elif level == split - 1:
                sent_ref[head] = value
            else:
                late_ref[level - split, head] = value

        columns = pl.ds(head * head_size, head_size)
        payload_cell(
            flags, gates, rows, range(len(levels)), q_ref, k_ref, v_ref, g_ref, columns, store
        )
    for place in range(levels[-1] + 1 - split):
        row = place * half
        keep_ref[row : row + half] = late_ref[place, pl.ds(core * half, half)]
        sent_ref[head_count + row : head_count + row + half] = late_ref[
            place, pl.ds((1 - core) * half, half)
        ]


def share_kernel(head_count, places, flag_ref, seen_ref, keep_ref, after_ref, *refs):
    lead_refs = refs[:-4]
    out_refs = refs[-4:]
    quarter = head_count // 4
    eighth = head_count // 8
    z_place = flag_ref[1] + 2 * flag_ref[2]
    for offs in range(4):
        place = jnp.bitwise_xor(z_place, offs)
        row = 0
        for lead in range(places[0] - 1):
            out_refs[offs][row : row + quarter] = lead_refs[0][lead, pl.ds(place * quarter, quarter)]
            row += quarter
        out_refs[offs][row : row + quarter] = seen_ref[pl.ds(place * quarter, quarter)]
        row += quarter
        for late in range(places[1]):
            first = late * (head_count // 2) + place * eighth
            total = wide(keep_ref[pl.ds(first, eighth)])
            total = total + wide(seen_ref[pl.ds(head_count + first, eighth)])
            out_refs[offs][row : row + eighth] = narrow(total)
            row += eighth


def lower_kernel(
    offset,
    head_size,
    flag_ref,
    class_ref,
    table_ref,
    q_ref,
    k_ref,
    v_ref,
    g_ref,
    after_ref,
    two_own_ref,
    two_other_ref,
    zero_ref,
    one_ref,
    two_ref,
):
    head_count = table_ref.shape[1]
    half = head_count // 2
    x_place = flag_ref[0]
    gates = gate_lanes(class_ref, table_ref, offset, offset + NEAR)
    flags = [flag_ref[level] for level in range(NEAR)]
    for head in range(head_count):
        rows = [place * head_count + head for place in range(NEAR)]

        def store(place, value):
            (zero_ref, one_ref, two_ref)[place][head] = value

        columns = pl.ds(head * head_size, head_size)
        payload_cell(flags, gates, rows, range(NEAR), q_ref, k_ref, v_ref, g_ref, columns, store)
    two_own_ref[...] = two_ref[pl.ds(x_place * half, half)]
    two_other_ref[...] = two_ref[pl.ds((1 - x_place) * half, half)]


def four_sum_kernel(top_rows, own_ref, after_ref, *refs):
    came_refs = refs[:-2]
    below_ref, top_ref = refs[-2:]
    total = wide(own_ref[...])
    for came_ref in came_refs:
        total = total + wide(came_ref[...])
    rows = total.shape[0] - top_rows
    below_ref[...] = narrow(total[:rows])
    top_ref[...] = narrow(total[rows:])


def pair_sum_kernel(below_ref, far_ref, near_top_ref, far_top_ref, *refs):
    out_ref = refs[-1]
    rows = below_ref.shape[0]
    out_ref[:rows] = narrow(wide(below_ref[...]) + wide(far_ref[...]))
    out_ref[rows:] = narrow(wide(near_top_ref[...]) + wide(far_top_ref[...]))


def gather_kernel(cut, piece0_ref, piece1_ref, piece2_ref, piece3_ref, after_ref, out_ref):
    for offs, piece_ref in enumerate((piece0_ref, piece1_ref, piece2_ref, piece3_ref)):
        split_levels = out_ref.shape[0]
        eighth = out_ref.shape[1] // 4
        for level in range(split_levels):
            first = cut + level * eighth
            out_ref[level, offs * eighth : (offs + 1) * eighth] = piece_ref[first : first + eighth]


def tick_kernel(after_ref, out_ref):
    out_ref[...] = jnp.zeros_like(out_ref)


def two_sum_kernel(own_ref, seen_ref, after_ref, out_ref):
    out_ref[...] = narrow(wide(own_ref[...]) + wide(seen_ref[...]))


def local_kernel(
    block_depth,
    head_size,
    class_ref,
    table_ref,
    q_ref,
    k_ref,
    v_ref,
    g_ref,
    after_ref,
    qo_ref,
    ko_ref,
    vo_ref,
):
    head_count = table_ref.shape[1]
    tokens = q_ref.shape[0]
    gates = gate_lanes(class_ref, table_ref, 0, block_depth + 1)
    source = lax.broadcasted_iota(jnp.int32, (tokens, tokens), 0)
    target = lax.broadcasted_iota(jnp.int32, (tokens, tokens), 1)
    apart = jnp.bitwise_xor(source, target)
    causal = source <= target
    for head in range(head_count):
        columns = pl.ds(head * head_size, head_size)
        query_here = q_ref[:, columns]
        key_here = k_ref[:, columns]
        value_here = v_ref[:, columns]
        grad_here = g_ref[:, columns]
        weight = jnp.broadcast_to(gates[head : head + 1, :], (tokens, tokens))
        for level in range(1, block_depth + 1):
            row = level * head_count + head
            weight = jnp.where(apart >= 2 ** (level - 1), gates[row : row + 1, :], weight)
        weight = jnp.where(causal, weight, 0.0)
        weighted_scores = narrow(weight * product(key_here, query_here, 1, 1))
        weighted_grads = narrow(weight * product(value_here, grad_here, 1, 1))
        qo_ref[:, columns] = product(weighted_grads, key_here, 0, 0)
        ko_ref[:, columns] = product(weighted_grads, query_here, 1, 0)
        vo_ref[:, columns] = product(weighted_scores, grad_here, 1, 0)


def gate_columns(class_ref, table_ref, first, last):
    return gate_lanes(class_ref, table_ref, first, last).T


def final_kernel(
    offset,
    head_size,
    total,
    inner,
    flag_ref,
    class_ref,
    table_ref,
    k_ref,
    v_ref,
    g_ref,
    ql_ref,
    kl_ref,
    vl_ref,
    zero_ref,
    one_ref,
    two_own_ref,
    two_other_ref,
    piece0_ref,
    piece1_ref,
    piece2_ref,
    piece3_ref,
    split_own_ref,
    split_other_ref,
    qo_ref,
    ko_ref,
    vo_ref,
    held_ref,
):
    head_count = table_ref.shape[1]
    half = head_count // 2
    quarter = head_count // 4
    eighth = head_count // 8
    gates = gate_columns(class_ref, table_ref, offset, offset + total)
    x_place = flag_ref[0]
    z_place = flag_ref[1] + 2 * flag_ref[2]
    core = flag_ref[inner]
    held_ref[0] = zero_ref[...]
    held_ref[1] = one_ref[...]
    held_ref[2, pl.ds(x_place * half, half)] = two_own_ref[...]
    held_ref[2, pl.ds((1 - x_place) * half, half)] = two_other_ref[...]
    pieces = (piece0_ref, piece1_ref, piece2_ref, piece3_ref)
    split = inner + 1
    for level in range(NEAR, split):
        for offs in range(4):
            first = jnp.bitwise_xor(z_place, offs) * quarter
            row = (level - NEAR) * quarter
            held_ref[level, pl.ds(first, quarter)] = pieces[offs][row : row + quarter]
    for level in range(split, total):
        for offs in range(4):
            first = jnp.bitwise_xor(z_place, offs) * eighth
            rows = pl.ds(offs * eighth, eighth)
            held_ref[level, pl.ds(core * half + first, eighth)] = split_own_ref[level - split, rows]
            held_ref[level, pl.ds((1 - core) * half + first, eighth)] = split_other_ref[
                level - split, rows
            ]
    for head in range(head_count):
        columns = pl.ds(head * head_size, head_size)
        grad_here = g_ref[:, columns]
        query_total = ql_ref[:, columns]
        state_grad = jnp.zeros((head_size, head_size), jnp.float32)
        for level in range(total):
            state = held_ref[level, head]
            term = product(grad_here, state, 1, 1)
            row = level * head_count + head
            on = wide(flag_ref[level])
            query_total = query_total + (gates[:, row : row + 1] * on) * term
            state_grad = state_grad + wide(state) * (1.0 - on)
        grad_rounded = narrow(state_grad)
        qo_ref[:, columns] = narrow(query_total)
        ko_ref[:, columns] = narrow(
            kl_ref[:, columns] + product(v_ref[:, columns], grad_rounded, 1, 1)
        )
        vo_ref[:, columns] = narrow(
            vl_ref[:, columns] + product(k_ref[:, columns], grad_rounded, 1, 0)
        )


def per_device(query_rows, key_rows, value_rows, out_grad, gate_class, gate_table):
    row_count, width = query_rows.shape
    head_count = gate_table.shape[2]
    head_size = width // head_count
    inner_bits = level_bits(lax.axis_size("gy"))
    outer_bits = level_bits(lax.axis_size("gx"))
    total = inner_bits + outer_bits
    block_depth = level_bits(row_count)
    offset = block_depth + 1
    inner_index = lax.axis_index("gy")
    outer_index = lax.axis_index("gx")
    block_index = (outer_index << inner_bits) | inner_index
    flag_bits = (block_index >> jnp.arange(total, dtype=jnp.int32)) & 1
    inner_size = lax.axis_size("gy")
    device_count = inner_size * lax.axis_size("gx")

    def swap(block, *bits):
        mask = sum(1 << bit for bit in bits)
        if mask < inner_size:
            return lax.ppermute(block, "gy", [(i, i ^ mask) for i in range(inner_size)])
        if mask % inner_size == 0:
            mask = mask // inner_size
            size = lax.axis_size("gx")
            return lax.ppermute(block, "gx", [(i, i ^ mask) for i in range(size)])
        return lax.ppermute(block, ("gx", "gy"), [(i, i ^ mask) for i in range(device_count)])

    class_lanes = gate_class.reshape(1, row_count)
    table = jnp.transpose(gate_table, (1, 2, 0))
    smem = pl.BlockSpec(memory_space=pltpu.SMEM)
    vmem = pl.BlockSpec(memory_space=pltpu.VMEM)
    hbm = pl.BlockSpec(memory_space=pltpu.HBM)
    anywhere = pl.BlockSpec(memory_space=pl.ANY)
    cell = (head_size, head_size)

    def cells(*lead):
        return jax.ShapeDtypeStruct(lead + cell, jnp.bfloat16)

    def call(kernel, in_specs, outs, operands, flops=0, scratch=(), grant=VMEM_BYTES, carry=()):
        moved = sum(operand.size * operand.dtype.itemsize for operand in operands)
        outs = tuple(outs) if isinstance(outs, (tuple, list)) else (outs,)
        count, taken = len(outs), len(operands)
        if carry:
            inner = kernel
            held = len(carry)

            def kernel(*refs):
                inner(*refs[:taken], *refs[taken + held : taken + held + count], *refs[taken + 2 * held + count :])

        results = pl.pallas_call(
            kernel,
            out_shape=outs + tuple(jax.ShapeDtypeStruct(item.shape, item.dtype) for item in carry),
            in_specs=in_specs + [anywhere] * len(carry),
            out_specs=(vmem,) * count + (anywhere,) * len(carry),
            input_output_aliases={taken + place: count + place for place in range(len(carry))},
            scratch_shapes=scratch,
            compiler_params=pltpu.CompilerParams(vmem_limit_bytes=grant),
            cost_estimate=pl.CostEstimate(flops=flops, bytes_accessed=moved, transcendentals=0),
        )(*operands, *carry)
        return results if len(results) > 1 else results[0]

    quarter = head_count // 4
    half = head_count // 2
    eighth = head_count // 8
    split = inner_bits + 1
    whole_levels = split - NEAR
    split_levels = total - split
    cut = whole_levels * quarter
    share_rows = cut + split_levels * eighth
    block = pltpu.VMEM((row_count, width), jnp.bfloat16)

    levels = tuple(range(NEAR, total))
    first_reads = (class_lanes, table, query_rows, key_rows, value_rows, out_grad)
    outs = (cells(head_count + split_levels * half), cells(split_levels * half))
    if whole_levels > 1:
        outs = outs + (cells(whole_levels - 1, head_count),)
    sent, keep, *lead = call(
        functools.partial(upper_kernel, levels, split, offset, head_size),
        [smem] + [hbm] * 6,
        outs,
        (flag_bits, *[pltpu.with_memory_space_constraint(held, pltpu.HBM) for held in first_reads]),
        flops=2 * len(levels) * row_count * width * head_size,
        scratch=[
            pltpu.VMEM(class_lanes.shape, jnp.int32),
            pltpu.VMEM(table.shape, jnp.float32),
            block,
            block,
            block,
            block,
            pltpu.VMEM((split_levels, head_count) + cell, jnp.bfloat16),
            pltpu.SemaphoreType.DMA((6,)),
        ],
        grant=FIRST_BYTES,
    )
    seen = swap(sent, inner_bits)
    two_own, two_other, zero, one = call(
        functools.partial(lower_kernel, offset, head_size),
        [smem] + [vmem] * 6 + [anywhere],
        (cells(half), cells(half), cells(head_count), cells(head_count)),
        (flag_bits, class_lanes, table, query_rows, key_rows, value_rows, out_grad, keep),
        flops=2 * NEAR * row_count * width * head_size,
        scratch=[pltpu.VMEM((head_count,) + cell, jnp.bfloat16)],
    )
    own_share, *shares_out, zero = call(
        functools.partial(share_kernel, head_count, (whole_levels, split_levels)),
        [smem] + [vmem] * 2 + [anywhere] + [vmem] * len(lead),
        (cells(share_rows),) * 4,
        (flag_bits, seen, keep, two_own, *lead),
        carry=(zero,),
    )
    two_sum = call(
        two_sum_kernel,
        [vmem] * 2 + [anywhere],
        cells(half),
        (two_own, swap(two_other, 0), own_share),
    )
    big = jax.ShapeDtypeStruct((row_count, width), jnp.float32)
    query_local, key_local, value_local = call(
        functools.partial(local_kernel, block_depth, head_size),
        [vmem] * 6 + [anywhere],
        (big, big, big),
        (class_lanes, table, query_rows, key_rows, value_rows, out_grad, two_sum),
        flops=10 * row_count * width * row_count,
    )

    def z_bits(offs):
        return [bit + 1 for bit in range(2) if offs >> bit & 1]

    came = [swap(shares_out[offs - 1], *z_bits(offs)) for offs in (3, 2, 1)]
    top = total - 1
    below, top_sent = call(
        functools.partial(four_sum_kernel, eighth),
        [vmem, anywhere] + [vmem] * 3,
        (cells(share_rows - eighth), cells(eighth)),
        (own_share, query_local, *came),
    )
    middle = [bit for bit in range(NEAR, top) if bit != inner_bits]
    if middle:
        part = wide(jnp.concatenate([below, top_sent], axis=0))
        parts = {
            level: part[(level - NEAR) * quarter : (level - NEAR + 1) * quarter]
            for level in range(NEAR, split)
        }
        for level in range(split, total):
            row = cut + (level - split) * eighth
            parts[level] = part[row : row + eighth]
        for bit in middle:
            going = range(bit, total)
            block_sent = narrow(jnp.concatenate([parts[level] for level in going], axis=0))
            seen_part = wide(swap(block_sent, bit))
            row = 0
            for level in going:
                size = parts[level].shape[0]
                got = seen_part[row : row + size]
                parts[level] = got if level == bit else parts[level] + got
                row += size
        below = narrow(jnp.concatenate([parts[level] for level in range(NEAR, top)], axis=0))
        top_sent = narrow(parts[top])
    two_sum = call(
        two_sum_kernel, [vmem] * 2 + [anywhere], cells(half), (two_sum, swap(two_sum, 1), two_sum)
    )
    one_sum = call(
        two_sum_kernel, [vmem] * 2 + [anywhere], cells(head_count), (one, swap(one, 0), query_local)
    )
    one_done = swap(one_sum, 1)
    zero_done = swap(zero, 0)
    two_half = swap(two_sum, 2)
    two_rest = swap(two_half, 0)
    shares = call(
        pair_sum_kernel,
        [vmem] * 4 + [anywhere] * 3,
        cells(share_rows),
        (below, swap(below, 0), swap(top_sent, top), swap(top_sent, 0, top), two_sum, one_sum, zero_done),
    )
    pieces = [shares] + [swap(shares, *z_bits(offs)) for offs in (1, 2, 3)]
    split_own = call(
        functools.partial(gather_kernel, cut),
        [vmem] * 4 + [anywhere],
        cells(split_levels, half),
        (*pieces, two_half),
    )
    split_other = swap(split_own, inner_bits)

    small = jax.ShapeDtypeStruct((row_count, width), jnp.bfloat16)
    return call(
        functools.partial(final_kernel, offset, head_size, total, inner_bits),
        [smem] + [vmem] * 18,
        (small, small, small),
        (
            flag_bits,
            class_lanes,
            table,
            key_rows,
            value_rows,
            out_grad,
            query_local,
            key_local,
            value_local,
            zero_done,
            one_done,
            two_half,
            two_rest,
            *pieces,
            split_own,
            split_other,
        ),
        flops=(2 * total + 4) * row_count * width * head_size,
        scratch=[pltpu.VMEM((total, head_count) + cell, jnp.bfloat16)],
    )


def solution(mesh):
    rows = P(("gx", "gy"), None)
    return jax.shard_map(
        per_device,
        mesh=mesh,
        in_specs=(rows, rows, rows, rows, P(("gx", "gy")), P()),
        out_specs=(rows, rows, rows),
        check_vma=False,
    )
```

```python
import functools

import jax
import jax.numpy as jnp
from jax import lax
from jax.experimental import pallas as pl
from jax.experimental.pallas import tpu as pltpu
from jax.sharding import PartitionSpec as P

NEAR = 3
VMEM_BYTES = 16 * 1024 * 1024
FIRST_BYTES = 16 * 1024 * 1024


def level_bits(amount):
    return amount.bit_length() - 1


def wide(values):
    return values.astype(jnp.float32)


def narrow(values):
    return values.astype(jnp.bfloat16)


def product(left, right, left_dim, right_dim):
    return lax.dot_general(
        left,
        right,
        (((left_dim,), (right_dim,)), ((), ())),
        preferred_element_type=jnp.float32,
    )


def gate_lanes(class_ref, table_ref, first, last):
    classes = table_ref.shape[2]
    tokens = class_ref.shape[1]
    rows = (last - first) * table_ref.shape[1]
    numbers = lax.broadcasted_iota(jnp.int32, (classes, tokens), 0)
    picker = (numbers == class_ref[...]).astype(jnp.float32)
    table = table_ref[first:last].reshape(rows, classes)
    return jnp.dot(
        table, picker, precision=lax.Precision.HIGHEST, preferred_element_type=jnp.float32
    )


def payload_cell(flags, gates, rows, level_places, q_ref, k_ref, v_ref, g_ref, columns, store):
    query_turned = wide(q_ref[:, columns].T)
    key_turned = wide(k_ref[:, columns].T)
    grad_here = wide(g_ref[:, columns])
    value_here = wide(v_ref[:, columns])
    for place in level_places:
        row = rows[place]
        flag = flags[place] == 1
        left = jnp.where(flag, gates[row : row + 1, :] * query_turned, key_turned)
        right = jnp.where(flag, grad_here, value_here)
        store(place, narrow(product(narrow(left), narrow(right), 1, 0)))


def upper_kernel(
    levels,
    split,
    offset,
    head_size,
    flag_ref,
    class_hbm,
    table_hbm,
    q_hbm,
    k_hbm,
    v_hbm,
    g_hbm,
    sent_ref,
    keep_ref,
    *rest,
):
    lead_refs = rest[:-8]
    class_ref, table_ref, q_ref, k_ref, v_ref, g_ref, late_ref, arrived = rest[-8:]
    moves = [
        pltpu.make_async_copy(source, target, arrived.at[place])
        for place, (source, target) in enumerate(
            (
                (class_hbm, class_ref),
                (table_hbm, table_ref),
                (q_hbm, q_ref),
                (k_hbm, k_ref),
                (g_hbm, g_ref),
                (v_hbm, v_ref),
            )
        )
    ]
    for move in moves:
        move.start()
    moves[0].wait()
    moves[1].wait()
    head_count = table_ref.shape[1]
    half = head_count // 2
    core = flag_ref[split - 1]
    gates = gate_lanes(class_ref, table_ref, offset + levels[0], offset + levels[-1] + 1)
    for move in moves[2:]:
        move.wait()
    flags = [flag_ref[level] for level in levels]
    for head in range(head_count):
        rows = [place * head_count + head for place in range(len(levels))]

        def store(place, value):
            level = levels[place]
            if level < split - 1:
                lead_refs[0][level - levels[0], head] = value
            elif level == split - 1:
                sent_ref[head] = value
            else:
                late_ref[level - split, head] = value

        columns = pl.ds(head * head_size, head_size)
        payload_cell(
            flags, gates, rows, range(len(levels)), q_ref, k_ref, v_ref, g_ref, columns, store
        )
    for place in range(levels[-1] + 1 - split):
        row = place * half
        keep_ref[row : row + half] = late_ref[place, pl.ds(core * half, half)]
        sent_ref[head_count + row : head_count + row + half] = late_ref[
            place, pl.ds((1 - core) * half, half)
        ]


def share_kernel(head_count, places, flag_ref, seen_ref, keep_ref, after_ref, *refs):
    lead_refs = refs[:-4]
    out_refs = refs[-4:]
    quarter = head_count // 4
    eighth = head_count // 8
    z_place = flag_ref[1] + 2 * flag_ref[2]
    for offs in range(4):
        place = jnp.bitwise_xor(z_place, offs)
        row = 0
        for lead in range(places[0] - 1):
            out_refs[offs][row : row + quarter] = lead_refs[0][lead, pl.ds(place * quarter, quarter)]
            row += quarter
        out_refs[offs][row : row + quarter] = seen_ref[pl.ds(place * quarter, quarter)]
        row += quarter
        for late in range(places[1]):
            first = late * (head_count // 2) + place * eighth
            total = wide(keep_ref[pl.ds(first, eighth)])
            total = total + wide(seen_ref[pl.ds(head_count + first, eighth)])
            out_refs[offs][row : row + eighth] = narrow(total)
            row += eighth


def lower_kernel(
    offset,
    head_size,
    flag_ref,
    class_ref,
    table_ref,
    q_ref,
    k_ref,
    v_ref,
    g_ref,
    after_ref,
    two_own_ref,
    sent_ref,
    zero_ref,
    two_ref,
):
    head_count = table_ref.shape[1]
    half = head_count // 2
    x_place = flag_ref[0]
    gates = gate_lanes(class_ref, table_ref, offset, offset + NEAR)
    flags = [flag_ref[level] for level in range(NEAR)]
    for head in range(head_count):
        rows = [place * head_count + head for place in range(NEAR)]

        def store(place, value):
            if place == 0:
                zero_ref[head] = value
            elif place == 1:
                sent_ref[half + head] = value
            else:
                two_ref[head] = value

        columns = pl.ds(head * head_size, head_size)
        payload_cell(flags, gates, rows, range(NEAR), q_ref, k_ref, v_ref, g_ref, columns, store)
    two_own_ref[...] = two_ref[pl.ds(x_place * half, half)]
    sent_ref[:half] = two_ref[pl.ds((1 - x_place) * half, half)]


def four_sum_kernel(top_rows, own_ref, after_ref, *refs):
    came_refs = refs[:-2]
    below_ref, top_ref = refs[-2:]
    total = wide(own_ref[...])
    for came_ref in came_refs:
        total = total + wide(came_ref[...])
    rows = total.shape[0] - top_rows
    below_ref[...] = narrow(total[:rows])
    top_ref[...] = narrow(total[rows:])


def pair_sum_kernel(below_ref, far_ref, near_top_ref, far_top_ref, *refs):
    out_ref = refs[-1]
    rows = below_ref.shape[0]
    out_ref[:rows] = narrow(wide(below_ref[...]) + wide(far_ref[...]))
    out_ref[rows:] = narrow(wide(near_top_ref[...]) + wide(far_top_ref[...]))


def gather_kernel(cut, piece0_ref, piece1_ref, piece2_ref, piece3_ref, after_ref, out_ref):
    for offs, piece_ref in enumerate((piece0_ref, piece1_ref, piece2_ref, piece3_ref)):
        split_levels = out_ref.shape[0]
        eighth = out_ref.shape[1] // 4
        for level in range(split_levels):
            first = cut + level * eighth
            out_ref[level, offs * eighth : (offs + 1) * eighth] = piece_ref[first : first + eighth]


def two_sum_kernel(own_ref, seen_ref, after_ref, two_ref):
    two_ref[...] = narrow(wide(own_ref[...]) + wide(seen_ref[: own_ref.shape[0]]))


def one_sum_kernel(sent_ref, seen_ref, after_ref, one_ref):
    first = sent_ref.shape[0] - one_ref.shape[0]
    one_ref[...] = narrow(wide(sent_ref[first:]) + wide(seen_ref[first:]))


def local_kernel(
    block_depth,
    head_size,
    class_ref,
    table_ref,
    q_ref,
    k_ref,
    v_ref,
    g_ref,
    after_ref,
    qo_ref,
    ko_ref,
    vo_ref,
):
    head_count = table_ref.shape[1]
    tokens = q_ref.shape[0]
    gates = gate_lanes(class_ref, table_ref, 0, block_depth + 1)
    source = lax.broadcasted_iota(jnp.int32, (tokens, tokens), 0)
    target = lax.broadcasted_iota(jnp.int32, (tokens, tokens), 1)
    apart = jnp.bitwise_xor(source, target)
    causal = source <= target
    for head in range(head_count):
        columns = pl.ds(head * head_size, head_size)
        query_here = q_ref[:, columns]
        key_here = k_ref[:, columns]
        value_here = v_ref[:, columns]
        grad_here = g_ref[:, columns]
        weight = jnp.broadcast_to(gates[head : head + 1, :], (tokens, tokens))
        for level in range(1, block_depth + 1):
            row = level * head_count + head
            weight = jnp.where(apart >= 2 ** (level - 1), gates[row : row + 1, :], weight)
        weight = jnp.where(causal, weight, 0.0)
        weighted_scores = narrow(weight * product(key_here, query_here, 1, 1))
        weighted_grads = narrow(weight * product(value_here, grad_here, 1, 1))
        qo_ref[:, columns] = product(weighted_grads, key_here, 0, 0)
        ko_ref[:, columns] = product(weighted_grads, query_here, 1, 0)
        vo_ref[:, columns] = product(weighted_scores, grad_here, 1, 0)


def gate_columns(class_ref, table_ref, first, last):
    return gate_lanes(class_ref, table_ref, first, last).T


def final_kernel(
    offset,
    head_size,
    total,
    inner,
    flag_ref,
    class_ref,
    table_ref,
    k_ref,
    v_ref,
    g_ref,
    ql_ref,
    kl_ref,
    vl_ref,
    zero_ref,
    one_ref,
    two_own_ref,
    two_other_ref,
    piece0_ref,
    piece1_ref,
    piece2_ref,
    piece3_ref,
    split_own_ref,
    split_other_ref,
    qo_ref,
    ko_ref,
    vo_ref,
    held_ref,
):
    head_count = table_ref.shape[1]
    half = head_count // 2
    quarter = head_count // 4
    eighth = head_count // 8
    gates = gate_columns(class_ref, table_ref, offset, offset + total)
    x_place = flag_ref[0]
    z_place = flag_ref[1] + 2 * flag_ref[2]
    core = flag_ref[inner]
    held_ref[0] = zero_ref[...]
    held_ref[1] = one_ref[...]
    held_ref[2, pl.ds(x_place * half, half)] = two_own_ref[...]
    held_ref[2, pl.ds((1 - x_place) * half, half)] = two_other_ref[...]
    pieces = (piece0_ref, piece1_ref, piece2_ref, piece3_ref)
    split = inner + 1
    for level in range(NEAR, split):
        for offs in range(4):
            first = jnp.bitwise_xor(z_place, offs) * quarter
            row = (level - NEAR) * quarter
            held_ref[level, pl.ds(first, quarter)] = pieces[offs][row : row + quarter]
    for level in range(split, total):
        for offs in range(4):
            first = jnp.bitwise_xor(z_place, offs) * eighth
            rows = pl.ds(offs * eighth, eighth)
            held_ref[level, pl.ds(core * half + first, eighth)] = split_own_ref[level - split, rows]
            held_ref[level, pl.ds((1 - core) * half + first, eighth)] = split_other_ref[
                level - split, rows
            ]
    for head in range(head_count):
        columns = pl.ds(head * head_size, head_size)
        grad_here = g_ref[:, columns]
        query_total = ql_ref[:, columns]
        state_grad = jnp.zeros((head_size, head_size), jnp.float32)
        for level in range(total):
            state = held_ref[level, head]
            term = product(grad_here, state, 1, 1)
            row = level * head_count + head
            on = wide(flag_ref[level])
            query_total = query_total + (gates[:, row : row + 1] * on) * term
            state_grad = state_grad + wide(state) * (1.0 - on)
        grad_rounded = narrow(state_grad)
        qo_ref[:, columns] = narrow(query_total)
        ko_ref[:, columns] = narrow(
            kl_ref[:, columns] + product(v_ref[:, columns], grad_rounded, 1, 1)
        )
        vo_ref[:, columns] = narrow(
            vl_ref[:, columns] + product(k_ref[:, columns], grad_rounded, 1, 0)
        )


def per_device(query_rows, key_rows, value_rows, out_grad, gate_class, gate_table):
    row_count, width = query_rows.shape
    head_count = gate_table.shape[2]
    head_size = width // head_count
    inner_bits = level_bits(lax.axis_size("gy"))
    outer_bits = level_bits(lax.axis_size("gx"))
    total = inner_bits + outer_bits
    block_depth = level_bits(row_count)
    offset = block_depth + 1
    inner_index = lax.axis_index("gy")
    outer_index = lax.axis_index("gx")
    block_index = (outer_index << inner_bits) | inner_index
    flag_bits = (block_index >> jnp.arange(total, dtype=jnp.int32)) & 1
    inner_size = lax.axis_size("gy")
    device_count = inner_size * lax.axis_size("gx")

    def swap(block, *bits):
        mask = sum(1 << bit for bit in bits)
        if mask < inner_size:
            return lax.ppermute(block, "gy", [(i, i ^ mask) for i in range(inner_size)])
        if mask % inner_size == 0:
            mask = mask // inner_size
            size = lax.axis_size("gx")
            return lax.ppermute(block, "gx", [(i, i ^ mask) for i in range(size)])
        return lax.ppermute(block, ("gx", "gy"), [(i, i ^ mask) for i in range(device_count)])

    class_lanes = gate_class.reshape(1, row_count)
    table = jnp.transpose(gate_table, (1, 2, 0))
    smem = pl.BlockSpec(memory_space=pltpu.SMEM)
    vmem = pl.BlockSpec(memory_space=pltpu.VMEM)
    hbm = pl.BlockSpec(memory_space=pltpu.HBM)
    anywhere = pl.BlockSpec(memory_space=pl.ANY)
    cell = (head_size, head_size)

    def cells(*lead):
        return jax.ShapeDtypeStruct(lead + cell, jnp.bfloat16)

    def call(kernel, in_specs, outs, operands, flops=0, scratch=(), grant=VMEM_BYTES, out_specs=None, aliases=None):
        moved = sum(operand.size * operand.dtype.itemsize for operand in operands)
        return pl.pallas_call(
            kernel,
            out_shape=outs,
            in_specs=in_specs,
            out_specs=out_specs or jax.tree.map(lambda _: vmem, outs),
            input_output_aliases=aliases or {},
            scratch_shapes=scratch,
            compiler_params=pltpu.CompilerParams(vmem_limit_bytes=grant),
            cost_estimate=pl.CostEstimate(flops=flops, bytes_accessed=moved, transcendentals=0),
        )(*operands)

    quarter = head_count // 4
    half = head_count // 2
    eighth = head_count // 8
    split = inner_bits + 1
    whole_levels = split - NEAR
    split_levels = total - split
    cut = whole_levels * quarter
    share_rows = cut + split_levels * eighth
    block = pltpu.VMEM((row_count, width), jnp.bfloat16)

    levels = tuple(range(NEAR, total))
    first_reads = (class_lanes, table, query_rows, key_rows, value_rows, out_grad)
    outs = (cells(head_count + split_levels * half), cells(split_levels * half))
    if whole_levels > 1:
        outs = outs + (cells(whole_levels - 1, head_count),)
    sent, keep, *lead = call(
        functools.partial(upper_kernel, levels, split, offset, head_size),
        [smem] + [hbm] * 6,
        outs,
        (flag_bits, *[pltpu.with_memory_space_constraint(held, pltpu.HBM) for held in first_reads]),
        flops=2 * len(levels) * row_count * width * head_size,
        scratch=[
            pltpu.VMEM(class_lanes.shape, jnp.int32),
            pltpu.VMEM(table.shape, jnp.float32),
            block,
            block,
            block,
            block,
            pltpu.VMEM((split_levels, head_count) + cell, jnp.bfloat16),
            pltpu.SemaphoreType.DMA((6,)),
        ],
        grant=FIRST_BYTES,
    )
    seen = swap(sent, inner_bits)
    two_own, lower_sent, zero = call(
        functools.partial(lower_kernel, offset, head_size),
        [smem] + [vmem] * 6 + [anywhere],
        (cells(half), cells(half + head_count), cells(head_count)),
        (flag_bits, class_lanes, table, query_rows, key_rows, value_rows, out_grad, keep),
        flops=2 * NEAR * row_count * width * head_size,
        scratch=[pltpu.VMEM((head_count,) + cell, jnp.bfloat16)],
    )
    own_share, *shares_out = call(
        functools.partial(share_kernel, head_count, (whole_levels, split_levels)),
        [smem] + [vmem] * 2 + [anywhere] + [vmem] * len(lead),
        (cells(share_rows),) * 4,
        (flag_bits, seen, keep, two_own, *lead),
    )
    lower_seen = swap(lower_sent, 0)
    two_sum = call(
        two_sum_kernel, [vmem] * 2 + [anywhere], cells(half), (two_own, lower_seen, own_share)
    )
    big = jax.ShapeDtypeStruct((row_count, width), jnp.float32)
    query_local, key_local, value_local = call(
        functools.partial(local_kernel, block_depth, head_size),
        [vmem] * 6 + [anywhere],
        (big, big, big),
        (class_lanes, table, query_rows, key_rows, value_rows, out_grad, own_share),
        flops=10 * row_count * width * row_count,
    )

    def z_bits(offs):
        return [bit + 1 for bit in range(2) if offs >> bit & 1]

    came = [swap(shares_out[offs - 1], *z_bits(offs)) for offs in (3, 2, 1)]
    top = total - 1
    below, top_sent = call(
        functools.partial(four_sum_kernel, eighth),
        [vmem, anywhere] + [vmem] * 3,
        (cells(share_rows - eighth), cells(eighth)),
        (own_share, query_local, *came),
    )
    middle = [bit for bit in range(NEAR, top) if bit != inner_bits]
    if middle:
        part = wide(jnp.concatenate([below, top_sent], axis=0))
        parts = {
            level: part[(level - NEAR) * quarter : (level - NEAR + 1) * quarter]
            for level in range(NEAR, split)
        }
        for level in range(split, total):
            row = cut + (level - split) * eighth
            parts[level] = part[row : row + eighth]
        for bit in middle:
            going = range(bit, total)
            block_sent = narrow(jnp.concatenate([parts[level] for level in going], axis=0))
            seen_part = wide(swap(block_sent, bit))
            row = 0
            for level in going:
                size = parts[level].shape[0]
                got = seen_part[row : row + size]
                parts[level] = got if level == bit else parts[level] + got
                row += size
        below = narrow(jnp.concatenate([parts[level] for level in range(NEAR, top)], axis=0))
        top_sent = narrow(parts[top])
    one_sum = call(
        one_sum_kernel,
        [vmem] * 2 + [anywhere],
        cells(head_count),
        (lower_sent, lower_seen, below),
    )
    two_sum = call(
        two_sum_kernel, [vmem] * 2 + [anywhere], cells(half), (two_sum, swap(two_sum, 1), two_sum)
    )
    two_half = swap(two_sum, 2)
    two_rest = swap(two_half, 0)
    one_done = swap(one_sum, 1)
    zero_done = swap(zero, 0)
    shares = call(
        pair_sum_kernel,
        [vmem] * 4 + [anywhere] * 2,
        cells(share_rows),
        (below, swap(below, 0), swap(top_sent, top), swap(top_sent, 0, top), two_sum, zero_done),
    )
    pieces = [shares] + [swap(shares, *z_bits(offs)) for offs in (1, 2, 3)]
    split_own = call(
        functools.partial(gather_kernel, cut),
        [vmem] * 4 + [anywhere],
        cells(split_levels, half),
        (*pieces, two_half),
    )
    split_other = swap(split_own, inner_bits)

    small = jax.ShapeDtypeStruct((row_count, width), jnp.bfloat16)
    return call(
        functools.partial(final_kernel, offset, head_size, total, inner_bits),
        [smem] + [vmem] * 18,
        (small, small, small),
        (
            flag_bits,
            class_lanes,
            table,
            key_rows,
            value_rows,
            out_grad,
            query_local,
            key_local,
            value_local,
            zero_done,
            one_done,
            two_half,
            two_rest,
            *pieces,
            split_own,
            split_other,
        ),
        flops=(2 * total + 4) * row_count * width * head_size,
        scratch=[pltpu.VMEM((total, head_count) + cell, jnp.bfloat16)],
    )


def solution(mesh):
    rows = P(("gx", "gy"), None)
    return jax.shard_map(
        per_device,
        mesh=mesh,
        in_specs=(rows, rows, rows, rows, P(("gx", "gy")), P()),
        out_specs=(rows, rows, rows),
        check_vma=False,
    )
```

```python
import functools

import jax
import jax.numpy as jnp
from jax import lax
from jax.experimental import pallas as pl
from jax.experimental.pallas import tpu as pltpu
from jax.sharding import PartitionSpec as P

NEAR = 3
VMEM_BYTES = 16 * 1024 * 1024
FIRST_BYTES = 16 * 1024 * 1024


def level_bits(amount):
    return amount.bit_length() - 1


def wide(values):
    return values.astype(jnp.float32)


def narrow(values):
    return values.astype(jnp.bfloat16)


def product(left, right, left_dim, right_dim):
    return lax.dot_general(
        left,
        right,
        (((left_dim,), (right_dim,)), ((), ())),
        preferred_element_type=jnp.float32,
    )


def gate_lanes(class_ref, table_ref, first, last):
    classes = table_ref.shape[2]
    tokens = class_ref.shape[1]
    rows = (last - first) * table_ref.shape[1]
    numbers = lax.broadcasted_iota(jnp.int32, (classes, tokens), 0)
    picker = (numbers == class_ref[...]).astype(jnp.float32)
    table = table_ref[first:last].reshape(rows, classes)
    return jnp.dot(
        table, picker, precision=lax.Precision.HIGHEST, preferred_element_type=jnp.float32
    )


def payload_cell(flags, gates, rows, level_places, q_ref, k_ref, v_ref, g_ref, columns, store):
    query_turned = wide(q_ref[:, columns].T)
    key_turned = wide(k_ref[:, columns].T)
    grad_here = wide(g_ref[:, columns])
    value_here = wide(v_ref[:, columns])
    for place in level_places:
        row = rows[place]
        flag = flags[place] == 1
        left = jnp.where(flag, gates[row : row + 1, :] * query_turned, key_turned)
        right = jnp.where(flag, grad_here, value_here)
        store(place, narrow(product(narrow(left), narrow(right), 1, 0)))


def upper_kernel(
    levels,
    split,
    offset,
    head_size,
    flag_ref,
    class_hbm,
    table_hbm,
    q_hbm,
    k_hbm,
    v_hbm,
    g_hbm,
    sent_ref,
    keep_ref,
    *rest,
):
    lead_refs = rest[:-8]
    class_ref, table_ref, q_ref, k_ref, v_ref, g_ref, late_ref, arrived = rest[-8:]
    moves = [
        pltpu.make_async_copy(source, target, arrived.at[place])
        for place, (source, target) in enumerate(
            (
                (class_hbm, class_ref),
                (table_hbm, table_ref),
                (q_hbm, q_ref),
                (k_hbm, k_ref),
                (g_hbm, g_ref),
                (v_hbm, v_ref),
            )
        )
    ]
    for move in moves:
        move.start()
    moves[0].wait()
    moves[1].wait()
    head_count = table_ref.shape[1]
    half = head_count // 2
    core = flag_ref[split - 1]
    gates = gate_lanes(class_ref, table_ref, offset + levels[0], offset + levels[-1] + 1)
    for move in moves[2:]:
        move.wait()
    flags = [flag_ref[level] for level in levels]
    for head in range(head_count):
        rows = [place * head_count + head for place in range(len(levels))]

        def store(place, value):
            level = levels[place]
            if level < split - 1:
                lead_refs[0][level - levels[0], head] = value
            elif level == split - 1:
                sent_ref[head] = value
            else:
                late_ref[level - split, head] = value

        columns = pl.ds(head * head_size, head_size)
        payload_cell(
            flags, gates, rows, range(len(levels)), q_ref, k_ref, v_ref, g_ref, columns, store
        )
    for place in range(levels[-1] + 1 - split):
        row = place * half
        keep_ref[row : row + half] = late_ref[place, pl.ds(core * half, half)]
        sent_ref[head_count + row : head_count + row + half] = late_ref[
            place, pl.ds((1 - core) * half, half)
        ]


def share_kernel(head_count, places, flag_ref, seen_ref, keep_ref, after_ref, *refs):
    lead_refs = refs[:-4]
    out_refs = refs[-4:]
    quarter = head_count // 4
    eighth = head_count // 8
    z_place = flag_ref[1] + 2 * flag_ref[2]
    for offs in range(4):
        place = jnp.bitwise_xor(z_place, offs)
        row = 0
        for lead in range(places[0] - 1):
            out_refs[offs][row : row + quarter] = lead_refs[0][lead, pl.ds(place * quarter, quarter)]
            row += quarter
        out_refs[offs][row : row + quarter] = seen_ref[pl.ds(place * quarter, quarter)]
        row += quarter
        for late in range(places[1]):
            first = late * (head_count // 2) + place * eighth
            total = wide(keep_ref[pl.ds(first, eighth)])
            total = total + wide(seen_ref[pl.ds(head_count + first, eighth)])
            out_refs[offs][row : row + eighth] = narrow(total)
            row += eighth


def lower_kernel(
    offset,
    head_size,
    flag_ref,
    class_ref,
    table_ref,
    q_ref,
    k_ref,
    v_ref,
    g_ref,
    after_ref,
    two_own_ref,
    sent_ref,
    zero_ref,
    two_ref,
):
    head_count = table_ref.shape[1]
    half = head_count // 2
    x_place = flag_ref[0]
    gates = gate_lanes(class_ref, table_ref, offset, offset + NEAR)
    flags = [flag_ref[level] for level in range(NEAR)]
    for head in range(head_count):
        rows = [place * head_count + head for place in range(NEAR)]

        def store(place, value):
            if place == 0:
                zero_ref[head] = value
            elif place == 1:
                sent_ref[half + head] = value
            else:
                two_ref[head] = value

        columns = pl.ds(head * head_size, head_size)
        payload_cell(flags, gates, rows, range(NEAR), q_ref, k_ref, v_ref, g_ref, columns, store)
    two_own_ref[...] = two_ref[pl.ds(x_place * half, half)]
    sent_ref[:half] = two_ref[pl.ds((1 - x_place) * half, half)]


def four_sum_kernel(top_rows, own_ref, after_ref, *refs):
    came_refs = refs[:-2]
    below_ref, top_ref = refs[-2:]
    total = wide(own_ref[...])
    for came_ref in came_refs:
        total = total + wide(came_ref[...])
    rows = total.shape[0] - top_rows
    below_ref[...] = narrow(total[:rows])
    top_ref[...] = narrow(total[rows:])


def pair_sum_kernel(below_ref, far_ref, near_top_ref, far_top_ref, *refs):
    out_ref = refs[-1]
    rows = below_ref.shape[0]
    out_ref[:rows] = narrow(wide(below_ref[...]) + wide(far_ref[...]))
    out_ref[rows:] = narrow(wide(near_top_ref[...]) + wide(far_top_ref[...]))


def gather_kernel(cut, piece0_ref, piece1_ref, piece2_ref, piece3_ref, after_ref, local_ref, out_ref):
    for offs, piece_ref in enumerate((piece0_ref, piece1_ref, piece2_ref, piece3_ref)):
        split_levels = out_ref.shape[0]
        eighth = out_ref.shape[1] // 4
        for level in range(split_levels):
            first = cut + level * eighth
            out_ref[level, offs * eighth : (offs + 1) * eighth] = piece_ref[first : first + eighth]


def two_sum_kernel(own_ref, seen_ref, after_ref, two_ref):
    two_ref[...] = narrow(wide(own_ref[...]) + wide(seen_ref[: own_ref.shape[0]]))


def one_sum_kernel(sent_ref, seen_ref, after_ref, one_ref):
    first = sent_ref.shape[0] - one_ref.shape[0]
    one_ref[...] = narrow(wide(sent_ref[first:]) + wide(seen_ref[first:]))


def local_kernel(
    block_depth,
    head_size,
    class_ref,
    table_ref,
    q_ref,
    k_ref,
    v_ref,
    g_ref,
    after_ref,
    qo_ref,
    ko_ref,
    vo_ref,
):
    head_count = table_ref.shape[1]
    tokens = q_ref.shape[0]
    gates = gate_lanes(class_ref, table_ref, 0, block_depth + 1)
    source = lax.broadcasted_iota(jnp.int32, (tokens, tokens), 0)
    target = lax.broadcasted_iota(jnp.int32, (tokens, tokens), 1)
    apart = jnp.bitwise_xor(source, target)
    causal = source <= target
    for head in range(head_count):
        columns = pl.ds(head * head_size, head_size)
        query_here = q_ref[:, columns]
        key_here = k_ref[:, columns]
        value_here = v_ref[:, columns]
        grad_here = g_ref[:, columns]
        weight = jnp.broadcast_to(gates[head : head + 1, :], (tokens, tokens))
        for level in range(1, block_depth + 1):
            row = level * head_count + head
            weight = jnp.where(apart >= 2 ** (level - 1), gates[row : row + 1, :], weight)
        weight = jnp.where(causal, weight, 0.0)
        weighted_scores = narrow(weight * product(key_here, query_here, 1, 1))
        weighted_grads = narrow(weight * product(value_here, grad_here, 1, 1))
        qo_ref[:, columns] = product(weighted_grads, key_here, 0, 0)
        ko_ref[:, columns] = product(weighted_grads, query_here, 1, 0)
        vo_ref[:, columns] = product(weighted_scores, grad_here, 1, 0)


def gate_columns(class_ref, table_ref, first, last):
    return gate_lanes(class_ref, table_ref, first, last).T


def final_kernel(
    offset,
    head_size,
    total,
    inner,
    flag_ref,
    class_ref,
    table_ref,
    k_ref,
    v_ref,
    g_ref,
    ql_ref,
    kl_ref,
    vl_ref,
    zero_ref,
    one_ref,
    two_own_ref,
    two_other_ref,
    piece0_ref,
    piece1_ref,
    piece2_ref,
    piece3_ref,
    split_own_ref,
    split_other_ref,
    qo_ref,
    ko_ref,
    vo_ref,
    held_ref,
):
    head_count = table_ref.shape[1]
    half = head_count // 2
    quarter = head_count // 4
    eighth = head_count // 8
    gates = gate_columns(class_ref, table_ref, offset, offset + total)
    x_place = flag_ref[0]
    z_place = flag_ref[1] + 2 * flag_ref[2]
    core = flag_ref[inner]
    held_ref[0] = zero_ref[...]
    held_ref[1] = one_ref[...]
    held_ref[2, pl.ds(x_place * half, half)] = two_own_ref[...]
    held_ref[2, pl.ds((1 - x_place) * half, half)] = two_other_ref[...]
    pieces = (piece0_ref, piece1_ref, piece2_ref, piece3_ref)
    split = inner + 1
    for level in range(NEAR, split):
        for offs in range(4):
            first = jnp.bitwise_xor(z_place, offs) * quarter
            row = (level - NEAR) * quarter
            held_ref[level, pl.ds(first, quarter)] = pieces[offs][row : row + quarter]
    for level in range(split, total):
        for offs in range(4):
            first = jnp.bitwise_xor(z_place, offs) * eighth
            rows = pl.ds(offs * eighth, eighth)
            held_ref[level, pl.ds(core * half + first, eighth)] = split_own_ref[level - split, rows]
            held_ref[level, pl.ds((1 - core) * half + first, eighth)] = split_other_ref[
                level - split, rows
            ]
    for head in range(head_count):
        columns = pl.ds(head * head_size, head_size)
        grad_here = g_ref[:, columns]
        query_total = ql_ref[:, columns]
        state_grad = jnp.zeros((head_size, head_size), jnp.float32)
        for level in range(total):
            state = held_ref[level, head]
            term = product(grad_here, state, 1, 1)
            row = level * head_count + head
            on = wide(flag_ref[level])
            query_total = query_total + (gates[:, row : row + 1] * on) * term
            state_grad = state_grad + wide(state) * (1.0 - on)
        grad_rounded = narrow(state_grad)
        qo_ref[:, columns] = narrow(query_total)
        ko_ref[:, columns] = narrow(
            kl_ref[:, columns] + product(v_ref[:, columns], grad_rounded, 1, 1)
        )
        vo_ref[:, columns] = narrow(
            vl_ref[:, columns] + product(k_ref[:, columns], grad_rounded, 1, 0)
        )


def per_device(query_rows, key_rows, value_rows, out_grad, gate_class, gate_table):
    row_count, width = query_rows.shape
    head_count = gate_table.shape[2]
    head_size = width // head_count
    inner_bits = level_bits(lax.axis_size("gy"))
    outer_bits = level_bits(lax.axis_size("gx"))
    total = inner_bits + outer_bits
    block_depth = level_bits(row_count)
    offset = block_depth + 1
    inner_index = lax.axis_index("gy")
    outer_index = lax.axis_index("gx")
    block_index = (outer_index << inner_bits) | inner_index
    flag_bits = (block_index >> jnp.arange(total, dtype=jnp.int32)) & 1
    inner_size = lax.axis_size("gy")
    device_count = inner_size * lax.axis_size("gx")

    def swap(block, *bits):
        mask = sum(1 << bit for bit in bits)
        if mask < inner_size:
            return lax.ppermute(block, "gy", [(i, i ^ mask) for i in range(inner_size)])
        if mask % inner_size == 0:
            mask = mask // inner_size
            size = lax.axis_size("gx")
            return lax.ppermute(block, "gx", [(i, i ^ mask) for i in range(size)])
        return lax.ppermute(block, ("gx", "gy"), [(i, i ^ mask) for i in range(device_count)])

    class_lanes = gate_class.reshape(1, row_count)
    table = jnp.transpose(gate_table, (1, 2, 0))
    smem = pl.BlockSpec(memory_space=pltpu.SMEM)
    vmem = pl.BlockSpec(memory_space=pltpu.VMEM)
    hbm = pl.BlockSpec(memory_space=pltpu.HBM)
    anywhere = pl.BlockSpec(memory_space=pl.ANY)
    cell = (head_size, head_size)

    def cells(*lead):
        return jax.ShapeDtypeStruct(lead + cell, jnp.bfloat16)

    def call(kernel, in_specs, outs, operands, flops=0, scratch=(), grant=VMEM_BYTES, out_specs=None, aliases=None):
        moved = sum(operand.size * operand.dtype.itemsize for operand in operands)
        return pl.pallas_call(
            kernel,
            out_shape=outs,
            in_specs=in_specs,
            out_specs=out_specs or jax.tree.map(lambda _: vmem, outs),
            input_output_aliases=aliases or {},
            scratch_shapes=scratch,
            compiler_params=pltpu.CompilerParams(vmem_limit_bytes=grant),
            cost_estimate=pl.CostEstimate(flops=flops, bytes_accessed=moved, transcendentals=0),
        )(*operands)

    quarter = head_count // 4
    half = head_count // 2
    eighth = head_count // 8
    split = inner_bits + 1
    whole_levels = split - NEAR
    split_levels = total - split
    cut = whole_levels * quarter
    share_rows = cut + split_levels * eighth
    block = pltpu.VMEM((row_count, width), jnp.bfloat16)

    levels = tuple(range(NEAR, total))
    first_reads = (class_lanes, table, query_rows, key_rows, value_rows, out_grad)
    outs = (cells(head_count + split_levels * half), cells(split_levels * half))
    if whole_levels > 1:
        outs = outs + (cells(whole_levels - 1, head_count),)
    sent, keep, *lead = call(
        functools.partial(upper_kernel, levels, split, offset, head_size),
        [smem] + [hbm] * 6,
        outs,
        (flag_bits, *[pltpu.with_memory_space_constraint(held, pltpu.HBM) for held in first_reads]),
        flops=2 * len(levels) * row_count * width * head_size,
        scratch=[
            pltpu.VMEM(class_lanes.shape, jnp.int32),
            pltpu.VMEM(table.shape, jnp.float32),
            block,
            block,
            block,
            block,
            pltpu.VMEM((split_levels, head_count) + cell, jnp.bfloat16),
            pltpu.SemaphoreType.DMA((6,)),
        ],
        grant=FIRST_BYTES,
    )
    seen = swap(sent, inner_bits)
    two_own, lower_sent, zero = call(
        functools.partial(lower_kernel, offset, head_size),
        [smem] + [vmem] * 6 + [anywhere],
        (cells(half), cells(half + head_count), cells(head_count)),
        (flag_bits, class_lanes, table, query_rows, key_rows, value_rows, out_grad, keep),
        flops=2 * NEAR * row_count * width * head_size,
        scratch=[pltpu.VMEM((head_count,) + cell, jnp.bfloat16)],
    )
    own_share, *shares_out = call(
        functools.partial(share_kernel, head_count, (whole_levels, split_levels)),
        [smem] + [vmem] * 2 + [anywhere] + [vmem] * len(lead),
        (cells(share_rows),) * 4,
        (flag_bits, seen, keep, two_own, *lead),
    )
    lower_seen = swap(lower_sent, 0)
    two_sum = call(
        two_sum_kernel, [vmem] * 2 + [anywhere], cells(half), (two_own, lower_seen, own_share)
    )
    big = jax.ShapeDtypeStruct((row_count, width), jnp.float32)

    def z_bits(offs):
        return [bit + 1 for bit in range(2) if offs >> bit & 1]

    came = [swap(shares_out[offs - 1], *z_bits(offs)) for offs in (3, 2, 1)]
    top = total - 1
    below, top_sent = call(
        functools.partial(four_sum_kernel, eighth),
        [vmem, anywhere] + [vmem] * 3,
        (cells(share_rows - eighth), cells(eighth)),
        (own_share, own_share, *came),
    )
    middle = [bit for bit in range(NEAR, top) if bit != inner_bits]
    if middle:
        part = wide(jnp.concatenate([below, top_sent], axis=0))
        parts = {
            level: part[(level - NEAR) * quarter : (level - NEAR + 1) * quarter]
            for level in range(NEAR, split)
        }
        for level in range(split, total):
            row = cut + (level - split) * eighth
            parts[level] = part[row : row + eighth]
        for bit in middle:
            going = range(bit, total)
            block_sent = narrow(jnp.concatenate([parts[level] for level in going], axis=0))
            seen_part = wide(swap(block_sent, bit))
            row = 0
            for level in going:
                size = parts[level].shape[0]
                got = seen_part[row : row + size]
                parts[level] = got if level == bit else parts[level] + got
                row += size
        below = narrow(jnp.concatenate([parts[level] for level in range(NEAR, top)], axis=0))
        top_sent = narrow(parts[top])
    one_sum = call(
        one_sum_kernel,
        [vmem] * 2 + [anywhere],
        cells(head_count),
        (lower_sent, lower_seen, below),
    )
    two_sum = call(
        two_sum_kernel, [vmem] * 2 + [anywhere], cells(half), (two_sum, swap(two_sum, 1), two_sum)
    )
    two_half = swap(two_sum, 2)
    two_rest = swap(two_half, 0)
    one_done = swap(one_sum, 1)
    zero_done = swap(zero, 0)
    shares = call(
        pair_sum_kernel,
        [vmem] * 4 + [anywhere] * 2,
        cells(share_rows),
        (below, swap(below, 0), swap(top_sent, top), swap(top_sent, 0, top), two_sum, zero_done),
    )
    query_local, key_local, value_local = call(
        functools.partial(local_kernel, block_depth, head_size),
        [vmem] * 6 + [anywhere],
        (big, big, big),
        (class_lanes, table, query_rows, key_rows, value_rows, out_grad, shares),
        flops=10 * row_count * width * row_count,
    )
    pieces = [shares] + [swap(shares, *z_bits(offs)) for offs in (1, 2, 3)]
    split_own = call(
        functools.partial(gather_kernel, cut),
        [vmem] * 4 + [anywhere] * 2,
        cells(split_levels, half),
        (*pieces, two_half, query_local),
    )
    split_other = swap(split_own, inner_bits)

    small = jax.ShapeDtypeStruct((row_count, width), jnp.bfloat16)
    return call(
        functools.partial(final_kernel, offset, head_size, total, inner_bits),
        [smem] + [vmem] * 18,
        (small, small, small),
        (
            flag_bits,
            class_lanes,
            table,
            key_rows,
            value_rows,
            out_grad,
            query_local,
            key_local,
            value_local,
            zero_done,
            one_done,
            two_half,
            two_rest,
            *pieces,
            split_own,
            split_other,
        ),
        flops=(2 * total + 4) * row_count * width * head_size,
        scratch=[pltpu.VMEM((total, head_count) + cell, jnp.bfloat16)],
    )


def solution(mesh):
    rows = P(("gx", "gy"), None)
    return jax.shard_map(
        per_device,
        mesh=mesh,
        in_specs=(rows, rows, rows, rows, P(("gx", "gy")), P()),
        out_specs=(rows, rows, rows),
        check_vma=False,
    )
```

```python
import functools

import jax
import jax.numpy as jnp
from jax import lax
from jax.experimental import pallas as pl
from jax.experimental.pallas import tpu as pltpu
from jax.sharding import PartitionSpec as P

NEAR = 3
VMEM_BYTES = 16 * 1024 * 1024
FIRST_BYTES = 16 * 1024 * 1024


def level_bits(amount):
    return amount.bit_length() - 1


def wide(values):
    return values.astype(jnp.float32)


def narrow(values):
    return values.astype(jnp.bfloat16)


def product(left, right, left_dim, right_dim):
    return lax.dot_general(
        left,
        right,
        (((left_dim,), (right_dim,)), ((), ())),
        preferred_element_type=jnp.float32,
    )


def gate_lanes(class_ref, table_ref, first, last):
    classes = table_ref.shape[2]
    tokens = class_ref.shape[1]
    rows = (last - first) * table_ref.shape[1]
    numbers = lax.broadcasted_iota(jnp.int32, (classes, tokens), 0)
    picker = (numbers == class_ref[...]).astype(jnp.float32)
    table = table_ref[first:last].reshape(rows, classes)
    return jnp.dot(
        table, picker, precision=lax.Precision.HIGHEST, preferred_element_type=jnp.float32
    )


def payload_cell(flags, gates, rows, level_places, q_ref, k_ref, v_ref, g_ref, columns, store):
    query_turned = wide(q_ref[:, columns].T)
    key_turned = wide(k_ref[:, columns].T)
    grad_here = wide(g_ref[:, columns])
    value_here = wide(v_ref[:, columns])
    for place in level_places:
        row = rows[place]
        flag = flags[place] == 1
        left = jnp.where(flag, gates[row : row + 1, :] * query_turned, key_turned)
        right = jnp.where(flag, grad_here, value_here)
        store(place, narrow(product(narrow(left), narrow(right), 1, 0)))


def upper_kernel(
    levels,
    split,
    offset,
    head_size,
    flag_ref,
    class_hbm,
    table_hbm,
    q_hbm,
    k_hbm,
    v_hbm,
    g_hbm,
    sent_ref,
    keep_ref,
    *rest,
):
    lead_refs = rest[:-8]
    class_ref, table_ref, q_ref, k_ref, v_ref, g_ref, late_ref, arrived = rest[-8:]
    moves = [
        pltpu.make_async_copy(source, target, arrived.at[place])
        for place, (source, target) in enumerate(
            (
                (class_hbm, class_ref),
                (table_hbm, table_ref),
                (q_hbm, q_ref),
                (k_hbm, k_ref),
                (g_hbm, g_ref),
                (v_hbm, v_ref),
            )
        )
    ]
    for move in moves:
        move.start()
    moves[0].wait()
    moves[1].wait()
    head_count = table_ref.shape[1]
    half = head_count // 2
    core = flag_ref[split - 1]
    gates = gate_lanes(class_ref, table_ref, offset + levels[0], offset + levels[-1] + 1)
    for move in moves[2:]:
        move.wait()
    flags = [flag_ref[level] for level in levels]
    for head in range(head_count):
        rows = [place * head_count + head for place in range(len(levels))]

        def store(place, value):
            level = levels[place]
            if level < split - 1:
                lead_refs[0][level - levels[0], head] = value
            elif level == split - 1:
                sent_ref[head] = value
            else:
                late_ref[level - split, head] = value

        columns = pl.ds(head * head_size, head_size)
        payload_cell(
            flags, gates, rows, range(len(levels)), q_ref, k_ref, v_ref, g_ref, columns, store
        )
    for place in range(levels[-1] + 1 - split):
        row = place * half
        keep_ref[row : row + half] = late_ref[place, pl.ds(core * half, half)]
        sent_ref[head_count + row : head_count + row + half] = late_ref[
            place, pl.ds((1 - core) * half, half)
        ]


def share_kernel(head_count, places, flag_ref, seen_ref, keep_ref, after_ref, *refs):
    lead_refs = refs[:-4]
    out_refs = refs[-4:]
    quarter = head_count // 4
    eighth = head_count // 8
    z_place = flag_ref[1] + 2 * flag_ref[2]
    for offs in range(4):
        place = jnp.bitwise_xor(z_place, offs)
        row = 0
        for lead in range(places[0] - 1):
            out_refs[offs][row : row + quarter] = lead_refs[0][lead, pl.ds(place * quarter, quarter)]
            row += quarter
        out_refs[offs][row : row + quarter] = seen_ref[pl.ds(place * quarter, quarter)]
        row += quarter
        for late in range(places[1]):
            first = late * (head_count // 2) + place * eighth
            total = wide(keep_ref[pl.ds(first, eighth)])
            total = total + wide(seen_ref[pl.ds(head_count + first, eighth)])
            out_refs[offs][row : row + eighth] = narrow(total)
            row += eighth


def lower_kernel(
    offset,
    head_size,
    flag_ref,
    class_ref,
    table_ref,
    q_ref,
    k_ref,
    v_ref,
    g_ref,
    after_ref,
    two_own_ref,
    sent_ref,
    zero_ref,
    two_ref,
):
    head_count = table_ref.shape[1]
    half = head_count // 2
    x_place = flag_ref[0]
    gates = gate_lanes(class_ref, table_ref, offset, offset + NEAR)
    flags = [flag_ref[level] for level in range(NEAR)]
    for head in range(head_count):
        rows = [place * head_count + head for place in range(NEAR)]

        def store(place, value):
            if place == 0:
                zero_ref[head] = value
            elif place == 1:
                sent_ref[half + head] = value
            else:
                two_ref[head] = value

        columns = pl.ds(head * head_size, head_size)
        payload_cell(flags, gates, rows, range(NEAR), q_ref, k_ref, v_ref, g_ref, columns, store)
    two_own_ref[...] = two_ref[pl.ds(x_place * half, half)]
    sent_ref[:half] = two_ref[pl.ds((1 - x_place) * half, half)]


def four_sum_kernel(top_rows, own_ref, after_ref, *refs):
    came_refs = refs[:-2]
    below_ref, top_ref = refs[-2:]
    total = wide(own_ref[...])
    for came_ref in came_refs:
        total = total + wide(came_ref[...])
    rows = total.shape[0] - top_rows
    below_ref[...] = narrow(total[:rows])
    top_ref[...] = narrow(total[rows:])


def pair_sum_kernel(below_ref, far_ref, near_top_ref, far_top_ref, *refs):
    out_ref = refs[-1]
    rows = below_ref.shape[0]
    out_ref[:rows] = narrow(wide(below_ref[...]) + wide(far_ref[...]))
    out_ref[rows:] = narrow(wide(near_top_ref[...]) + wide(far_top_ref[...]))


def gather_kernel(cut, piece0_ref, piece1_ref, piece2_ref, piece3_ref, after_ref, local_ref, out_ref):
    for offs, piece_ref in enumerate((piece0_ref, piece1_ref, piece2_ref, piece3_ref)):
        split_levels = out_ref.shape[0]
        eighth = out_ref.shape[1] // 4
        for level in range(split_levels):
            first = cut + level * eighth
            out_ref[level, offs * eighth : (offs + 1) * eighth] = piece_ref[first : first + eighth]


def two_sum_kernel(flag_ref, own_ref, seen_ref, after_ref, near_ref, far_ref):
    rows = near_ref.shape[0]
    place = flag_ref[1]
    for out_ref, part in ((near_ref, place), (far_ref, 1 - place)):
        cells = pl.ds(part * rows, rows)
        out_ref[...] = narrow(wide(own_ref[cells]) + wide(seen_ref[cells]))


def cross_kernel(near_ref, far_ref, out_ref):
    out_ref[...] = narrow(wide(near_ref[...]) + wide(far_ref[...]))


def join_kernel(flag_ref, own_ref, other_ref, out_ref):
    rows = own_ref.shape[0]
    place = flag_ref[1]
    out_ref[pl.ds(place * rows, rows)] = own_ref[...]
    out_ref[pl.ds((1 - place) * rows, rows)] = other_ref[...]


def one_sum_kernel(sent_ref, seen_ref, after_ref, one_ref):
    first = sent_ref.shape[0] - one_ref.shape[0]
    one_ref[...] = narrow(wide(sent_ref[first:]) + wide(seen_ref[first:]))


def local_kernel(
    block_depth,
    head_size,
    class_ref,
    table_ref,
    q_ref,
    k_ref,
    v_ref,
    g_ref,
    after_ref,
    qo_ref,
    ko_ref,
    vo_ref,
):
    head_count = table_ref.shape[1]
    tokens = q_ref.shape[0]
    gates = gate_lanes(class_ref, table_ref, 0, block_depth + 1)
    source = lax.broadcasted_iota(jnp.int32, (tokens, tokens), 0)
    target = lax.broadcasted_iota(jnp.int32, (tokens, tokens), 1)
    apart = jnp.bitwise_xor(source, target)
    causal = source <= target
    for head in range(head_count):
        columns = pl.ds(head * head_size, head_size)
        query_here = q_ref[:, columns]
        key_here = k_ref[:, columns]
        value_here = v_ref[:, columns]
        grad_here = g_ref[:, columns]
        weight = jnp.broadcast_to(gates[head : head + 1, :], (tokens, tokens))
        for level in range(1, block_depth + 1):
            row = level * head_count + head
            weight = jnp.where(apart >= 2 ** (level - 1), gates[row : row + 1, :], weight)
        weight = jnp.where(causal, weight, 0.0)
        weighted_scores = narrow(weight * product(key_here, query_here, 1, 1))
        weighted_grads = narrow(weight * product(value_here, grad_here, 1, 1))
        qo_ref[:, columns] = product(weighted_grads, key_here, 0, 0)
        ko_ref[:, columns] = product(weighted_grads, query_here, 1, 0)
        vo_ref[:, columns] = product(weighted_scores, grad_here, 1, 0)


def gate_columns(class_ref, table_ref, first, last):
    return gate_lanes(class_ref, table_ref, first, last).T


def final_kernel(
    offset,
    head_size,
    total,
    inner,
    flag_ref,
    class_ref,
    table_ref,
    k_ref,
    v_ref,
    g_ref,
    ql_ref,
    kl_ref,
    vl_ref,
    zero_ref,
    one_ref,
    two_own_ref,
    two_other_ref,
    piece0_ref,
    piece1_ref,
    piece2_ref,
    piece3_ref,
    split_own_ref,
    split_other_ref,
    qo_ref,
    ko_ref,
    vo_ref,
    held_ref,
):
    head_count = table_ref.shape[1]
    half = head_count // 2
    quarter = head_count // 4
    eighth = head_count // 8
    gates = gate_columns(class_ref, table_ref, offset, offset + total)
    x_place = flag_ref[0]
    z_place = flag_ref[1] + 2 * flag_ref[2]
    core = flag_ref[inner]
    held_ref[0] = zero_ref[...]
    held_ref[1] = one_ref[...]
    held_ref[2, pl.ds(x_place * half, half)] = two_own_ref[...]
    held_ref[2, pl.ds((1 - x_place) * half, half)] = two_other_ref[...]
    pieces = (piece0_ref, piece1_ref, piece2_ref, piece3_ref)
    split = inner + 1
    for level in range(NEAR, split):
        for offs in range(4):
            first = jnp.bitwise_xor(z_place, offs) * quarter
            row = (level - NEAR) * quarter
            held_ref[level, pl.ds(first, quarter)] = pieces[offs][row : row + quarter]
    for level in range(split, total):
        for offs in range(4):
            first = jnp.bitwise_xor(z_place, offs) * eighth
            rows = pl.ds(offs * eighth, eighth)
            held_ref[level, pl.ds(core * half + first, eighth)] = split_own_ref[level - split, rows]
            held_ref[level, pl.ds((1 - core) * half + first, eighth)] = split_other_ref[
                level - split, rows
            ]
    for head in range(head_count):
        columns = pl.ds(head * head_size, head_size)
        grad_here = g_ref[:, columns]
        query_total = ql_ref[:, columns]
        state_grad = jnp.zeros((head_size, head_size), jnp.float32)
        for level in range(total):
            state = held_ref[level, head]
            term = product(grad_here, state, 1, 1)
            row = level * head_count + head
            on = wide(flag_ref[level])
            query_total = query_total + (gates[:, row : row + 1] * on) * term
            state_grad = state_grad + wide(state) * (1.0 - on)
        grad_rounded = narrow(state_grad)
        qo_ref[:, columns] = narrow(query_total)
        ko_ref[:, columns] = narrow(
            kl_ref[:, columns] + product(v_ref[:, columns], grad_rounded, 1, 1)
        )
        vo_ref[:, columns] = narrow(
            vl_ref[:, columns] + product(k_ref[:, columns], grad_rounded, 1, 0)
        )


def per_device(query_rows, key_rows, value_rows, out_grad, gate_class, gate_table):
    row_count, width = query_rows.shape
    head_count = gate_table.shape[2]
    head_size = width // head_count
    inner_bits = level_bits(lax.axis_size("gy"))
    outer_bits = level_bits(lax.axis_size("gx"))
    total = inner_bits + outer_bits
    block_depth = level_bits(row_count)
    offset = block_depth + 1
    inner_index = lax.axis_index("gy")
    outer_index = lax.axis_index("gx")
    block_index = (outer_index << inner_bits) | inner_index
    flag_bits = (block_index >> jnp.arange(total, dtype=jnp.int32)) & 1
    inner_size = lax.axis_size("gy")
    device_count = inner_size * lax.axis_size("gx")

    def swap(block, *bits):
        mask = sum(1 << bit for bit in bits)
        if mask < inner_size:
            return lax.ppermute(block, "gy", [(i, i ^ mask) for i in range(inner_size)])
        if mask % inner_size == 0:
            mask = mask // inner_size
            size = lax.axis_size("gx")
            return lax.ppermute(block, "gx", [(i, i ^ mask) for i in range(size)])
        return lax.ppermute(block, ("gx", "gy"), [(i, i ^ mask) for i in range(device_count)])

    class_lanes = gate_class.reshape(1, row_count)
    table = jnp.transpose(gate_table, (1, 2, 0))
    smem = pl.BlockSpec(memory_space=pltpu.SMEM)
    vmem = pl.BlockSpec(memory_space=pltpu.VMEM)
    hbm = pl.BlockSpec(memory_space=pltpu.HBM)
    anywhere = pl.BlockSpec(memory_space=pl.ANY)
    cell = (head_size, head_size)

    def cells(*lead):
        return jax.ShapeDtypeStruct(lead + cell, jnp.bfloat16)

    def call(kernel, in_specs, outs, operands, flops=0, scratch=(), grant=VMEM_BYTES, out_specs=None, aliases=None):
        moved = sum(operand.size * operand.dtype.itemsize for operand in operands)
        return pl.pallas_call(
            kernel,
            out_shape=outs,
            in_specs=in_specs,
            out_specs=out_specs or jax.tree.map(lambda _: vmem, outs),
            input_output_aliases=aliases or {},
            scratch_shapes=scratch,
            compiler_params=pltpu.CompilerParams(vmem_limit_bytes=grant),
            cost_estimate=pl.CostEstimate(flops=flops, bytes_accessed=moved, transcendentals=0),
        )(*operands)

    quarter = head_count // 4
    half = head_count // 2
    eighth = head_count // 8
    split = inner_bits + 1
    whole_levels = split - NEAR
    split_levels = total - split
    cut = whole_levels * quarter
    share_rows = cut + split_levels * eighth
    block = pltpu.VMEM((row_count, width), jnp.bfloat16)

    levels = tuple(range(NEAR, total))
    first_reads = (class_lanes, table, query_rows, key_rows, value_rows, out_grad)
    outs = (cells(head_count + split_levels * half), cells(split_levels * half))
    if whole_levels > 1:
        outs = outs + (cells(whole_levels - 1, head_count),)
    sent, keep, *lead = call(
        functools.partial(upper_kernel, levels, split, offset, head_size),
        [smem] + [hbm] * 6,
        outs,
        (flag_bits, *[pltpu.with_memory_space_constraint(held, pltpu.HBM) for held in first_reads]),
        flops=2 * len(levels) * row_count * width * head_size,
        scratch=[
            pltpu.VMEM(class_lanes.shape, jnp.int32),
            pltpu.VMEM(table.shape, jnp.float32),
            block,
            block,
            block,
            block,
            pltpu.VMEM((split_levels, head_count) + cell, jnp.bfloat16),
            pltpu.SemaphoreType.DMA((6,)),
        ],
        grant=FIRST_BYTES,
    )
    seen = swap(sent, inner_bits)
    two_own, lower_sent, zero = call(
        functools.partial(lower_kernel, offset, head_size),
        [smem] + [vmem] * 6 + [anywhere],
        (cells(half), cells(half + head_count), cells(head_count)),
        (flag_bits, class_lanes, table, query_rows, key_rows, value_rows, out_grad, keep),
        flops=2 * NEAR * row_count * width * head_size,
        scratch=[pltpu.VMEM((head_count,) + cell, jnp.bfloat16)],
    )
    own_share, *shares_out = call(
        functools.partial(share_kernel, head_count, (whole_levels, split_levels)),
        [smem] + [vmem] * 2 + [anywhere] + [vmem] * len(lead),
        (cells(share_rows),) * 4,
        (flag_bits, seen, keep, two_own, *lead),
    )
    lower_seen = swap(lower_sent, 0)
    two_near, two_far = call(
        two_sum_kernel,
        [smem] + [vmem] * 2 + [anywhere],
        (cells(quarter), cells(quarter)),
        (flag_bits, two_own, lower_seen, own_share),
    )
    two_cross = call(
        cross_kernel, [vmem] * 2, cells(quarter), (swap(two_near, 2), swap(two_far, 1, 2))
    )
    big = jax.ShapeDtypeStruct((row_count, width), jnp.float32)

    def z_bits(offs):
        return [bit + 1 for bit in range(2) if offs >> bit & 1]

    came = [swap(shares_out[offs - 1], *z_bits(offs)) for offs in (3, 2, 1)]
    top = total - 1
    below, top_sent = call(
        functools.partial(four_sum_kernel, eighth),
        [vmem, anywhere] + [vmem] * 3,
        (cells(share_rows - eighth), cells(eighth)),
        (own_share, own_share, *came),
    )
    middle = [bit for bit in range(NEAR, top) if bit != inner_bits]
    if middle:
        part = wide(jnp.concatenate([below, top_sent], axis=0))
        parts = {
            level: part[(level - NEAR) * quarter : (level - NEAR + 1) * quarter]
            for level in range(NEAR, split)
        }
        for level in range(split, total):
            row = cut + (level - split) * eighth
            parts[level] = part[row : row + eighth]
        for bit in middle:
            going = range(bit, total)
            block_sent = narrow(jnp.concatenate([parts[level] for level in going], axis=0))
            seen_part = wide(swap(block_sent, bit))
            row = 0
            for level in going:
                size = parts[level].shape[0]
                got = seen_part[row : row + size]
                parts[level] = got if level == bit else parts[level] + got
                row += size
        below = narrow(jnp.concatenate([parts[level] for level in range(NEAR, top)], axis=0))
        top_sent = narrow(parts[top])
    one_sum = call(
        one_sum_kernel,
        [vmem] * 2 + [anywhere],
        cells(head_count),
        (lower_sent, lower_seen, below),
    )
    two_half = call(
        join_kernel,
        [smem] + [vmem] * 2,
        cells(half),
        (flag_bits, two_cross, swap(two_cross, 1)),
    )
    two_rest = swap(two_half, 0)
    one_done = swap(one_sum, 1)
    zero_done = swap(zero, 0)
    shares = call(
        pair_sum_kernel,
        [vmem] * 4 + [anywhere] * 2,
        cells(share_rows),
        (below, swap(below, 0), swap(top_sent, top), swap(top_sent, 0, top), two_cross, zero_done),
    )
    query_local, key_local, value_local = call(
        functools.partial(local_kernel, block_depth, head_size),
        [vmem] * 6 + [anywhere],
        (big, big, big),
        (class_lanes, table, query_rows, key_rows, value_rows, out_grad, shares),
        flops=10 * row_count * width * row_count,
    )
    pieces = [shares] + [swap(shares, *z_bits(offs)) for offs in (1, 2, 3)]
    split_own = call(
        functools.partial(gather_kernel, cut),
        [vmem] * 4 + [anywhere] * 2,
        cells(split_levels, half),
        (*pieces, two_half, query_local),
    )
    split_other = swap(split_own, inner_bits)

    small = jax.ShapeDtypeStruct((row_count, width), jnp.bfloat16)
    return call(
        functools.partial(final_kernel, offset, head_size, total, inner_bits),
        [smem] + [vmem] * 18,
        (small, small, small),
        (
            flag_bits,
            class_lanes,
            table,
            key_rows,
            value_rows,
            out_grad,
            query_local,
            key_local,
            value_local,
            zero_done,
            one_done,
            two_half,
            two_rest,
            *pieces,
            split_own,
            split_other,
        ),
        flops=(2 * total + 4) * row_count * width * head_size,
        scratch=[pltpu.VMEM((total, head_count) + cell, jnp.bfloat16)],
    )


def solution(mesh):
    rows = P(("gx", "gy"), None)
    return jax.shard_map(
        per_device,
        mesh=mesh,
        in_specs=(rows, rows, rows, rows, P(("gx", "gy")), P()),
        out_specs=(rows, rows, rows),
        check_vma=False,
    )
```

```python
import functools

import jax
import jax.numpy as jnp
from jax import lax
from jax.experimental import pallas as pl
from jax.experimental.pallas import tpu as pltpu
from jax.sharding import PartitionSpec as P

NEAR = 3
VMEM_BYTES = 16 * 1024 * 1024
FIRST_BYTES = 16 * 1024 * 1024


def level_bits(amount):
    return amount.bit_length() - 1


def wide(values):
    return values.astype(jnp.float32)


def narrow(values):
    return values.astype(jnp.bfloat16)


def product(left, right, left_dim, right_dim):
    return lax.dot_general(
        left,
        right,
        (((left_dim,), (right_dim,)), ((), ())),
        preferred_element_type=jnp.float32,
    )


def gate_lanes(class_ref, table_ref, first, last):
    classes = table_ref.shape[2]
    tokens = class_ref.shape[1]
    rows = (last - first) * table_ref.shape[1]
    numbers = lax.broadcasted_iota(jnp.int32, (classes, tokens), 0)
    picker = (numbers == class_ref[...]).astype(jnp.float32)
    table = table_ref[first:last].reshape(rows, classes)
    return jnp.dot(
        table, picker, precision=lax.Precision.HIGHEST, preferred_element_type=jnp.float32
    )


def payload_cell(flags, gates, rows, level_places, q_ref, k_ref, v_ref, g_ref, columns, store):
    query_turned = wide(q_ref[:, columns].T)
    key_turned = wide(k_ref[:, columns].T)
    grad_here = wide(g_ref[:, columns])
    value_here = wide(v_ref[:, columns])
    for place in level_places:
        row = rows[place]
        flag = flags[place] == 1
        left = jnp.where(flag, gates[row : row + 1, :] * query_turned, key_turned)
        right = jnp.where(flag, grad_here, value_here)
        store(place, narrow(product(narrow(left), narrow(right), 1, 0)))


def upper_kernel(
    levels,
    split,
    offset,
    head_size,
    flag_ref,
    class_hbm,
    table_hbm,
    q_hbm,
    k_hbm,
    v_hbm,
    g_hbm,
    sent_ref,
    keep_ref,
    *rest,
):
    lead_refs = rest[:-8]
    class_ref, table_ref, q_ref, k_ref, v_ref, g_ref, late_ref, arrived = rest[-8:]
    moves = [
        pltpu.make_async_copy(source, target, arrived.at[place])
        for place, (source, target) in enumerate(
            (
                (class_hbm, class_ref),
                (table_hbm, table_ref),
                (q_hbm, q_ref),
                (k_hbm, k_ref),
                (g_hbm, g_ref),
                (v_hbm, v_ref),
            )
        )
    ]
    for move in moves:
        move.start()
    moves[0].wait()
    moves[1].wait()
    head_count = table_ref.shape[1]
    half = head_count // 2
    core = flag_ref[split - 1]
    gates = gate_lanes(class_ref, table_ref, offset + levels[0], offset + levels[-1] + 1)
    for move in moves[2:]:
        move.wait()
    flags = [flag_ref[level] for level in levels]
    for head in range(head_count):
        rows = [place * head_count + head for place in range(len(levels))]

        def store(place, value):
            level = levels[place]
            if level < split - 1:
                lead_refs[0][level - levels[0], head] = value
            elif level == split - 1:
                sent_ref[head] = value
            else:
                late_ref[level - split, head] = value

        columns = pl.ds(head * head_size, head_size)
        payload_cell(
            flags, gates, rows, range(len(levels)), q_ref, k_ref, v_ref, g_ref, columns, store
        )
    for place in range(levels[-1] + 1 - split):
        row = place * half
        keep_ref[row : row + half] = late_ref[place, pl.ds(core * half, half)]
        sent_ref[head_count + row : head_count + row + half] = late_ref[
            place, pl.ds((1 - core) * half, half)
        ]


def share_kernel(head_count, places, flag_ref, seen_ref, keep_ref, after_ref, *refs):
    lead_refs = refs[:-4]
    out_refs = refs[-4:]
    quarter = head_count // 4
    eighth = head_count // 8
    z_place = flag_ref[1] + 2 * flag_ref[2]
    for offs in range(4):
        place = jnp.bitwise_xor(z_place, offs)
        row = 0
        for lead in range(places[0] - 1):
            out_refs[offs][row : row + quarter] = lead_refs[0][lead, pl.ds(place * quarter, quarter)]
            row += quarter
        out_refs[offs][row : row + quarter] = seen_ref[pl.ds(place * quarter, quarter)]
        row += quarter
        for late in range(places[1]):
            first = late * (head_count // 2) + place * eighth
            total = wide(keep_ref[pl.ds(first, eighth)])
            total = total + wide(seen_ref[pl.ds(head_count + first, eighth)])
            out_refs[offs][row : row + eighth] = narrow(total)
            row += eighth


def lower_kernel(
    offset,
    head_size,
    flag_ref,
    class_ref,
    table_ref,
    q_ref,
    k_ref,
    v_ref,
    g_ref,
    after_ref,
    two_own_ref,
    sent_ref,
    rest_ref,
    two_ref,
):
    head_count = table_ref.shape[1]
    half = head_count // 2
    x_place = flag_ref[0]
    gates = gate_lanes(class_ref, table_ref, offset, offset + NEAR)
    flags = [flag_ref[level] for level in range(NEAR)]
    for head in range(head_count):
        rows = [place * head_count + head for place in range(NEAR)]

        def store(place, value):
            if place == 0:
                rest_ref[half + head] = value
            elif place == 1:
                if head < half:
                    sent_ref[half + head] = value
                else:
                    rest_ref[head - half] = value
            else:
                two_ref[head] = value

        columns = pl.ds(head * head_size, head_size)
        payload_cell(flags, gates, rows, range(NEAR), q_ref, k_ref, v_ref, g_ref, columns, store)
    two_own_ref[...] = two_ref[pl.ds(x_place * half, half)]
    sent_ref[:half] = two_ref[pl.ds((1 - x_place) * half, half)]


def four_sum_kernel(top_rows, own_ref, after_ref, *refs):
    came_refs = refs[:-2]
    below_ref, top_ref = refs[-2:]
    total = wide(own_ref[...])
    for came_ref in came_refs:
        total = total + wide(came_ref[...])
    rows = total.shape[0] - top_rows
    below_ref[...] = narrow(total[:rows])
    top_ref[...] = narrow(total[rows:])


def pair_sum_kernel(below_ref, far_ref, near_top_ref, far_top_ref, *refs):
    out_ref = refs[-1]
    rows = below_ref.shape[0]
    out_ref[:rows] = narrow(wide(below_ref[...]) + wide(far_ref[...]))
    out_ref[rows:] = narrow(wide(near_top_ref[...]) + wide(far_top_ref[...]))


def gather_kernel(cut, piece0_ref, piece1_ref, piece2_ref, piece3_ref, after_ref, local_ref, out_ref):
    for offs, piece_ref in enumerate((piece0_ref, piece1_ref, piece2_ref, piece3_ref)):
        split_levels = out_ref.shape[0]
        eighth = out_ref.shape[1] // 4
        for level in range(split_levels):
            first = cut + level * eighth
            out_ref[level, offs * eighth : (offs + 1) * eighth] = piece_ref[first : first + eighth]


def two_sum_kernel(own_ref, seen_ref, after_ref, two_ref):
    two_ref[...] = narrow(wide(own_ref[...]) + wide(seen_ref[: own_ref.shape[0]]))


def one_sum_kernel(sent_ref, seen_ref, rest_ref, rest_seen_ref, after_ref, one_ref):
    half = one_ref.shape[0] // 2
    one_ref[:half] = narrow(wide(sent_ref[half:]) + wide(seen_ref[half:]))
    one_ref[half:] = narrow(wide(rest_ref[:half]) + wide(rest_seen_ref[:half]))


def local_kernel(
    block_depth,
    head_size,
    class_ref,
    table_ref,
    q_ref,
    k_ref,
    v_ref,
    g_ref,
    after_ref,
    qo_ref,
    ko_ref,
    vo_ref,
):
    head_count = table_ref.shape[1]
    tokens = q_ref.shape[0]
    gates = gate_lanes(class_ref, table_ref, 0, block_depth + 1)
    source = lax.broadcasted_iota(jnp.int32, (tokens, tokens), 0)
    target = lax.broadcasted_iota(jnp.int32, (tokens, tokens), 1)
    apart = jnp.bitwise_xor(source, target)
    causal = source <= target
    for head in range(head_count):
        columns = pl.ds(head * head_size, head_size)
        query_here = q_ref[:, columns]
        key_here = k_ref[:, columns]
        value_here = v_ref[:, columns]
        grad_here = g_ref[:, columns]
        weight = jnp.broadcast_to(gates[head : head + 1, :], (tokens, tokens))
        for level in range(1, block_depth + 1):
            row = level * head_count + head
            weight = jnp.where(apart >= 2 ** (level - 1), gates[row : row + 1, :], weight)
        weight = jnp.where(causal, weight, 0.0)
        weighted_scores = narrow(weight * product(key_here, query_here, 1, 1))
        weighted_grads = narrow(weight * product(value_here, grad_here, 1, 1))
        qo_ref[:, columns] = product(weighted_grads, key_here, 0, 0)
        ko_ref[:, columns] = product(weighted_grads, query_here, 1, 0)
        vo_ref[:, columns] = product(weighted_scores, grad_here, 1, 0)


def gate_columns(class_ref, table_ref, first, last):
    return gate_lanes(class_ref, table_ref, first, last).T


def final_kernel(
    offset,
    head_size,
    total,
    inner,
    flag_ref,
    class_ref,
    table_ref,
    k_ref,
    v_ref,
    g_ref,
    ql_ref,
    kl_ref,
    vl_ref,
    zero_ref,
    one_ref,
    two_own_ref,
    two_other_ref,
    piece0_ref,
    piece1_ref,
    piece2_ref,
    piece3_ref,
    split_own_ref,
    split_other_ref,
    qo_ref,
    ko_ref,
    vo_ref,
    held_ref,
):
    head_count = table_ref.shape[1]
    half = head_count // 2
    quarter = head_count // 4
    eighth = head_count // 8
    gates = gate_columns(class_ref, table_ref, offset, offset + total)
    x_place = flag_ref[0]
    z_place = flag_ref[1] + 2 * flag_ref[2]
    core = flag_ref[inner]
    held_ref[0] = zero_ref[zero_ref.shape[0] - head_count :]
    held_ref[1] = one_ref[...]
    held_ref[2, pl.ds(x_place * half, half)] = two_own_ref[...]
    held_ref[2, pl.ds((1 - x_place) * half, half)] = two_other_ref[...]
    pieces = (piece0_ref, piece1_ref, piece2_ref, piece3_ref)
    split = inner + 1
    for level in range(NEAR, split):
        for offs in range(4):
            first = jnp.bitwise_xor(z_place, offs) * quarter
            row = (level - NEAR) * quarter
            held_ref[level, pl.ds(first, quarter)] = pieces[offs][row : row + quarter]
    for level in range(split, total):
        for offs in range(4):
            first = jnp.bitwise_xor(z_place, offs) * eighth
            rows = pl.ds(offs * eighth, eighth)
            held_ref[level, pl.ds(core * half + first, eighth)] = split_own_ref[level - split, rows]
            held_ref[level, pl.ds((1 - core) * half + first, eighth)] = split_other_ref[
                level - split, rows
            ]
    for head in range(head_count):
        columns = pl.ds(head * head_size, head_size)
        grad_here = g_ref[:, columns]
        query_total = ql_ref[:, columns]
        state_grad = jnp.zeros((head_size, head_size), jnp.float32)
        for level in range(total):
            state = held_ref[level, head]
            term = product(grad_here, state, 1, 1)
            row = level * head_count + head
            on = wide(flag_ref[level])
            query_total = query_total + (gates[:, row : row + 1] * on) * term
            state_grad = state_grad + wide(state) * (1.0 - on)
        grad_rounded = narrow(state_grad)
        qo_ref[:, columns] = narrow(query_total)
        ko_ref[:, columns] = narrow(
            kl_ref[:, columns] + product(v_ref[:, columns], grad_rounded, 1, 1)
        )
        vo_ref[:, columns] = narrow(
            vl_ref[:, columns] + product(k_ref[:, columns], grad_rounded, 1, 0)
        )


def per_device(query_rows, key_rows, value_rows, out_grad, gate_class, gate_table):
    row_count, width = query_rows.shape
    head_count = gate_table.shape[2]
    head_size = width // head_count
    inner_bits = level_bits(lax.axis_size("gy"))
    outer_bits = level_bits(lax.axis_size("gx"))
    total = inner_bits + outer_bits
    block_depth = level_bits(row_count)
    offset = block_depth + 1
    inner_index = lax.axis_index("gy")
    outer_index = lax.axis_index("gx")
    block_index = (outer_index << inner_bits) | inner_index
    flag_bits = (block_index >> jnp.arange(total, dtype=jnp.int32)) & 1
    inner_size = lax.axis_size("gy")
    device_count = inner_size * lax.axis_size("gx")

    def swap(block, *bits):
        mask = sum(1 << bit for bit in bits)
        if mask < inner_size:
            return lax.ppermute(block, "gy", [(i, i ^ mask) for i in range(inner_size)])
        if mask % inner_size == 0:
            mask = mask // inner_size
            size = lax.axis_size("gx")
            return lax.ppermute(block, "gx", [(i, i ^ mask) for i in range(size)])
        return lax.ppermute(block, ("gx", "gy"), [(i, i ^ mask) for i in range(device_count)])

    class_lanes = gate_class.reshape(1, row_count)
    table = jnp.transpose(gate_table, (1, 2, 0))
    smem = pl.BlockSpec(memory_space=pltpu.SMEM)
    vmem = pl.BlockSpec(memory_space=pltpu.VMEM)
    hbm = pl.BlockSpec(memory_space=pltpu.HBM)
    anywhere = pl.BlockSpec(memory_space=pl.ANY)
    cell = (head_size, head_size)

    def cells(*lead):
        return jax.ShapeDtypeStruct(lead + cell, jnp.bfloat16)

    def call(kernel, in_specs, outs, operands, flops=0, scratch=(), grant=VMEM_BYTES, out_specs=None, aliases=None):
        moved = sum(operand.size * operand.dtype.itemsize for operand in operands)
        return pl.pallas_call(
            kernel,
            out_shape=outs,
            in_specs=in_specs,
            out_specs=out_specs or jax.tree.map(lambda _: vmem, outs),
            input_output_aliases=aliases or {},
            scratch_shapes=scratch,
            compiler_params=pltpu.CompilerParams(vmem_limit_bytes=grant),
            cost_estimate=pl.CostEstimate(flops=flops, bytes_accessed=moved, transcendentals=0),
        )(*operands)

    quarter = head_count // 4
    half = head_count // 2
    eighth = head_count // 8
    split = inner_bits + 1
    whole_levels = split - NEAR
    split_levels = total - split
    cut = whole_levels * quarter
    share_rows = cut + split_levels * eighth
    block = pltpu.VMEM((row_count, width), jnp.bfloat16)

    levels = tuple(range(NEAR, total))
    first_reads = (class_lanes, table, query_rows, key_rows, value_rows, out_grad)
    outs = (cells(head_count + split_levels * half), cells(split_levels * half))
    if whole_levels > 1:
        outs = outs + (cells(whole_levels - 1, head_count),)
    sent, keep, *lead = call(
        functools.partial(upper_kernel, levels, split, offset, head_size),
        [smem] + [hbm] * 6,
        outs,
        (flag_bits, *[pltpu.with_memory_space_constraint(held, pltpu.HBM) for held in first_reads]),
        flops=2 * len(levels) * row_count * width * head_size,
        scratch=[
            pltpu.VMEM(class_lanes.shape, jnp.int32),
            pltpu.VMEM(table.shape, jnp.float32),
            block,
            block,
            block,
            block,
            pltpu.VMEM((split_levels, head_count) + cell, jnp.bfloat16),
            pltpu.SemaphoreType.DMA((6,)),
        ],
        grant=FIRST_BYTES,
    )
    seen = swap(sent, inner_bits)
    two_own, lower_sent, rest = call(
        functools.partial(lower_kernel, offset, head_size),
        [smem] + [vmem] * 6 + [anywhere],
        (cells(half), cells(2 * half), cells(half + head_count)),
        (flag_bits, class_lanes, table, query_rows, key_rows, value_rows, out_grad, keep),
        flops=2 * NEAR * row_count * width * head_size,
        scratch=[pltpu.VMEM((head_count,) + cell, jnp.bfloat16)],
    )
    own_share, *shares_out = call(
        functools.partial(share_kernel, head_count, (whole_levels, split_levels)),
        [smem] + [vmem] * 2 + [anywhere] + [vmem] * len(lead),
        (cells(share_rows),) * 4,
        (flag_bits, seen, keep, two_own, *lead),
    )
    lower_seen = swap(lower_sent, 0)
    rest_seen = swap(rest, 0)
    two_sum = call(
        two_sum_kernel, [vmem] * 2 + [anywhere], cells(half), (two_own, lower_seen, own_share)
    )
    big = jax.ShapeDtypeStruct((row_count, width), jnp.float32)

    def z_bits(offs):
        return [bit + 1 for bit in range(2) if offs >> bit & 1]

    came = [swap(shares_out[offs - 1], *z_bits(offs)) for offs in (3, 2, 1)]
    top = total - 1
    below, top_sent = call(
        functools.partial(four_sum_kernel, eighth),
        [vmem, anywhere] + [vmem] * 3,
        (cells(share_rows - eighth), cells(eighth)),
        (own_share, own_share, *came),
    )
    middle = [bit for bit in range(NEAR, top) if bit != inner_bits]
    if middle:
        part = wide(jnp.concatenate([below, top_sent], axis=0))
        parts = {
            level: part[(level - NEAR) * quarter : (level - NEAR + 1) * quarter]
            for level in range(NEAR, split)
        }
        for level in range(split, total):
            row = cut + (level - split) * eighth
            parts[level] = part[row : row + eighth]
        for bit in middle:
            going = range(bit, total)
            block_sent = narrow(jnp.concatenate([parts[level] for level in going], axis=0))
            seen_part = wide(swap(block_sent, bit))
            row = 0
            for level in going:
                size = parts[level].shape[0]
                got = seen_part[row : row + size]
                parts[level] = got if level == bit else parts[level] + got
                row += size
        below = narrow(jnp.concatenate([parts[level] for level in range(NEAR, top)], axis=0))
        top_sent = narrow(parts[top])
    one_sum = call(
        one_sum_kernel,
        [vmem] * 4 + [anywhere],
        cells(head_count),
        (lower_sent, lower_seen, rest, rest_seen, below),
    )
    two_sum = call(
        two_sum_kernel, [vmem] * 2 + [anywhere], cells(half), (two_sum, swap(two_sum, 1), two_sum)
    )
    two_half = swap(two_sum, 2)
    two_rest = swap(two_half, 0)
    one_done = swap(one_sum, 1)
    shares = call(
        pair_sum_kernel,
        [vmem] * 4 + [anywhere] * 2,
        cells(share_rows),
        (below, swap(below, 0), swap(top_sent, top), swap(top_sent, 0, top), two_sum, rest_seen),
    )
    query_local, key_local, value_local = call(
        functools.partial(local_kernel, block_depth, head_size),
        [vmem] * 6 + [anywhere],
        (big, big, big),
        (class_lanes, table, query_rows, key_rows, value_rows, out_grad, shares),
        flops=10 * row_count * width * row_count,
    )
    pieces = [shares] + [swap(shares, *z_bits(offs)) for offs in (1, 2, 3)]
    split_own = call(
        functools.partial(gather_kernel, cut),
        [vmem] * 4 + [anywhere] * 2,
        cells(split_levels, half),
        (*pieces, two_half, query_local),
    )
    split_other = swap(split_own, inner_bits)

    small = jax.ShapeDtypeStruct((row_count, width), jnp.bfloat16)
    return call(
        functools.partial(final_kernel, offset, head_size, total, inner_bits),
        [smem] + [vmem] * 18,
        (small, small, small),
        (
            flag_bits,
            class_lanes,
            table,
            key_rows,
            value_rows,
            out_grad,
            query_local,
            key_local,
            value_local,
            rest_seen,
            one_done,
            two_half,
            two_rest,
            *pieces,
            split_own,
            split_other,
        ),
        flops=(2 * total + 4) * row_count * width * head_size,
        scratch=[pltpu.VMEM((total, head_count) + cell, jnp.bfloat16)],
    )


def solution(mesh):
    rows = P(("gx", "gy"), None)
    return jax.shard_map(
        per_device,
        mesh=mesh,
        in_specs=(rows, rows, rows, rows, P(("gx", "gy")), P()),
        out_specs=(rows, rows, rows),
        check_vma=False,
    )
```

```python
import functools

import jax
import jax.numpy as jnp
from jax import lax
from jax.experimental import pallas as pl
from jax.experimental.pallas import tpu as pltpu
from jax.sharding import PartitionSpec as P

NEAR = 3
VMEM_BYTES = 16 * 1024 * 1024
FIRST_BYTES = 16 * 1024 * 1024


def level_bits(amount):
    return amount.bit_length() - 1


def wide(values):
    return values.astype(jnp.float32)


def narrow(values):
    return values.astype(jnp.bfloat16)


def product(left, right, left_dim, right_dim):
    return lax.dot_general(
        left,
        right,
        (((left_dim,), (right_dim,)), ((), ())),
        preferred_element_type=jnp.float32,
    )


def gate_lanes(class_ref, table_ref, first, last):
    classes = table_ref.shape[2]
    tokens = class_ref.shape[1]
    rows = (last - first) * table_ref.shape[1]
    numbers = lax.broadcasted_iota(jnp.int32, (classes, tokens), 0)
    picker = (numbers == class_ref[...]).astype(jnp.float32)
    table = table_ref[first:last].reshape(rows, classes)
    return jnp.dot(
        table, picker, precision=lax.Precision.HIGHEST, preferred_element_type=jnp.float32
    )


def payload_cell(flags, gates, rows, level_places, q_ref, k_ref, v_ref, g_ref, columns, store):
    query_turned = wide(q_ref[:, columns].T)
    key_turned = wide(k_ref[:, columns].T)
    grad_here = wide(g_ref[:, columns])
    value_here = wide(v_ref[:, columns])
    for place in level_places:
        row = rows[place]
        flag = flags[place] == 1
        left = jnp.where(flag, gates[row : row + 1, :] * query_turned, key_turned)
        right = jnp.where(flag, grad_here, value_here)
        store(place, narrow(product(narrow(left), narrow(right), 1, 0)))


def upper_kernel(
    levels,
    split,
    offset,
    head_size,
    flag_ref,
    class_hbm,
    table_hbm,
    q_hbm,
    k_hbm,
    v_hbm,
    g_hbm,
    sent_ref,
    keep_ref,
    *rest,
):
    lead_refs = rest[:-8]
    class_ref, table_ref, q_ref, k_ref, v_ref, g_ref, late_ref, arrived = rest[-8:]
    moves = [
        pltpu.make_async_copy(source, target, arrived.at[place])
        for place, (source, target) in enumerate(
            (
                (class_hbm, class_ref),
                (table_hbm, table_ref),
                (q_hbm, q_ref),
                (k_hbm, k_ref),
                (g_hbm, g_ref),
                (v_hbm, v_ref),
            )
        )
    ]
    for move in moves:
        move.start()
    moves[0].wait()
    moves[1].wait()
    head_count = table_ref.shape[1]
    half = head_count // 2
    core = flag_ref[split - 1]
    gates = gate_lanes(class_ref, table_ref, offset + levels[0], offset + levels[-1] + 1)
    for move in moves[2:]:
        move.wait()
    flags = [flag_ref[level] for level in levels]
    for head in range(head_count):
        rows = [place * head_count + head for place in range(len(levels))]

        def store(place, value):
            level = levels[place]
            if level < split - 1:
                lead_refs[0][level - levels[0], head] = value
            elif level == split - 1:
                sent_ref[head] = value
            else:
                late_ref[level - split, head] = value

        columns = pl.ds(head * head_size, head_size)
        payload_cell(
            flags, gates, rows, range(len(levels)), q_ref, k_ref, v_ref, g_ref, columns, store
        )
    for place in range(levels[-1] + 1 - split):
        row = place * half
        keep_ref[row : row + half] = late_ref[place, pl.ds(core * half, half)]
        sent_ref[head_count + row : head_count + row + half] = late_ref[
            place, pl.ds((1 - core) * half, half)
        ]


def share_kernel(head_count, places, flag_ref, seen_ref, keep_ref, after_ref, *refs):
    lead_refs = refs[:-4]
    out_refs = refs[-4:]
    quarter = head_count // 4
    eighth = head_count // 8
    z_place = flag_ref[1] + 2 * flag_ref[2]
    for offs in range(4):
        place = jnp.bitwise_xor(z_place, offs)
        row = 0
        for lead in range(places[0] - 1):
            out_refs[offs][row : row + quarter] = lead_refs[0][lead, pl.ds(place * quarter, quarter)]
            row += quarter
        out_refs[offs][row : row + quarter] = seen_ref[pl.ds(place * quarter, quarter)]
        row += quarter
        for late in range(places[1]):
            first = late * (head_count // 2) + place * eighth
            total = wide(keep_ref[pl.ds(first, eighth)])
            total = total + wide(seen_ref[pl.ds(head_count + first, eighth)])
            out_refs[offs][row : row + eighth] = narrow(total)
            row += eighth


def lower_kernel(
    offset,
    head_size,
    flag_ref,
    class_ref,
    table_ref,
    q_ref,
    k_ref,
    v_ref,
    g_ref,
    after_ref,
    two_own_ref,
    sent_ref,
    rest_ref,
    two_ref,
):
    head_count = table_ref.shape[1]
    half = head_count // 2
    x_place = flag_ref[0]
    gates = gate_lanes(class_ref, table_ref, offset, offset + NEAR)
    flags = [flag_ref[level] for level in range(NEAR)]
    for head in range(head_count):
        rows = [place * head_count + head for place in range(NEAR)]

        def store(place, value):
            if place == 0:
                rest_ref[half + head] = value
            elif place == 1:
                if head < half:
                    sent_ref[half + head] = value
                else:
                    rest_ref[head - half] = value
            else:
                two_ref[head] = value

        columns = pl.ds(head * head_size, head_size)
        payload_cell(flags, gates, rows, range(NEAR), q_ref, k_ref, v_ref, g_ref, columns, store)
    two_own_ref[...] = two_ref[pl.ds(x_place * half, half)]
    sent_ref[:half] = two_ref[pl.ds((1 - x_place) * half, half)]


def four_sum_kernel(top_rows, own_ref, after_ref, *refs):
    came_refs = refs[:-2]
    below_ref, top_ref = refs[-2:]
    total = wide(own_ref[...])
    for came_ref in came_refs:
        total = total + wide(came_ref[...])
    rows = total.shape[0] - top_rows
    below_ref[...] = narrow(total[:rows])
    top_ref[...] = narrow(total[rows:])


def pair_sum_kernel(below_ref, far_ref, near_top_ref, far_top_ref, *refs):
    out_ref = refs[-1]
    rows = below_ref.shape[0]
    out_ref[:rows] = narrow(wide(below_ref[...]) + wide(far_ref[...]))
    out_ref[rows:] = narrow(wide(near_top_ref[...]) + wide(far_top_ref[...]))


def gather_kernel(cut, piece0_ref, piece1_ref, piece2_ref, piece3_ref, after_ref, local_ref, out_ref):
    for offs, piece_ref in enumerate((piece0_ref, piece1_ref, piece2_ref, piece3_ref)):
        split_levels = out_ref.shape[0]
        eighth = out_ref.shape[1] // 4
        for level in range(split_levels):
            first = cut + level * eighth
            out_ref[level, offs * eighth : (offs + 1) * eighth] = piece_ref[first : first + eighth]


def two_sum_kernel(own_ref, seen_ref, after_ref, two_ref):
    two_ref[...] = narrow(wide(own_ref[...]) + wide(seen_ref[: own_ref.shape[0]]))


def one_sum_kernel(sent_ref, seen_ref, rest_ref, rest_seen_ref, after_ref, one_ref):
    half = one_ref.shape[0] // 2
    one_ref[:half] = narrow(wide(sent_ref[half:]) + wide(seen_ref[half:]))
    one_ref[half:] = narrow(wide(rest_ref[:half]) + wide(rest_seen_ref[:half]))


def local_kernel(
    block_depth,
    head_size,
    class_ref,
    table_ref,
    q_ref,
    k_ref,
    v_ref,
    g_ref,
    after_ref,
    qo_ref,
    ko_ref,
    vo_ref,
):
    head_count = table_ref.shape[1]
    tokens = q_ref.shape[0]
    gates = gate_lanes(class_ref, table_ref, 0, block_depth + 1)
    source = lax.broadcasted_iota(jnp.int32, (tokens, tokens), 0)
    target = lax.broadcasted_iota(jnp.int32, (tokens, tokens), 1)
    apart = jnp.bitwise_xor(source, target)
    causal = source <= target
    for head in range(head_count):
        columns = pl.ds(head * head_size, head_size)
        query_here = q_ref[:, columns]
        key_here = k_ref[:, columns]
        value_here = v_ref[:, columns]
        grad_here = g_ref[:, columns]
        weight = jnp.broadcast_to(gates[head : head + 1, :], (tokens, tokens))
        for level in range(1, block_depth + 1):
            row = level * head_count + head
            weight = jnp.where(apart >= 2 ** (level - 1), gates[row : row + 1, :], weight)
        weight = jnp.where(causal, weight, 0.0)
        weighted_scores = narrow(weight * product(key_here, query_here, 1, 1))
        weighted_grads = narrow(weight * product(value_here, grad_here, 1, 1))
        qo_ref[:, columns] = product(weighted_grads, key_here, 0, 0)
        ko_ref[:, columns] = product(weighted_grads, query_here, 1, 0)
        vo_ref[:, columns] = product(weighted_scores, grad_here, 1, 0)


def gate_columns(class_ref, table_ref, first, last):
    return gate_lanes(class_ref, table_ref, first, last).T


def final_kernel(
    offset,
    head_size,
    total,
    inner,
    flag_ref,
    class_ref,
    table_ref,
    k_ref,
    v_ref,
    g_ref,
    ql_ref,
    kl_ref,
    vl_ref,
    zero_ref,
    one_ref,
    two_own_ref,
    two_other_ref,
    piece0_ref,
    piece1_ref,
    piece2_ref,
    piece3_ref,
    split_own_ref,
    split_other_ref,
    qo_ref,
    ko_ref,
    vo_ref,
    held_ref,
):
    head_count = table_ref.shape[1]
    half = head_count // 2
    quarter = head_count // 4
    eighth = head_count // 8
    gates = gate_columns(class_ref, table_ref, offset, offset + total)
    x_place = flag_ref[0]
    z_place = flag_ref[1] + 2 * flag_ref[2]
    core = flag_ref[inner]
    held_ref[0] = zero_ref[zero_ref.shape[0] - head_count :]
    held_ref[1] = one_ref[...]
    held_ref[2, pl.ds(x_place * half, half)] = two_own_ref[...]
    held_ref[2, pl.ds((1 - x_place) * half, half)] = two_other_ref[...]
    pieces = (piece0_ref, piece1_ref, piece2_ref, piece3_ref)
    split = inner + 1
    for level in range(NEAR, split):
        for offs in range(4):
            first = jnp.bitwise_xor(z_place, offs) * quarter
            row = (level - NEAR) * quarter
            held_ref[level, pl.ds(first, quarter)] = pieces[offs][row : row + quarter]
    for level in range(split, total):
        for offs in range(4):
            first = jnp.bitwise_xor(z_place, offs) * eighth
            rows = pl.ds(offs * eighth, eighth)
            held_ref[level, pl.ds(core * half + first, eighth)] = split_own_ref[level - split, rows]
            held_ref[level, pl.ds((1 - core) * half + first, eighth)] = split_other_ref[
                level - split, rows
            ]
    for head in range(head_count):
        columns = pl.ds(head * head_size, head_size)
        grad_here = g_ref[:, columns]
        query_total = ql_ref[:, columns]
        state_grad = jnp.zeros((head_size, head_size), jnp.float32)
        for level in range(total):
            state = held_ref[level, head]
            term = product(grad_here, state, 1, 1)
            row = level * head_count + head
            on = wide(flag_ref[level])
            query_total = query_total + (gates[:, row : row + 1] * on) * term
            state_grad = state_grad + wide(state) * (1.0 - on)
        grad_rounded = narrow(state_grad)
        qo_ref[:, columns] = narrow(query_total)
        ko_ref[:, columns] = narrow(
            kl_ref[:, columns] + product(v_ref[:, columns], grad_rounded, 1, 1)
        )
        vo_ref[:, columns] = narrow(
            vl_ref[:, columns] + product(k_ref[:, columns], grad_rounded, 1, 0)
        )


def per_device(query_rows, key_rows, value_rows, out_grad, gate_class, gate_table):
    row_count, width = query_rows.shape
    head_count = gate_table.shape[2]
    head_size = width // head_count
    inner_bits = level_bits(lax.axis_size("gy"))
    outer_bits = level_bits(lax.axis_size("gx"))
    total = inner_bits + outer_bits
    block_depth = level_bits(row_count)
    offset = block_depth + 1
    inner_index = lax.axis_index("gy")
    outer_index = lax.axis_index("gx")
    block_index = (outer_index << inner_bits) | inner_index
    flag_bits = (block_index >> jnp.arange(total, dtype=jnp.int32)) & 1
    inner_size = lax.axis_size("gy")
    device_count = inner_size * lax.axis_size("gx")

    def swap(block, *bits):
        mask = sum(1 << bit for bit in bits)
        if mask < inner_size:
            return lax.ppermute(block, "gy", [(i, i ^ mask) for i in range(inner_size)])
        if mask % inner_size == 0:
            mask = mask // inner_size
            size = lax.axis_size("gx")
            return lax.ppermute(block, "gx", [(i, i ^ mask) for i in range(size)])
        return lax.ppermute(block, ("gx", "gy"), [(i, i ^ mask) for i in range(device_count)])

    class_lanes = gate_class.reshape(1, row_count)
    table = jnp.transpose(gate_table, (1, 2, 0))
    smem = pl.BlockSpec(memory_space=pltpu.SMEM)
    vmem = pl.BlockSpec(memory_space=pltpu.VMEM)
    hbm = pl.BlockSpec(memory_space=pltpu.HBM)
    anywhere = pl.BlockSpec(memory_space=pl.ANY)
    cell = (head_size, head_size)

    def cells(*lead):
        return jax.ShapeDtypeStruct(lead + cell, jnp.bfloat16)

    def call(kernel, in_specs, outs, operands, flops=0, scratch=(), grant=VMEM_BYTES, out_specs=None, aliases=None):
        moved = sum(operand.size * operand.dtype.itemsize for operand in operands)
        return pl.pallas_call(
            kernel,
            out_shape=outs,
            in_specs=in_specs,
            out_specs=out_specs or jax.tree.map(lambda _: vmem, outs),
            input_output_aliases=aliases or {},
            scratch_shapes=scratch,
            compiler_params=pltpu.CompilerParams(vmem_limit_bytes=grant),
            cost_estimate=pl.CostEstimate(flops=flops, bytes_accessed=moved, transcendentals=0),
        )(*operands)

    quarter = head_count // 4
    half = head_count // 2
    eighth = head_count // 8
    split = inner_bits + 1
    whole_levels = split - NEAR
    split_levels = total - split
    cut = whole_levels * quarter
    share_rows = cut + split_levels * eighth
    block = pltpu.VMEM((row_count, width), jnp.bfloat16)

    levels = tuple(range(NEAR, total))
    first_reads = (class_lanes, table, query_rows, key_rows, value_rows, out_grad)
    outs = (cells(head_count + split_levels * half), cells(split_levels * half))
    if whole_levels > 1:
        outs = outs + (cells(whole_levels - 1, head_count),)
    sent, keep, *lead = call(
        functools.partial(upper_kernel, levels, split, offset, head_size),
        [smem] + [hbm] * 6,
        outs,
        (flag_bits, *[pltpu.with_memory_space_constraint(held, pltpu.HBM) for held in first_reads]),
        flops=2 * len(levels) * row_count * width * head_size,
        scratch=[
            pltpu.VMEM(class_lanes.shape, jnp.int32),
            pltpu.VMEM(table.shape, jnp.float32),
            block,
            block,
            block,
            block,
            pltpu.VMEM((split_levels, head_count) + cell, jnp.bfloat16),
            pltpu.SemaphoreType.DMA((6,)),
        ],
        grant=FIRST_BYTES,
    )
    seen = swap(sent, inner_bits)
    two_own, lower_sent, rest = call(
        functools.partial(lower_kernel, offset, head_size),
        [smem] + [vmem] * 6 + [anywhere],
        (cells(half), cells(2 * half), cells(half + head_count)),
        (flag_bits, class_lanes, table, query_rows, key_rows, value_rows, out_grad, keep),
        flops=2 * NEAR * row_count * width * head_size,
        scratch=[pltpu.VMEM((head_count,) + cell, jnp.bfloat16)],
    )
    own_share, *shares_out = call(
        functools.partial(share_kernel, head_count, (whole_levels, split_levels)),
        [smem] + [vmem] * 2 + [anywhere] + [vmem] * len(lead),
        (cells(share_rows),) * 4,
        (flag_bits, seen, keep, two_own, *lead),
    )
    lower_seen = swap(lower_sent, 0)
    rest_seen = swap(rest, 0)
    two_sum = call(
        two_sum_kernel, [vmem] * 2 + [anywhere], cells(half), (two_own, lower_seen, own_share)
    )
    big = jax.ShapeDtypeStruct((row_count, width), jnp.float32)

    def z_bits(offs):
        return [bit + 1 for bit in range(2) if offs >> bit & 1]

    came = [swap(shares_out[offs - 1], *z_bits(offs)) for offs in (3, 2, 1)]
    top = total - 1
    below, top_sent = call(
        functools.partial(four_sum_kernel, eighth),
        [vmem, anywhere] + [vmem] * 3,
        (cells(share_rows - eighth), cells(eighth)),
        (own_share, own_share, *came),
    )
    middle = [bit for bit in range(NEAR, top) if bit != inner_bits]
    if middle:
        part = wide(jnp.concatenate([below, top_sent], axis=0))
        parts = {
            level: part[(level - NEAR) * quarter : (level - NEAR + 1) * quarter]
            for level in range(NEAR, split)
        }
        for level in range(split, total):
            row = cut + (level - split) * eighth
            parts[level] = part[row : row + eighth]
        for bit in middle:
            going = range(bit, total)
            block_sent = narrow(jnp.concatenate([parts[level] for level in going], axis=0))
            seen_part = wide(swap(block_sent, bit))
            row = 0
            for level in going:
                size = parts[level].shape[0]
                got = seen_part[row : row + size]
                parts[level] = got if level == bit else parts[level] + got
                row += size
        below = narrow(jnp.concatenate([parts[level] for level in range(NEAR, top)], axis=0))
        top_sent = narrow(parts[top])
    two_sum = call(
        two_sum_kernel, [vmem] * 2 + [anywhere], cells(half), (two_sum, swap(two_sum, 1), two_sum)
    )
    two_half = swap(two_sum, 2)
    two_rest = swap(two_half, 0)
    shares = call(
        pair_sum_kernel,
        [vmem] * 4 + [anywhere] * 2,
        cells(share_rows),
        (below, swap(below, 0), swap(top_sent, top), swap(top_sent, 0, top), two_sum, rest_seen),
    )
    one_sum = call(
        one_sum_kernel,
        [vmem] * 4 + [anywhere],
        cells(head_count),
        (lower_sent, lower_seen, rest, rest_seen, shares),
    )
    one_done = swap(one_sum, 1)
    query_local, key_local, value_local = call(
        functools.partial(local_kernel, block_depth, head_size),
        [vmem] * 6 + [anywhere],
        (big, big, big),
        (class_lanes, table, query_rows, key_rows, value_rows, out_grad, shares),
        flops=10 * row_count * width * row_count,
    )
    pieces = [shares] + [swap(shares, *z_bits(offs)) for offs in (1, 2, 3)]
    split_own = call(
        functools.partial(gather_kernel, cut),
        [vmem] * 4 + [anywhere] * 2,
        cells(split_levels, half),
        (*pieces, two_half, query_local),
    )
    split_other = swap(split_own, inner_bits)

    small = jax.ShapeDtypeStruct((row_count, width), jnp.bfloat16)
    return call(
        functools.partial(final_kernel, offset, head_size, total, inner_bits),
        [smem] + [vmem] * 18,
        (small, small, small),
        (
            flag_bits,
            class_lanes,
            table,
            key_rows,
            value_rows,
            out_grad,
            query_local,
            key_local,
            value_local,
            rest_seen,
            one_done,
            two_half,
            two_rest,
            *pieces,
            split_own,
            split_other,
        ),
        flops=(2 * total + 4) * row_count * width * head_size,
        scratch=[pltpu.VMEM((total, head_count) + cell, jnp.bfloat16)],
    )


def solution(mesh):
    rows = P(("gx", "gy"), None)
    return jax.shard_map(
        per_device,
        mesh=mesh,
        in_specs=(rows, rows, rows, rows, P(("gx", "gy")), P()),
        out_specs=(rows, rows, rows),
        check_vma=False,
    )
```

```python
import functools

import jax
import jax.numpy as jnp
from jax import lax
from jax.experimental import pallas as pl
from jax.experimental.pallas import tpu as pltpu
from jax.sharding import PartitionSpec as P

NEAR = 3
VMEM_BYTES = 16 * 1024 * 1024
FIRST_BYTES = 16 * 1024 * 1024


def level_bits(amount):
    return amount.bit_length() - 1


def wide(values):
    return values.astype(jnp.float32)


def narrow(values):
    return values.astype(jnp.bfloat16)


def product(left, right, left_dim, right_dim):
    return lax.dot_general(
        left,
        right,
        (((left_dim,), (right_dim,)), ((), ())),
        preferred_element_type=jnp.float32,
    )


def gate_lanes(class_ref, table_ref, first, last):
    classes = table_ref.shape[2]
    tokens = class_ref.shape[1]
    rows = (last - first) * table_ref.shape[1]
    numbers = lax.broadcasted_iota(jnp.int32, (classes, tokens), 0)
    picker = (numbers == class_ref[...]).astype(jnp.float32)
    table = table_ref[first:last].reshape(rows, classes)
    return jnp.dot(
        table, picker, precision=lax.Precision.HIGHEST, preferred_element_type=jnp.float32
    )


def payload_cell(flags, gates, rows, level_places, q_ref, k_ref, v_ref, g_ref, columns, store):
    query_turned = wide(q_ref[:, columns].T)
    key_turned = wide(k_ref[:, columns].T)
    grad_here = wide(g_ref[:, columns])
    value_here = wide(v_ref[:, columns])
    for place in level_places:
        row = rows[place]
        flag = flags[place] == 1
        left = jnp.where(flag, gates[row : row + 1, :] * query_turned, key_turned)
        right = jnp.where(flag, grad_here, value_here)
        store(place, narrow(product(narrow(left), narrow(right), 1, 0)))


def upper_kernel(
    levels,
    split,
    offset,
    head_size,
    flag_ref,
    class_hbm,
    table_hbm,
    q_hbm,
    k_hbm,
    v_hbm,
    g_hbm,
    sent_ref,
    keep_ref,
    *rest,
):
    lead_refs = rest[:-8]
    class_ref, table_ref, q_ref, k_ref, v_ref, g_ref, late_ref, arrived = rest[-8:]
    moves = [
        pltpu.make_async_copy(source, target, arrived.at[place])
        for place, (source, target) in enumerate(
            (
                (class_hbm, class_ref),
                (table_hbm, table_ref),
                (q_hbm, q_ref),
                (k_hbm, k_ref),
                (g_hbm, g_ref),
                (v_hbm, v_ref),
            )
        )
    ]
    for move in moves:
        move.start()
    moves[0].wait()
    moves[1].wait()
    head_count = table_ref.shape[1]
    half = head_count // 2
    core = flag_ref[split - 1]
    gates = gate_lanes(class_ref, table_ref, offset + levels[0], offset + levels[-1] + 1)
    for move in moves[2:]:
        move.wait()
    flags = [flag_ref[level] for level in levels]
    for head in range(head_count):
        rows = [place * head_count + head for place in range(len(levels))]

        def store(place, value):
            level = levels[place]
            if level < split - 1:
                lead_refs[0][level - levels[0], head] = value
            elif level == split - 1:
                sent_ref[head] = value
            else:
                late_ref[level - split, head] = value

        columns = pl.ds(head * head_size, head_size)
        payload_cell(
            flags, gates, rows, range(len(levels)), q_ref, k_ref, v_ref, g_ref, columns, store
        )
    for place in range(levels[-1] + 1 - split):
        row = place * half
        keep_ref[row : row + half] = late_ref[place, pl.ds(core * half, half)]
        sent_ref[head_count + row : head_count + row + half] = late_ref[
            place, pl.ds((1 - core) * half, half)
        ]


def share_kernel(head_count, places, flag_ref, seen_ref, keep_ref, after_ref, *refs):
    lead_refs = refs[:-4]
    out_refs = refs[-4:]
    quarter = head_count // 4
    eighth = head_count // 8
    z_place = flag_ref[1] + 2 * flag_ref[2]
    for offs in range(4):
        place = jnp.bitwise_xor(z_place, offs)
        row = 0
        for lead in range(places[0] - 1):
            out_refs[offs][row : row + quarter] = lead_refs[0][lead, pl.ds(place * quarter, quarter)]
            row += quarter
        out_refs[offs][row : row + quarter] = seen_ref[pl.ds(place * quarter, quarter)]
        row += quarter
        for late in range(places[1]):
            first = late * (head_count // 2) + place * eighth
            total = wide(keep_ref[pl.ds(first, eighth)])
            total = total + wide(seen_ref[pl.ds(head_count + first, eighth)])
            out_refs[offs][row : row + eighth] = narrow(total)
            row += eighth


def lower_kernel(
    offset,
    head_size,
    flag_ref,
    class_ref,
    table_ref,
    q_ref,
    k_ref,
    v_ref,
    g_ref,
    after_ref,
    two_own_ref,
    sent_ref,
    rest_ref,
    two_ref,
):
    head_count = table_ref.shape[1]
    half = head_count // 2
    x_place = flag_ref[0]
    gates = gate_lanes(class_ref, table_ref, offset, offset + NEAR)
    flags = [flag_ref[level] for level in range(NEAR)]
    for head in range(head_count):
        rows = [place * head_count + head for place in range(NEAR)]

        def store(place, value):
            if place == 0:
                rest_ref[half + head] = value
            elif place == 1:
                if head < half:
                    sent_ref[half + head] = value
                else:
                    rest_ref[head - half] = value
            else:
                two_ref[head] = value

        columns = pl.ds(head * head_size, head_size)
        payload_cell(flags, gates, rows, range(NEAR), q_ref, k_ref, v_ref, g_ref, columns, store)
    two_own_ref[...] = two_ref[pl.ds(x_place * half, half)]
    sent_ref[:half] = two_ref[pl.ds((1 - x_place) * half, half)]


def four_sum_kernel(top_rows, own_ref, after_ref, *refs):
    came_refs = refs[:-2]
    below_ref, top_ref = refs[-2:]
    total = wide(own_ref[...])
    for came_ref in came_refs:
        total = total + wide(came_ref[...])
    rows = total.shape[0] - top_rows
    below_ref[...] = narrow(total[:rows])
    top_ref[...] = narrow(total[rows:])


def pair_sum_kernel(below_ref, far_ref, near_top_ref, far_top_ref, *refs):
    out_ref = refs[-1]
    rows = below_ref.shape[0]
    out_ref[:rows] = narrow(wide(below_ref[...]) + wide(far_ref[...]))
    out_ref[rows:] = narrow(wide(near_top_ref[...]) + wide(far_top_ref[...]))


def gather_kernel(cut, piece0_ref, piece1_ref, piece2_ref, piece3_ref, after_ref, local_ref, out_ref):
    for offs, piece_ref in enumerate((piece0_ref, piece1_ref, piece2_ref, piece3_ref)):
        split_levels = out_ref.shape[0]
        eighth = out_ref.shape[1] // 4
        for level in range(split_levels):
            first = cut + level * eighth
            out_ref[level, offs * eighth : (offs + 1) * eighth] = piece_ref[first : first + eighth]


def two_sum_kernel(own_ref, seen_ref, after_ref, two_ref):
    two_ref[...] = narrow(wide(own_ref[...]) + wide(seen_ref[: own_ref.shape[0]]))


def one_sum_kernel(sent_ref, seen_ref, rest_ref, rest_seen_ref, after_ref, one_ref):
    half = one_ref.shape[0] // 2
    one_ref[:half] = narrow(wide(sent_ref[half:]) + wide(seen_ref[half:]))
    one_ref[half:] = narrow(wide(rest_ref[:half]) + wide(rest_seen_ref[:half]))


def local_kernel(
    block_depth,
    head_size,
    flag_ref,
    zero_ref,
    class_ref,
    table_ref,
    q_ref,
    k_ref,
    v_ref,
    g_ref,
    after_ref,
    qo_ref,
    ko_ref,
    vo_ref,
):
    head_count = table_ref.shape[1]
    tokens = q_ref.shape[0]
    gates = gate_lanes(class_ref, table_ref, 0, block_depth + 2)
    outer = (gates[(block_depth + 1) * head_count :] * wide(flag_ref[0])).T
    zero_first = zero_ref.shape[0] - head_count
    source = lax.broadcasted_iota(jnp.int32, (tokens, tokens), 0)
    target = lax.broadcasted_iota(jnp.int32, (tokens, tokens), 1)
    apart = jnp.bitwise_xor(source, target)
    causal = source <= target
    for head in range(head_count):
        columns = pl.ds(head * head_size, head_size)
        query_here = q_ref[:, columns]
        key_here = k_ref[:, columns]
        value_here = v_ref[:, columns]
        grad_here = g_ref[:, columns]
        weight = jnp.broadcast_to(gates[head : head + 1, :], (tokens, tokens))
        for level in range(1, block_depth + 1):
            row = level * head_count + head
            weight = jnp.where(apart >= 2 ** (level - 1), gates[row : row + 1, :], weight)
        weight = jnp.where(causal, weight, 0.0)
        weighted_scores = narrow(weight * product(key_here, query_here, 1, 1))
        weighted_grads = narrow(weight * product(value_here, grad_here, 1, 1))
        outside = product(grad_here, zero_ref[zero_first + head], 1, 1)
        qo_ref[:, columns] = (
            product(weighted_grads, key_here, 0, 0) + outer[:, head : head + 1] * outside
        )
        ko_ref[:, columns] = product(weighted_grads, query_here, 1, 0)
        vo_ref[:, columns] = product(weighted_scores, grad_here, 1, 0)


def gate_columns(class_ref, table_ref, first, last):
    return gate_lanes(class_ref, table_ref, first, last).T


def final_kernel(
    offset,
    head_size,
    total,
    inner,
    flag_ref,
    class_ref,
    table_ref,
    k_ref,
    v_ref,
    g_ref,
    ql_ref,
    kl_ref,
    vl_ref,
    zero_ref,
    one_ref,
    two_own_ref,
    two_other_ref,
    piece0_ref,
    piece1_ref,
    piece2_ref,
    piece3_ref,
    split_own_ref,
    split_other_ref,
    qo_ref,
    ko_ref,
    vo_ref,
    held_ref,
):
    head_count = table_ref.shape[1]
    half = head_count // 2
    quarter = head_count // 4
    eighth = head_count // 8
    gates = gate_columns(class_ref, table_ref, offset, offset + total)
    x_place = flag_ref[0]
    z_place = flag_ref[1] + 2 * flag_ref[2]
    core = flag_ref[inner]
    held_ref[0] = zero_ref[zero_ref.shape[0] - head_count :]
    held_ref[1] = one_ref[...]
    held_ref[2, pl.ds(x_place * half, half)] = two_own_ref[...]
    held_ref[2, pl.ds((1 - x_place) * half, half)] = two_other_ref[...]
    pieces = (piece0_ref, piece1_ref, piece2_ref, piece3_ref)
    split = inner + 1
    for level in range(NEAR, split):
        for offs in range(4):
            first = jnp.bitwise_xor(z_place, offs) * quarter
            row = (level - NEAR) * quarter
            held_ref[level, pl.ds(first, quarter)] = pieces[offs][row : row + quarter]
    for level in range(split, total):
        for offs in range(4):
            first = jnp.bitwise_xor(z_place, offs) * eighth
            rows = pl.ds(offs * eighth, eighth)
            held_ref[level, pl.ds(core * half + first, eighth)] = split_own_ref[level - split, rows]
            held_ref[level, pl.ds((1 - core) * half + first, eighth)] = split_other_ref[
                level - split, rows
            ]
    for head in range(head_count):
        columns = pl.ds(head * head_size, head_size)
        grad_here = g_ref[:, columns]
        query_total = ql_ref[:, columns]
        state_grad = jnp.zeros((head_size, head_size), jnp.float32)
        for level in range(total):
            state = held_ref[level, head]
            term = product(grad_here, state, 1, 1)
            row = level * head_count + head
            on = wide(flag_ref[level])
            if level > 0:
                query_total = query_total + (gates[:, row : row + 1] * on) * term
            state_grad = state_grad + wide(state) * (1.0 - on)
        grad_rounded = narrow(state_grad)
        qo_ref[:, columns] = narrow(query_total)
        ko_ref[:, columns] = narrow(
            kl_ref[:, columns] + product(v_ref[:, columns], grad_rounded, 1, 1)
        )
        vo_ref[:, columns] = narrow(
            vl_ref[:, columns] + product(k_ref[:, columns], grad_rounded, 1, 0)
        )


def per_device(query_rows, key_rows, value_rows, out_grad, gate_class, gate_table):
    row_count, width = query_rows.shape
    head_count = gate_table.shape[2]
    head_size = width // head_count
    inner_bits = level_bits(lax.axis_size("gy"))
    outer_bits = level_bits(lax.axis_size("gx"))
    total = inner_bits + outer_bits
    block_depth = level_bits(row_count)
    offset = block_depth + 1
    inner_index = lax.axis_index("gy")
    outer_index = lax.axis_index("gx")
    block_index = (outer_index << inner_bits) | inner_index
    flag_bits = (block_index >> jnp.arange(total, dtype=jnp.int32)) & 1
    inner_size = lax.axis_size("gy")
    device_count = inner_size * lax.axis_size("gx")

    def swap(block, *bits):
        mask = sum(1 << bit for bit in bits)
        if mask < inner_size:
            return lax.ppermute(block, "gy", [(i, i ^ mask) for i in range(inner_size)])
        if mask % inner_size == 0:
            mask = mask // inner_size
            size = lax.axis_size("gx")
            return lax.ppermute(block, "gx", [(i, i ^ mask) for i in range(size)])
        return lax.ppermute(block, ("gx", "gy"), [(i, i ^ mask) for i in range(device_count)])

    class_lanes = gate_class.reshape(1, row_count)
    table = jnp.transpose(gate_table, (1, 2, 0))
    smem = pl.BlockSpec(memory_space=pltpu.SMEM)
    vmem = pl.BlockSpec(memory_space=pltpu.VMEM)
    hbm = pl.BlockSpec(memory_space=pltpu.HBM)
    anywhere = pl.BlockSpec(memory_space=pl.ANY)
    cell = (head_size, head_size)

    def cells(*lead):
        return jax.ShapeDtypeStruct(lead + cell, jnp.bfloat16)

    def call(kernel, in_specs, outs, operands, flops=0, scratch=(), grant=VMEM_BYTES, out_specs=None, aliases=None):
        moved = sum(operand.size * operand.dtype.itemsize for operand in operands)
        return pl.pallas_call(
            kernel,
            out_shape=outs,
            in_specs=in_specs,
            out_specs=out_specs or jax.tree.map(lambda _: vmem, outs),
            input_output_aliases=aliases or {},
            scratch_shapes=scratch,
            compiler_params=pltpu.CompilerParams(vmem_limit_bytes=grant),
            cost_estimate=pl.CostEstimate(flops=flops, bytes_accessed=moved, transcendentals=0),
        )(*operands)

    quarter = head_count // 4
    half = head_count // 2
    eighth = head_count // 8
    split = inner_bits + 1
    whole_levels = split - NEAR
    split_levels = total - split
    cut = whole_levels * quarter
    share_rows = cut + split_levels * eighth
    block = pltpu.VMEM((row_count, width), jnp.bfloat16)

    levels = tuple(range(NEAR, total))
    first_reads = (class_lanes, table, query_rows, key_rows, value_rows, out_grad)
    outs = (cells(head_count + split_levels * half), cells(split_levels * half))
    if whole_levels > 1:
        outs = outs + (cells(whole_levels - 1, head_count),)
    sent, keep, *lead = call(
        functools.partial(upper_kernel, levels, split, offset, head_size),
        [smem] + [hbm] * 6,
        outs,
        (flag_bits, *[pltpu.with_memory_space_constraint(held, pltpu.HBM) for held in first_reads]),
        flops=2 * len(levels) * row_count * width * head_size,
        scratch=[
            pltpu.VMEM(class_lanes.shape, jnp.int32),
            pltpu.VMEM(table.shape, jnp.float32),
            block,
            block,
            block,
            block,
            pltpu.VMEM((split_levels, head_count) + cell, jnp.bfloat16),
            pltpu.SemaphoreType.DMA((6,)),
        ],
        grant=FIRST_BYTES,
    )
    seen = swap(sent, inner_bits)
    two_own, lower_sent, rest = call(
        functools.partial(lower_kernel, offset, head_size),
        [smem] + [vmem] * 6 + [anywhere],
        (cells(half), cells(2 * half), cells(half + head_count)),
        (flag_bits, class_lanes, table, query_rows, key_rows, value_rows, out_grad, keep),
        flops=2 * NEAR * row_count * width * head_size,
        scratch=[pltpu.VMEM((head_count,) + cell, jnp.bfloat16)],
    )
    own_share, *shares_out = call(
        functools.partial(share_kernel, head_count, (whole_levels, split_levels)),
        [smem] + [vmem] * 2 + [anywhere] + [vmem] * len(lead),
        (cells(share_rows),) * 4,
        (flag_bits, seen, keep, two_own, *lead),
    )
    lower_seen = swap(lower_sent, 0)
    rest_seen = swap(rest, 0)
    two_sum = call(
        two_sum_kernel, [vmem] * 2 + [anywhere], cells(half), (two_own, lower_seen, own_share)
    )
    big = jax.ShapeDtypeStruct((row_count, width), jnp.float32)

    def z_bits(offs):
        return [bit + 1 for bit in range(2) if offs >> bit & 1]

    came = [swap(shares_out[offs - 1], *z_bits(offs)) for offs in (3, 2, 1)]
    top = total - 1
    below, top_sent = call(
        functools.partial(four_sum_kernel, eighth),
        [vmem, anywhere] + [vmem] * 3,
        (cells(share_rows - eighth), cells(eighth)),
        (own_share, own_share, *came),
    )
    middle = [bit for bit in range(NEAR, top) if bit != inner_bits]
    if middle:
        part = wide(jnp.concatenate([below, top_sent], axis=0))
        parts = {
            level: part[(level - NEAR) * quarter : (level - NEAR + 1) * quarter]
            for level in range(NEAR, split)
        }
        for level in range(split, total):
            row = cut + (level - split) * eighth
            parts[level] = part[row : row + eighth]
        for bit in middle:
            going = range(bit, total)
            block_sent = narrow(jnp.concatenate([parts[level] for level in going], axis=0))
            seen_part = wide(swap(block_sent, bit))
            row = 0
            for level in going:
                size = parts[level].shape[0]
                got = seen_part[row : row + size]
                parts[level] = got if level == bit else parts[level] + got
                row += size
        below = narrow(jnp.concatenate([parts[level] for level in range(NEAR, top)], axis=0))
        top_sent = narrow(parts[top])
    one_sum = call(
        one_sum_kernel,
        [vmem] * 4 + [anywhere],
        cells(head_count),
        (lower_sent, lower_seen, rest, rest_seen, below),
    )
    two_sum = call(
        two_sum_kernel, [vmem] * 2 + [anywhere], cells(half), (two_sum, swap(two_sum, 1), two_sum)
    )
    two_half = swap(two_sum, 2)
    two_rest = swap(two_half, 0)
    one_done = swap(one_sum, 1)
    shares = call(
        pair_sum_kernel,
        [vmem] * 4 + [anywhere] * 2,
        cells(share_rows),
        (below, swap(below, 0), swap(top_sent, top), swap(top_sent, 0, top), two_sum, rest_seen),
    )
    query_local, key_local, value_local = call(
        functools.partial(local_kernel, block_depth, head_size),
        [smem] + [vmem] * 7 + [anywhere],
        (big, big, big),
        (flag_bits, rest_seen, class_lanes, table, query_rows, key_rows, value_rows, out_grad, shares),
        flops=10 * row_count * width * row_count,
    )
    pieces = [shares] + [swap(shares, *z_bits(offs)) for offs in (1, 2, 3)]
    split_own = call(
        functools.partial(gather_kernel, cut),
        [vmem] * 4 + [anywhere] * 2,
        cells(split_levels, half),
        (*pieces, two_half, query_local),
    )
    split_other = swap(split_own, inner_bits)

    small = jax.ShapeDtypeStruct((row_count, width), jnp.bfloat16)
    return call(
        functools.partial(final_kernel, offset, head_size, total, inner_bits),
        [smem] + [vmem] * 18,
        (small, small, small),
        (
            flag_bits,
            class_lanes,
            table,
            key_rows,
            value_rows,
            out_grad,
            query_local,
            key_local,
            value_local,
            rest_seen,
            one_done,
            two_half,
            two_rest,
            *pieces,
            split_own,
            split_other,
        ),
        flops=(2 * total + 4) * row_count * width * head_size,
        scratch=[pltpu.VMEM((total, head_count) + cell, jnp.bfloat16)],
    )


def solution(mesh):
    rows = P(("gx", "gy"), None)
    return jax.shard_map(
        per_device,
        mesh=mesh,
        in_specs=(rows, rows, rows, rows, P(("gx", "gy")), P()),
        out_specs=(rows, rows, rows),
        check_vma=False,
    )
```
